32 devices in a mesh: head: 8 (over z, y), blk: 4 (over x, core).
Axes of the slice: x: 2, y: 2, z: 4, core: 2. Of those that a mesh axis runs over, the one named last changes fastest.
Arguments:
- inputs: bfloat16 [2, 4, 1024, 1024], P(None, 'blk', 'head'), may hold values from -6 to 6
- segments: int32 [2, 4, 1024], replicated, may hold values from 0 to 8, as said below
- bucket_table: int32 [257], replicated, may hold values from 0 to 31, as said below
- norm_gain: bfloat16 [1024], P(('head', 'blk')), may hold values from 0.25 to 1.75
- w_query: bfloat16 [1024, 1024], P(('head', 'blk')), may hold values from -0.09375 to 0.09375
- w_key: bfloat16 [1024, 1024], P(('head', 'blk')), may hold values from -0.09375 to 0.09375
- w_value: bfloat16 [1024, 1024], P(('head', 'blk')), may hold values from -0.1875 to 0.1875
- w_out: bfloat16 [1024, 1024], P(('head', 'blk')), may hold values from -0.375 to 0.375
- rel_bias: bfloat16 [512], P(('head', 'blk')), may hold values from -4 to 4
- ff_gain: bfloat16 [1024], P(('head', 'blk')), may hold values from 0.25 to 1.75
- w_in: bfloat16 [1024, 4096], P(('head', 'blk')), may hold values from -0.1875 to 0.1875
- w_down: bfloat16 [4096, 1024], P(('head', 'blk')), may hold values from -0.09375 to 0.09375
- cotangent: bfloat16 [2, 4, 1024, 1024], P(None, 'blk', 'head'), may hold values from -6 to 6
Outputs:
- layer_out: bfloat16 [2, 4, 1024, 1024], P(None, 'blk', 'head')
- input_grad: bfloat16 [2, 4, 1024, 1024], P(None, 'blk', 'head')
- grad_norm_gain: float32 [1024], P(('head', 'blk'))
- grad_query: float32 [1024, 1024], P(('head', 'blk'))
- grad_key: float32 [1024, 1024], P(('head', 'blk'))
- grad_value: float32 [1024, 1024], P(('head', 'blk'))
- grad_out: float32 [1024, 1024], P(('head', 'blk'))
- grad_rel: float32 [512], P(('head', 'blk'))
- grad_ff_gain: float32 [1024], P(('head', 'blk'))
- grad_in: float32 [1024, 4096], P(('head', 'blk'))
- grad_down: float32 [4096, 1024], P(('head', 'blk'))
The draws below stay inside these ranges and needn't reach their ends.
Inputs may be any that keep to these rules, and one draw needn't show every extreme that they name: `segments`: document numbers start at 0 in each sequence and never fall along it. In one sequence drawn from the seed the whole sequence is one document; in every other one each aligned run of min(512, 4096) positions holds exactly one document start, lying at least an eighth of the run away from the run's ends. `bucket_table`: A relabelling drawn from the seed of the bidirectional T5 buckets (32 buckets; exact distances below a quarter of them on each side, logarithmic up to 128) for offsets minus 128 to 128; entry 128 is offset 0.
All inputs are finite; a program needn't handle non-finite values.
Results may differ from the reference program's by a relative error of at most 0.02.
Values may be sent and summed in bfloat16 or wider, within the bound.
No kernel may reach another device: no remote copies, remote signals or barrier semaphores. Data moves between devices by JAX's collectives and lax.ppermute only.
A program may use at most 256 MiB of HBM per device.

```python
from functools import partial
import jax
import jax.numpy as jnp
import numpy as np
from jax import lax

D = 1024
HEADS = 16
HD = 64
FF = 4096
BUCKETS = 32
MAXREL = 128
SPAN = 1024
SEQS = 2
LEN = 4096
N_BLK = 4


def draw_segments(key, part):
    key = jax.random.fold_in(key, 11)
    piece = min(512, LEN)
    pieces = LEN // piece
    margin = piece // 8
    cut_key, whole_key = jax.random.split(key)
    starts = jax.random.randint(cut_key, (SEQS, pieces), margin, piece - margin) + jnp.arange(pieces, dtype=jnp.int32)[None, :] * piece
    places = jnp.arange(LEN, dtype=jnp.int32)
    numbers = jnp.sum((places[None, :, None] >= starts[:, None, :]).astype(jnp.int32), axis=2)
    chosen = jax.random.randint(whole_key, (), 0, SEQS)
    numbers = jnp.where(jnp.arange(SEQS, dtype=jnp.int32)[:, None] == chosen, 0, numbers)
    return numbers.reshape(SEQS, LEN // SPAN, SPAN).astype(jnp.int32)


def draw_bucket_table(key, part):
    key = jax.random.fold_in(key, 23)
    offsets = np.arange(-MAXREL, MAXREL + 1)
    half_count = BUCKETS // 2
    exact_count = half_count // 2
    distance = np.abs(offsets)
    far_part = exact_count + np.floor(np.log(np.maximum(distance, 1) / exact_count) / np.log(MAXREL / exact_count) * (half_count - exact_count)).astype(np.int64)
    base_table = np.where(distance < exact_count, distance, np.minimum(far_part, half_count - 1)) + np.where(offsets > 0, half_count, 0)
    labels = jax.random.permutation(key, BUCKETS).astype(jnp.int32)
    return labels[jnp.asarray(base_table, dtype=jnp.int32)].astype(jnp.int32)


def shard_levels(rng, extent, cuts, smallest, high):
    def one(position, blocks):
        draws = jax.random.uniform(jax.random.fold_in(jax.random.fold_in(rng, 6), position), (blocks,), jnp.float32, smallest / len(cuts), high / len(cuts))
        return jnp.repeat(jnp.exp(draws), extent[position] // blocks).reshape((-1,) + (1,) * (len(extent) - position - 1))

    loudness = one(*cuts[0])
    for cut in cuts[1:]:
        loudness = loudness * one(*cut)
    return loudness


def bell_draw(own_key, shape, deviation, limit, shards=(), held_as=jnp.bfloat16):
    result = deviation * jax.random.normal(own_key, shape, jnp.float32)
    if shards:
        result = result * shard_levels(own_key, shape, shards, -0.22, 0.18)
    return jnp.clip(result, -limit, limit).astype(held_as)


def setup_inputs(seed: int = 0) -> dict:
    keys = jax.random.split(jax.random.key(seed), 14)
    return {
        "inputs": bell_draw(keys[0], (SEQS, N_BLK, SPAN, D), 1.0, 6.0, ((1, 4), (2, 8))),
        "segments": draw_segments(jax.random.fold_in(keys[13], 71), 0),
        "bucket_table": draw_bucket_table(jax.random.fold_in(keys[13], 71), 0),
        "norm_gain": jnp.clip(1.0 + 0.15 * jax.random.normal(keys[3], (D,), jnp.float32), 0.25, 1.75).astype(jnp.bfloat16),
        "w_query": bell_draw(keys[4], (D, HEADS * HD), (4 * D) ** -0.5, 0.09375, ((0, 32),)),
        "w_key": bell_draw(keys[5], (D, HEADS * HD), (4 * D) ** -0.5, 0.09375, ((0, 32),)),
        "w_value": bell_draw(keys[6], (D, HEADS * HD), D ** -0.5, 0.1875, ((0, 32),)),
        "w_out": bell_draw(keys[7], (HEADS * HD, D), (D // 4) ** -0.5, 0.375, ((0, 32),)),
        "rel_bias": bell_draw(keys[8], (HEADS * BUCKETS,), 1.0, 4.0, ((0, 32),)),
        "ff_gain": jnp.clip(1.0 + 0.15 * jax.random.normal(keys[9], (D,), jnp.float32), 0.25, 1.75).astype(jnp.bfloat16),
        "w_in": bell_draw(keys[10], (D, FF), D ** -0.5, 0.1875, ((0, 32),)),
        "w_down": bell_draw(keys[11], (FF, D), FF ** -0.5, 0.09375, ((0, 32),)),
        "cotangent": bell_draw(keys[12], (SEQS, N_BLK, SPAN, D), 1.0, 6.0, ((1, 4), (2, 8))),
    }


@jax.custom_vjp
def low(v):
    return lax.optimization_barrier(v.astype(jnp.bfloat16)).astype(jnp.float32)

@jax.custom_vjp
def low_back(v):
    return v

def low_keep(v):
    return (low(v), None)

def low_pass(kept, grad):
    return (grad,)

def back_keep(v):
    return (v, None)

def back_low(kept, grad):
    return (low(grad),)
low.defvjp(low_keep, low_pass)
low_back.defvjp(back_keep, back_low)
EPS = 1e-06
FLOOR = -1e+30

def rounded_both(values):
    return low(low_back(values))

def product(left, right):
    return jnp.dot(left, right, precision=lax.Precision.HIGHEST)

def rms_scale(token_rows, gain_vector):
    return token_rows * lax.rsqrt(lax.optimization_barrier(jnp.mean(token_rows * token_rows, axis=-1, keepdims=True)) + EPS) * gain_vector

def attend_one(pieces, pair_bucket):
    queries, key_rows, value_rows, segment_row, rel_row = pieces
    position_bias = rel_row[pair_bucket]
    scores = low_back(product(queries, key_rows.T) + position_bias)
    scores = jnp.where(segment_row[:, None] == segment_row[None, :], scores, FLOOR)
    row_max = lax.optimization_barrier(jnp.max(scores, axis=1, keepdims=True))
    log_total = row_max + jnp.log(lax.optimization_barrier(jnp.sum(jnp.exp(scores - row_max), axis=1, keepdims=True)))
    probs = low(jnp.exp(scores - log_total))
    return rounded_both(product(probs, value_rows))

def encoder_layer(token_rows, gain_one, query_w, key_w, value_w, out_w, rel_flat, gain_two, in_w, down_w, segment_rows, pair_bucket):
    first_in = low(rms_scale(token_rows, gain_one))

    def heads_of(weight):
        made_rows = rounded_both(product(first_in, weight))
        return made_rows.reshape(SEQS, LEN, HEADS, HD).transpose(0, 2, 1, 3).reshape(SEQS * HEADS, LEN, HD)
    segment_items = jnp.repeat(segment_rows, HEADS, axis=0)
    rel_items = jnp.tile(rel_flat.reshape(HEADS, BUCKETS), (SEQS, 1))
    attended = lax.map(jax.checkpoint(partial(attend_one, pair_bucket=pair_bucket)), (heads_of(query_w), heads_of(key_w), heads_of(value_w), segment_items, rel_items))
    attn_rows = attended.reshape(SEQS, HEADS, LEN, HD).transpose(0, 2, 1, 3).reshape(SEQS * LEN, HEADS * HD)
    hidden_one = token_rows + low_back(product(attn_rows, out_w))
    second_in = low(rms_scale(hidden_one, gain_two))
    activated = low(jax.nn.gelu(low_back(product(second_in, in_w)), approximate=True))
    return hidden_one + product(activated, down_w)

def reference(inputs, segments, bucket_table, norm_gain, w_query, w_key, w_value, w_out, rel_bias, ff_gain, w_in, w_down, cotangent):
    token_rows = inputs.reshape(SEQS * LEN, D).astype(jnp.float32)
    segment_rows = segments.reshape(SEQS, LEN)
    places = jnp.arange(LEN, dtype=jnp.int32)
    offsets = (jnp.clip(places[None, :] - places[:, None], -MAXREL, MAXREL) + MAXREL).astype(jnp.int32)
    pair_bucket = bucket_table[offsets]
    layer_rows, backward = jax.vjp(partial(encoder_layer, segment_rows=segment_rows, pair_bucket=pair_bucket), token_rows, norm_gain.astype(jnp.float32), w_query.astype(jnp.float32), w_key.astype(jnp.float32), w_value.astype(jnp.float32), w_out.astype(jnp.float32), rel_bias.astype(jnp.float32), ff_gain.astype(jnp.float32), w_in.astype(jnp.float32), w_down.astype(jnp.float32))
    grads = backward(cotangent.reshape(SEQS * LEN, D).astype(jnp.float32))
    return (layer_rows.astype(jnp.bfloat16).reshape(inputs.shape), grads[0].astype(jnp.bfloat16).reshape(inputs.shape), grads[1], grads[2], grads[3], grads[4], grads[5], grads[6], grads[7], grads[8], grads[9])
```

```python
import functools

import jax
import jax.numpy as jnp
import numpy as np
from jax import lax
from jax.experimental import pallas as pl
from jax.experimental.pallas import tpu as pltpu
from jax.sharding import PartitionSpec as P

HEADS = 16
HD = 64
BUCKETS = 32
MAXREL = 128
EPS = 1e-06
FLOOR = -1e30


def from_behind(block, axis, distance):
    devices = range(lax.axis_size(axis))
    route = [((i - distance) % len(devices), i) for i in devices]
    return lax.ppermute(block, axis, route)


def rms_scale(token_rows, gain_vector):
    return (
        token_rows
        * lax.rsqrt(jnp.mean(token_rows * token_rows, axis=-1, keepdims=True) + EPS)
        * gain_vector
    )


def smooth(values):
    return jax.nn.gelu(values, approximate=True)


def band_layout(span_len):
    tile_side = min(128, span_len)
    reach = MAXREL // tile_side + 2
    return (tile_side, span_len // tile_side, reach)


def band_tables(bucket_table, rel_here, span_len):
    tile_side, _, reach = band_layout(span_len)
    kinds = 2 * reach + 1
    gaps = lax.iota(jnp.int32, kinds) - reach
    rows_in = lax.iota(jnp.int32, tile_side)
    offsets = gaps[:, None, None] * tile_side + rows_in[None, None, :] - rows_in[None, :, None]
    lookup = jnp.clip(offsets, -MAXREL, MAXREL) + MAXREL
    bucket = jnp.take(bucket_table, lookup.reshape(-1), axis=0)
    onehot = (bucket[:, None] == lax.iota(jnp.int32, BUCKETS)[None, :]).astype(jnp.float32)
    band_bias = jnp.dot(rel_here, onehot.T, precision=lax.Precision.HIGHEST)
    return (band_bias.reshape(rel_here.shape[0], kinds, tile_side, tile_side), onehot)


def band_index(block_gap, span_len):
    _, tiles, reach = band_layout(span_len)
    row_tile = lax.iota(jnp.int32, tiles)[:, None, None, None]
    col_tile = lax.iota(jnp.int32, tiles)[None, None, :, None]
    return jnp.clip(block_gap * tiles + col_tile - row_tile, -reach, reach) + reach


def bias_tile(band_bias, block_gap, span_len):
    heads_count, kinds, tile_side, _ = band_bias.shape
    tiles = span_len // tile_side
    which = band_index(block_gap, span_len)
    result = jnp.zeros((heads_count, tiles, tile_side, tiles, tile_side), jnp.float32)
    for kind in range(kinds):
        result = jnp.where(which[None] == kind, band_bias[:, kind][:, None, :, None, :], result)
    return result.reshape(heads_count, span_len, span_len)


def band_sums(tile_sum, block_gap, span_len):
    tile_side, tiles, reach = band_layout(span_len)
    heads_count = tile_sum.shape[0]
    split_sum = tile_sum.reshape(heads_count, tiles, tile_side, tiles, tile_side)
    which = band_index(block_gap, span_len)
    parts = []
    for kind in range(2 * reach + 1):
        parts.append(jnp.sum(jnp.where(which[None] == kind, split_sum, 0.0), axis=(1, 3)))
    return jnp.stack(parts, axis=1).reshape(heads_count, -1)


def pass_grads(key_grad, value_grad):
    return (
        from_behind(key_grad.astype(jnp.bfloat16), "blk", 1).astype(key_grad.dtype),
        from_behind(value_grad.astype(jnp.bfloat16), "blk", 1).astype(value_grad.dtype),
    )


def ring_body(
    inputs,
    segments,
    bucket_table,
    norm_gain,
    w_query,
    w_key,
    w_value,
    w_out,
    rel_bias,
    ff_gain,
    w_in,
    w_down,
    cotangent,
):
    seq_count, _, part_len, width = inputs.shape
    cycle_size = lax.axis_size("blk")
    head_groups = lax.axis_size("head")
    heads_here = HEADS // head_groups
    span_len = part_len * head_groups
    cycle_place = lax.axis_index("blk")
    head_place = lax.axis_index("head")
    gathered = (
        lax.all_gather(norm_gain, ("head", "blk"), axis=0, tiled=True),
        lax.all_gather(w_query, ("head", "blk"), axis=0, tiled=True),
        lax.all_gather(w_key, ("head", "blk"), axis=0, tiled=True),
        lax.all_gather(w_value, ("head", "blk"), axis=0, tiled=True),
        lax.all_gather(w_out, ("head", "blk"), axis=0, tiled=True),
        lax.all_gather(rel_bias, ("head", "blk"), axis=0, tiled=True),
        lax.all_gather(ff_gain, ("head", "blk"), axis=0, tiled=True),
        lax.all_gather(w_in, ("head", "blk"), axis=0, tiled=True),
        lax.all_gather(w_down, ("head", "blk"), axis=0, tiled=True),
    )
    gain_one, query_w, key_w, value_w, out_w, rel_flat, gain_two, in_w, down_w = gathered
    token_rows = inputs.reshape(-1, width).astype(jnp.float32)
    normed, norm_one_back = jax.vjp(rms_scale, token_rows, gain_one.astype(jnp.float32))
    first_in = normed.astype(jnp.bfloat16)

    def project(weight):
        made_rows = jnp.dot(first_in, weight, preferred_element_type=jnp.float32)
        return made_rows.astype(jnp.bfloat16).reshape(seq_count, part_len, -1)

    queries, keys_home, values_home = (
        lax.all_to_all(project(query_w), "head", split_axis=2, concat_axis=1, tiled=True),
        lax.all_to_all(project(key_w), "head", split_axis=2, concat_axis=1, tiled=True),
        lax.all_to_all(project(value_w), "head", split_axis=2, concat_axis=1, tiled=True),
    )
    head_shape = (seq_count, span_len, heads_here, HD)
    queries = queries.reshape(head_shape)
    keys_home = keys_home.reshape(head_shape)
    values_home = values_home.reshape(head_shape)
    rel_table = rel_flat.astype(jnp.float32).reshape(HEADS, BUCKETS)
    rel_here = lax.dynamic_slice_in_dim(rel_table, head_place * heads_here, heads_here, 0)
    band_bias, band_onehot = band_tables(bucket_table, rel_here, span_len)

    def tile_scores(query_rows, key_rows, query_block, key_block):
        query_ids = lax.dynamic_index_in_dim(segments, query_block, 1, keepdims=False)
        key_ids = lax.dynamic_index_in_dim(segments, key_block, 1, keepdims=False)
        plain_scores = (
            jnp.einsum("sihd,sjhd->shij", query_rows, key_rows, preferred_element_type=jnp.float32)
            + bias_tile(band_bias, key_block - query_block, span_len)[None]
        )
        same_doc = query_ids[:, None, :, None] == key_ids[:, None, None, :]
        return jnp.where(same_doc, plain_scores, FLOOR)

    first_scores = tile_scores(queries, keys_home, cycle_place, cycle_place)
    row_max = jnp.max(first_scores, axis=-1)
    first_weights = jnp.exp(first_scores - row_max[..., None])
    row_total = jnp.sum(first_weights, axis=-1)
    summed = jnp.einsum(
        "shij,sjhd->sihd",
        first_weights.astype(jnp.bfloat16),
        values_home,
        preferred_element_type=jnp.float32,
    )

    def forward_turn(cycle_turn, state_now):
        old_max, old_total, old_summed, key_rows, value_rows = state_now
        key_rows, value_rows = from_behind((key_rows, value_rows), "blk", 1)
        source = (cycle_place - cycle_turn) % cycle_size
        scores = tile_scores(queries, key_rows, cycle_place, source)
        new_max = jnp.maximum(old_max, jnp.max(scores, axis=-1))
        shrink = jnp.exp(old_max - new_max)
        weights_now = jnp.exp(scores - new_max[..., None])
        new_total = old_total * shrink + jnp.sum(weights_now, axis=-1)
        new_summed = old_summed * jnp.transpose(shrink, (0, 2, 1))[..., None] + jnp.einsum(
            "shij,sjhd->sihd",
            weights_now.astype(jnp.bfloat16),
            value_rows,
            preferred_element_type=jnp.float32,
        )
        return (new_max, new_total, new_summed, key_rows, value_rows)

    row_max, row_total, summed, _, _ = lax.fori_loop(
        1, cycle_size, forward_turn, (row_max, row_total, summed, keys_home, values_home)
    )
    log_total = row_max + jnp.log(row_total)
    attended = summed / jnp.transpose(row_total, (0, 2, 1))[..., None]
    attended_low = attended.astype(jnp.bfloat16).reshape(seq_count, span_len, heads_here * HD)
    attn_rows = lax.all_to_all(
        attended_low, "head", split_axis=1, concat_axis=2, tiled=True
    ).reshape(-1, HEADS * HD)
    hidden_one = token_rows + jnp.dot(attn_rows, out_w, preferred_element_type=jnp.float32)
    normed_two, norm_two_back = jax.vjp(rms_scale, hidden_one, gain_two.astype(jnp.float32))
    second_in = normed_two.astype(jnp.bfloat16)
    upward = jnp.dot(second_in, in_w, preferred_element_type=jnp.float32)
    activated, smooth_back = jax.vjp(smooth, upward)
    activated_low = activated.astype(jnp.bfloat16)
    layer_rows = hidden_one + jnp.dot(activated_low, down_w, preferred_element_type=jnp.float32)
    layer_out = layer_rows.astype(jnp.bfloat16).reshape(inputs.shape)
    back_query, back_key, back_value, back_out, back_in, back_down = (
        query_w,
        key_w,
        value_w,
        out_w,
        in_w,
        down_w,
    )
    incoming_low = cotangent.reshape(-1, width)
    incoming = incoming_low.astype(jnp.float32)
    grad_down = jnp.dot(activated_low.T, incoming_low, preferred_element_type=jnp.float32)
    (up_grad,) = smooth_back(jnp.dot(incoming_low, back_down.T, preferred_element_type=jnp.float32))
    up_low = up_grad.astype(jnp.bfloat16)
    grad_in = jnp.dot(second_in.T, up_low, preferred_element_type=jnp.float32)
    hidden_part, grad_gain_two = norm_two_back(
        jnp.dot(up_low, back_in.T, preferred_element_type=jnp.float32)
    )
    hidden_grad = incoming + hidden_part
    branch_low = hidden_grad.astype(jnp.bfloat16)
    grad_out = jnp.dot(attn_rows.T, branch_low, preferred_element_type=jnp.float32)
    attn_grad_low = jnp.dot(branch_low, back_out.T, preferred_element_type=jnp.float32).astype(
        jnp.bfloat16
    )
    grad_heads = lax.all_to_all(
        attn_grad_low.reshape(seq_count, part_len, HEADS * HD),
        "head",
        split_axis=2,
        concat_axis=1,
        tiled=True,
    ).reshape(head_shape)
    row_delta = jnp.transpose(
        jnp.sum(grad_heads.astype(jnp.float32) * attended, axis=-1), (0, 2, 1)
    )

    def tile_grads(
        query_rows, grad_rows, log_rows, delta_rows, key_rows, value_rows, query_block, key_block
    ):
        scores = tile_scores(query_rows, key_rows, query_block, key_block)
        probs = jnp.exp(scores - log_rows[..., None])
        value_part = jnp.einsum(
            "shij,sihd->sjhd",
            probs.astype(jnp.bfloat16),
            grad_rows,
            preferred_element_type=jnp.float32,
        )
        prob_grad = jnp.einsum(
            "sihd,sjhd->shij", grad_rows, value_rows, preferred_element_type=jnp.float32
        )
        score_low = (probs * (prob_grad - delta_rows[..., None])).astype(jnp.bfloat16)
        query_part = jnp.einsum(
            "shij,sjhd->sihd", score_low, key_rows, preferred_element_type=jnp.float32
        )
        key_part = jnp.einsum(
            "shij,sihd->sjhd", score_low, query_rows, preferred_element_type=jnp.float32
        )
        tile_sum = jnp.sum(score_low.astype(jnp.float32), axis=0)
        rel_part = jnp.dot(
            band_sums(tile_sum, key_block - query_block, span_len),
            band_onehot,
            precision=lax.Precision.HIGHEST,
        )
        return (query_part, key_part, value_part, rel_part)

    query_grad, key_grad, value_grad, rel_grad = tile_grads(
        queries, grad_heads, log_total, row_delta, keys_home, values_home, cycle_place, cycle_place
    )

    def key_turn(cycle_turn, state_now):
        key_rows, value_rows, key_sum, value_sum, query_sum, rel_sum = state_now
        key_sum, value_sum = pass_grads(key_sum, value_sum)
        key_rows, value_rows = from_behind((key_rows, value_rows), "blk", 1)
        source = (cycle_place - cycle_turn) % cycle_size
        query_part, key_part, value_part, rel_part = tile_grads(
            queries, grad_heads, log_total, row_delta, key_rows, value_rows, cycle_place, source
        )
        return (
            key_rows,
            value_rows,
            key_sum + key_part,
            value_sum + value_part,
            query_sum + query_part,
            rel_sum + rel_part,
        )

    state_first = (keys_home, values_home, key_grad, value_grad, query_grad, rel_grad)
    _, _, key_grad, value_grad, query_grad, rel_grad = lax.fori_loop(
        1, cycle_size, key_turn, state_first
    )
    key_grad, value_grad = pass_grads(key_grad, value_grad)
    block_shape = (seq_count, span_len, heads_here * HD)
    query_rows, key_rows_back, value_rows_back = (
        lax.all_to_all(
            query_grad.astype(jnp.bfloat16).reshape(block_shape),
            "head",
            split_axis=1,
            concat_axis=2,
            tiled=True,
        ),
        lax.all_to_all(
            key_grad.astype(jnp.bfloat16).reshape(block_shape),
            "head",
            split_axis=1,
            concat_axis=2,
            tiled=True,
        ),
        lax.all_to_all(
            value_grad.astype(jnp.bfloat16).reshape(block_shape),
            "head",
            split_axis=1,
            concat_axis=2,
            tiled=True,
        ),
    )
    query_rows = query_rows.reshape(-1, HEADS * HD)
    key_rows_back = key_rows_back.reshape(-1, HEADS * HD)
    value_rows_back = value_rows_back.reshape(-1, HEADS * HD)
    grad_query = jnp.dot(first_in.T, query_rows, preferred_element_type=jnp.float32)
    grad_key = jnp.dot(first_in.T, key_rows_back, preferred_element_type=jnp.float32)
    grad_value = jnp.dot(first_in.T, value_rows_back, preferred_element_type=jnp.float32)
    first_grad = (
        jnp.dot(query_rows, back_query.T, preferred_element_type=jnp.float32)
        + jnp.dot(key_rows_back, back_key.T, preferred_element_type=jnp.float32)
        + jnp.dot(value_rows_back, back_value.T, preferred_element_type=jnp.float32)
    )
    input_part, grad_gain_one = norm_one_back(first_grad)
    input_grad = (hidden_grad + input_part).astype(jnp.bfloat16).reshape(inputs.shape)
    rel_full = lax.dynamic_update_slice_in_dim(
        jnp.zeros((HEADS, BUCKETS), jnp.float32), rel_grad, head_place * heads_here, 0
    ).reshape(-1)
    shards = tuple(
        (
            lax.psum_scatter(grad_gain_one, ("head", "blk"), scatter_dimension=0, tiled=True),
            lax.psum_scatter(grad_query, ("head", "blk"), scatter_dimension=0, tiled=True),
            lax.psum_scatter(grad_key, ("head", "blk"), scatter_dimension=0, tiled=True),
            lax.psum_scatter(grad_value, ("head", "blk"), scatter_dimension=0, tiled=True),
            lax.psum_scatter(grad_out, ("head", "blk"), scatter_dimension=0, tiled=True),
            lax.psum_scatter(rel_full, ("head", "blk"), scatter_dimension=0, tiled=True),
            lax.psum_scatter(grad_gain_two, ("head", "blk"), scatter_dimension=0, tiled=True),
            lax.psum_scatter(grad_in, ("head", "blk"), scatter_dimension=0, tiled=True),
            lax.psum_scatter(grad_down, ("head", "blk"), scatter_dimension=0, tiled=True),
        )
    )
    return (
        layer_out,
        input_grad,
        shards[0],
        shards[1],
        shards[2],
        shards[3],
        shards[4],
        shards[5],
        shards[6],
        shards[7],
        shards[8],
    )


TQ = 512
KT = 512
MARGIN = 256
AUG = 80
NT = (((1,), (1,)), ((), ()))


def nn(left, right):
    return jnp.dot(left, right, preferred_element_type=jnp.float32)


def flipped(block):
    return block.astype(jnp.float32).T.astype(jnp.bfloat16)


def ones_row(width):
    first = lax.broadcasted_iota(jnp.int32, (AUG - HD, width), 0) == 0
    return jnp.where(first, 1.0, 0.0).astype(jnp.bfloat16)


def pieces_of(seq_count, part_len, groups):
    for seq in range(seq_count):
        for near in range(2):
            for source in range(groups):
                yield seq, near, source, slice((near * seq_count + seq) * part_len, (near * seq_count + seq + 1) * part_len)


def lanes_of(ref, lead, tile_at, per_tile, part_len, lane_base):
    parts = [ref[lead + (tile_at * per_tile + k, slice(None), pl.ds(lane_base, part_len))] for k in range(per_tile)]
    return parts[0] if per_tile == 1 else jnp.concatenate(parts, axis=1)


def tile_class(edge_ref, row, key_at, query_at):
    first_start, last_start, first_end, last_end = (edge_ref[row * 4 + k] for k in range(4))
    touched = (key_at + KT > first_start) & (key_at < last_end)
    gap = key_at - query_at
    whole = (key_at >= last_start) & (key_at + KT <= first_end)
    plain = whole & ((gap + KT <= -MAXREL + 1) | (gap >= TQ + MAXREL - 1))
    strip_at = jnp.clip(gap, -(KT + MARGIN), TQ + MARGIN) + KT + MARGIN
    return touched, plain, gap, pl.ds(pl.multiple_of(strip_at, 256), KT)


def masked(scores, bias, key_at, start_row, end_row):
    places = lax.broadcasted_iota(jnp.int32, scores.shape, 0) + key_at
    return jnp.where((places >= start_row) & (places < end_row), scores + bias, FLOOR)


def attend_kernel(chips, base_ref, edge_ref, far_ref, q_ref, *refs):
    kv_refs = refs[:chips]
    start_ref, end_ref, bias_ref, o_ref, ob_ref, lse_ref, k_rows, v_aug, top_ref, acc_ref = refs[chips:]
    groups, _, span = q_ref.shape
    blocks, seq_count, span_len, _ = k_rows.shape
    part_len = span_len // groups
    per_tile = TQ // part_len
    tiles, key_tiles = span_len // TQ, span_len // KT
    per_key = KT // part_len
    for far in range(chips):
        for seq, near, source, lanes in pieces_of(seq_count, part_len, groups):
            block = 2 * far + near
            k_rows[block, seq, source * part_len : (source + 1) * part_len, :] = flipped(kv_refs[far][source, :HD, lanes])
            at = source % per_key * part_len
            v_aug[block, seq, source // per_key, :HD, at : at + part_len] = kv_refs[far][source, HD:, lanes]
    for block in range(blocks):
        for seq in range(seq_count):
            for tile in range(key_tiles):
                v_aug[block, seq, tile, HD:, :] = ones_row(KT)

    for seq in range(seq_count):
        for near in range(2):
            lane_base = (near * seq_count + seq) * part_len

            def query_tile(tile, _, seq=seq, near=near, lane_base=lane_base):
                query_at = base_ref[near] + tile * TQ
                row = (near * seq_count + seq) * tiles + tile
                queries = lanes_of(q_ref, (), tile, per_tile, part_len, lane_base)
                top_ref[...] = jnp.full_like(top_ref, FLOOR)
                acc_ref[...] = jnp.zeros_like(acc_ref)
                start_row = start_ref[near, seq, pl.ds(tile, 1), :]
                end_row = end_ref[near, seq, pl.ds(tile, 1), :]

                def take(scores, shift, block, key_tile):
                    old_top = top_ref[0:1, :]
                    new_top = jnp.maximum(old_top, jnp.max(scores, axis=0, keepdims=True) + shift)
                    weights = jnp.exp(scores - (new_top - shift))
                    acc_ref[...] = acc_ref[...] * jnp.exp(old_top - new_top) + nn(
                        v_aug[block, seq, key_tile], weights.astype(jnp.bfloat16)
                    )
                    top_ref[0:1, :] = new_top

                def key_step(step, _):
                    block, key_tile = step // key_tiles, step % key_tiles
                    key_at = base_ref[block] + key_tile * KT
                    touched, plain, gap, strip = tile_class(edge_ref, row, key_at, query_at)

                    def raw():
                        keys = k_rows[block, seq, pl.ds(pl.multiple_of(key_tile * KT, KT), KT), :]
                        return nn(keys, queries)

                    @pl.when(touched & plain)
                    def _():
                        take(raw(), jnp.where(gap < 0, far_ref[0], far_ref[1]), block, key_tile)

                    @pl.when(touched & jnp.logical_not(plain))
                    def _():
                        take(masked(raw(), bias_ref[strip, :], key_at, start_row, end_row), 0.0, block, key_tile)

                    return 0

                lax.fori_loop(0, blocks * key_tiles, key_step, 0)
                total = acc_ref[HD : HD + 1, :]
                outs = acc_ref[:HD, :] / total
                lse_ref[near, seq, pl.ds(tile, 1), :] = top_ref[0:1, :] + jnp.log(total)
                for k in range(per_tile):
                    part = outs[:, k * part_len : (k + 1) * part_len]
                    o_ref[tile * per_tile + k, :, lane_base : lane_base + part_len] = part
                    ob_ref[tile * per_tile + k, :, lane_base : lane_base + part_len] = part.astype(jnp.bfloat16)
                return 0

            lax.fori_loop(0, tiles, query_tile, 0)


def attend_back_kernel(chips, base_ref, edge_ref, far_ref, q_ref, g_ref, o_ref, lse_ref, *refs):
    kv_refs = refs[:chips]
    start_ref, end_ref, bias_ref, dq_ref = refs[chips : chips + 4]
    dkv_refs = refs[chips + 4 : 2 * chips + 4]
    band_ref, sides_ref, k_rows, v_rows, k_aug, dk_acc, dv_acc, dq_acc = refs[2 * chips + 4 :]
    groups, _, span = q_ref.shape
    blocks, seq_count, span_len, _ = k_rows.shape
    part_len = span_len // groups
    per_tile = TQ // part_len
    tiles, key_tiles = span_len // TQ, span_len // KT
    per_key = KT // part_len
    for far in range(chips):
        for seq, near, source, lanes in pieces_of(seq_count, part_len, groups):
            block = 2 * far + near
            rows = slice(source * part_len, (source + 1) * part_len)
            piece = kv_refs[far][source, :HD, lanes]
            k_rows[block, seq, rows, :] = flipped(piece)
            v_rows[block, seq, rows, :] = flipped(kv_refs[far][source, HD:, lanes])
            at = source % per_key * part_len
            k_aug[block, seq, source // per_key, :HD, at : at + part_len] = piece
    for block in range(blocks):
        for seq in range(seq_count):
            for tile in range(key_tiles):
                k_aug[block, seq, tile, HD:, :] = ones_row(KT)
    dk_acc[...] = jnp.zeros_like(dk_acc)
    dv_acc[...] = jnp.zeros_like(dv_acc)
    band_ref[...] = jnp.zeros_like(band_ref)
    sides_ref[...] = jnp.zeros_like(sides_ref)

    for seq in range(seq_count):
        for near in range(2):
            lane_base = (near * seq_count + seq) * part_len

            def query_tile(tile, _, seq=seq, near=near, lane_base=lane_base):
                query_at = base_ref[near] + tile * TQ
                row = (near * seq_count + seq) * tiles + tile
                queries = lanes_of(q_ref, (), tile, per_tile, part_len, lane_base)
                grads = lanes_of(g_ref, (), tile, per_tile, part_len, lane_base)
                outs = lanes_of(o_ref, (), tile, per_tile, part_len, lane_base)
                delta = jnp.sum(grads.astype(jnp.float32) * outs, axis=0, keepdims=True)
                query_rows, grad_rows = flipped(queries), flipped(grads)
                lse = lse_ref[near, seq, pl.ds(tile, 1), :]
                start_row = start_ref[near, seq, pl.ds(tile, 1), :]
                end_row = end_ref[near, seq, pl.ds(tile, 1), :]
                dq_acc[...] = jnp.zeros_like(dq_acc)

                def take(scores, shift, block, key_tile):
                    rows = pl.ds(pl.multiple_of(key_tile * KT, KT), KT)
                    probs = jnp.exp(scores - (lse - shift))
                    score_grad = probs * (nn(v_rows[block, seq, rows, :], grads) - delta)
                    score_low = score_grad.astype(jnp.bfloat16)
                    dv_acc[block, seq, rows, :] += nn(probs.astype(jnp.bfloat16), grad_rows)
                    dk_acc[block, seq, rows, :] += nn(score_low, query_rows)
                    made = nn(k_aug[block, seq, key_tile], score_low)
                    dq_acc[...] += made
                    return score_grad, made[HD : HD + 1, :]

                def key_step(step, _):
                    block, key_tile = step // key_tiles, step % key_tiles
                    key_at = base_ref[block] + key_tile * KT
                    touched, plain, gap, strip = tile_class(edge_ref, row, key_at, query_at)

                    def raw():
                        keys = k_rows[block, seq, pl.ds(pl.multiple_of(key_tile * KT, KT), KT), :]
                        return nn(keys, queries)

                    @pl.when(touched & plain)
                    def _():
                        _, sums = take(raw(), jnp.where(gap < 0, far_ref[0], far_ref[1]), block, key_tile)
                        side = (gap > 0).astype(jnp.int32)
                        sides_ref[pl.ds(side, 1), :] += sums

                    @pl.when(touched & jnp.logical_not(plain))
                    def _():
                        whole_grad, _ = take(
                            masked(raw(), bias_ref[strip, :], key_at, start_row, end_row), 0.0, block, key_tile
                        )
                        band_ref[strip, :] += whole_grad

                    return 0

                lax.fori_loop(0, blocks * key_tiles, key_step, 0)
                for k in range(per_tile):
                    part = dq_acc[:HD, k * part_len : (k + 1) * part_len].astype(jnp.bfloat16)
                    dq_ref[tile * per_tile + k, :, lane_base : lane_base + part_len] = part
                return 0

            lax.fori_loop(0, tiles, query_tile, 0)
    for far in range(chips):
        for seq, near, source, lanes in pieces_of(seq_count, part_len, groups):
            block = 2 * far + near
            rows = slice(source * part_len, (source + 1) * part_len)
            dkv_refs[far][source, :HD, lanes] = dk_acc[block, seq, rows, :].T.astype(jnp.bfloat16)
            dkv_refs[far][source, HD:, lanes] = dv_acc[block, seq, rows, :].T.astype(jnp.bfloat16)


def strip_places():
    width = TQ + 128
    lane = np.arange(width)
    lane = np.where(lane < TQ, lane, lane - width)
    offset = 128 * (np.arange(TQ // 128 + 2)[:, None] - 1) - lane[None, :]
    return np.clip(offset, -MAXREL, MAXREL) + MAXREL


def strip_kernel(far_ref, wave_ref, strip_ref):
    near_blocks, _, width = wave_ref.shape
    first = KT + MARGIN - 128
    strip_ref[:first, :] = jnp.full((first, TQ), far_ref[0], jnp.float32)
    for k in range(near_blocks):
        spread = jnp.broadcast_to(wave_ref[k], (128, width))
        turned = pltpu.roll(spread, 0, 1, stride=1, stride_axis=0)
        strip_ref[first + 128 * k : first + 128 * (k + 1), :] = turned[:, :TQ]
    last = first + 128 * near_blocks
    strip_ref[last:, :] = jnp.full((strip_ref.shape[0] - last, TQ), far_ref[1], jnp.float32)


def bias_strip(far_bias, waves):
    return pl.pallas_call(
        strip_kernel,
        name="bias_strip",
        out_shape=jax.ShapeDtypeStruct((2 * KT + 2 * MARGIN + TQ, TQ), jnp.float32),
        in_specs=[SMEM, VMEM],
        out_specs=VMEM,
        compiler_params=pltpu.CompilerParams(vmem_limit_bytes=32 * 2**20),
    )(far_bias, waves)


def band_kernel(band_ref, sides_ref, near_ref, far_ref):
    near_blocks, _, width = near_ref.shape
    first = KT + MARGIN - 128
    last = first + 128 * near_blocks
    left = jnp.sum(band_ref[:first, :], axis=0, keepdims=True) + sides_ref[0:1, :]
    right = jnp.sum(band_ref[last:, :], axis=0, keepdims=True) + sides_ref[1:2, :]
    far_ref[...] = jnp.concatenate([left, right, jnp.zeros((6, TQ), jnp.float32)], axis=0)
    for k in range(near_blocks):
        rows = band_ref[first + 128 * k : first + 128 * (k + 1), :]
        spread = jnp.concatenate([rows, jnp.zeros((128, width - TQ), jnp.float32)], axis=1)
        row = lax.broadcasted_iota(jnp.int32, spread.shape, 0)
        for step in (1, 2, 4):
            spread = jnp.where((row & step) != 0, pltpu.roll(spread, width - step, 1), spread)
        total = spread[:8, :]
        for at in range(8, 128, 8):
            total = total + pltpu.roll(spread[at : at + 8, :], width - at, 1)
        near_ref[k] = jnp.sum(total, axis=0, keepdims=True)


def band_sums_of(band, sides):
    return pl.pallas_call(
        band_kernel,
        name="band_sums",
        out_shape=(
            jax.ShapeDtypeStruct((TQ // 128 + 2, 1, TQ + 128), jnp.float32),
            jax.ShapeDtypeStruct((8, TQ), jnp.float32),
        ),
        in_specs=[VMEM, VMEM],
        out_specs=(VMEM, VMEM),
        compiler_params=pltpu.CompilerParams(vmem_limit_bytes=32 * 2**20),
    )(band, sides)


SMEM = pl.BlockSpec(memory_space=pltpu.SMEM)
VMEM = pl.BlockSpec(memory_space=pltpu.VMEM)


def attend(base, edges, far_bias, q, kvs, starts, ends, bias):
    chips = len(kvs)
    groups, _, span = q.shape
    _, seq_count, tiles, _ = starts.shape
    blocks, span_len = 2 * chips, tiles * TQ
    return pl.pallas_call(
        functools.partial(attend_kernel, chips),
        name="attend",
        out_shape=(
            jax.ShapeDtypeStruct(q.shape, jnp.float32),
            jax.ShapeDtypeStruct(q.shape, jnp.bfloat16),
            jax.ShapeDtypeStruct(starts.shape, jnp.float32),
        ),
        in_specs=[SMEM] * 3 + [VMEM] * (1 + chips + 3),
        out_specs=(VMEM,) * 3,
        scratch_shapes=[
            pltpu.VMEM((blocks, seq_count, span_len, HD), jnp.bfloat16),
            pltpu.VMEM((blocks, seq_count, span_len // KT, AUG, KT), jnp.bfloat16),
            pltpu.VMEM((8, TQ), jnp.float32),
            pltpu.VMEM((AUG, TQ), jnp.float32),
        ],
        compiler_params=pltpu.CompilerParams(vmem_limit_bytes=48 * 2**20),
    )(base, edges, far_bias, q, *kvs, starts, ends, bias)


def attend_back(base, edges, far_bias, q, g, o, lse, kvs, starts, ends, bias):
    chips = len(kvs)
    groups, _, span = q.shape
    _, seq_count, tiles, _ = starts.shape
    blocks, span_len = 2 * chips, tiles * TQ
    low = jax.ShapeDtypeStruct(q.shape, jnp.bfloat16)
    made = pl.pallas_call(
        functools.partial(attend_back_kernel, chips),
        name="attend_back",
        out_shape=(low,)
        + (jax.ShapeDtypeStruct(kvs[0].shape, jnp.bfloat16),) * chips
        + (jax.ShapeDtypeStruct(bias.shape, jnp.float32), jax.ShapeDtypeStruct((8, TQ), jnp.float32)),
        in_specs=[SMEM] * 3 + [VMEM] * (4 + chips + 3),
        out_specs=(VMEM,) * (3 + chips),
        scratch_shapes=[
            pltpu.VMEM((blocks, seq_count, span_len, HD), jnp.bfloat16),
            pltpu.VMEM((blocks, seq_count, span_len, HD), jnp.bfloat16),
            pltpu.VMEM((blocks, seq_count, span_len // KT, AUG, KT), jnp.bfloat16),
            pltpu.VMEM((blocks, seq_count, span_len, HD), jnp.float32),
            pltpu.VMEM((blocks, seq_count, span_len, HD), jnp.float32),
            pltpu.VMEM((AUG, TQ), jnp.float32),
        ],
        compiler_params=pltpu.CompilerParams(vmem_limit_bytes=56 * 2**20),
    )(base, edges, far_bias, q, g, o, lse, *kvs, starts, ends, bias)
    return made[0], made[1 : 1 + chips], made[-2], made[-1]


AXES = ("head", "blk")


def trade(block, axis, bit):
    size = lax.axis_size(axis)
    return lax.ppermute(block, axis, [(i, i ^ bit) for i in range(size)])


def mate(block):
    return trade(block, "blk", 1)


def across_x(block):
    return trade(block, "blk", 2)


def across_y(block):
    return trade(block, "head", 1)


def across_z(block, distance):
    return trade(block, "head", 2 * distance)


def copy_kernel(plan, slots_ref, *arrays):
    for source, source_rows, target, target_rows, count in plan:
        views = []
        for which, (slot, scale, first, columns) in ((source, source_rows), (target, target_rows)):
            begin = first if slot is None else pl.multiple_of(slots_ref[slot] * scale, 16) + first
            views.append(arrays[which].at[pl.ds(begin, count), pl.ds(columns[0], columns[1])])
        views[1][...] = views[0][...]


def moved(name, slots, sources, shapes, plan):
    outs = tuple(jax.ShapeDtypeStruct(shape, jnp.bfloat16) for shape in shapes)
    return pl.pallas_call(
        functools.partial(copy_kernel, plan),
        name=name,
        out_shape=outs,
        in_specs=[SMEM] + [VMEM] * len(sources),
        out_specs=(VMEM,) * len(outs),
        compiler_params=pltpu.CompilerParams(vmem_limit_bytes=40 * 2**20),
    )(slots, *sources)


DEPTH = 4
CHIPS = 16


def relative_slots():
    n_blk = lax.axis_size("blk")
    chip = lax.axis_index("head") * (n_blk // 2) + lax.axis_index("blk") // 2
    turns = [4 * z + 2 * y + x for y, x in ((0, 0), (0, 1), (1, 0), (1, 1)) for z in range(DEPTH)]
    return chip ^ jnp.asarray(turns, jnp.int32)


def piece_rows(rows):
    for k in range(CHIPS):
        group, z = k // DEPTH, k % DEPTH
        if group < 3:
            yield k, group, z * rows
        else:
            yield k, 3 + z // 2, z % 2 * rows


def spread_out(name, slots, payload, parts):
    layout, shapes = parts
    rows, width = payload.shape
    own = jnp.concatenate([payload] + [across_z(payload, k) for k in range(1, DEPTH)], axis=0)
    by_x, by_y = across_x(own), across_y(own)
    half = DEPTH // 2 * rows
    low, high = across_y(by_x[:half]), across_x(by_y[half:])
    plan = []
    for k, piece, at in piece_rows(rows):
        for first, count, whole, take, put in layout:
            plan.append(
                (piece, (None, 0, at + first, take), 5 + whole, (k, count if put[2] is None else put[2], put[1], put[0]), count)
            )
    return moved(name, slots, (own, by_x, by_y, low, high), shapes, tuple(plan))


def drawn_in(name, slots, wholes, layout, rows, width):
    plan = []
    for k, piece, at in piece_rows(rows):
        for first, count, whole, take, put in layout:
            plan.append(
                (whole, (k, count if put[2] is None else put[2], put[1], put[0]), len(wholes) + piece, (None, 0, at + first, take), count)
            )
    full, half = DEPTH * rows, DEPTH // 2 * rows
    shapes = ((full, width),) * 3 + ((half, width),) * 2
    own, by_x, by_y, low, high = moved(name, slots, wholes, shapes, tuple(plan))
    low, high = across_y(low), across_x(high)
    wide = lambda block: block.astype(jnp.float32)
    by_x = jnp.concatenate([(wide(by_x[:half]) + wide(low)).astype(jnp.bfloat16), by_x[half:]], axis=0)
    by_y = jnp.concatenate([by_y[:half], (wide(by_y[half:]) + wide(high)).astype(jnp.bfloat16)], axis=0)
    by_x, by_y = across_x(by_x), across_y(by_y)
    column = wide(own) + wide(by_x) + wide(by_y)
    total = column[:rows]
    for k in range(1, DEPTH):
        total = total + wide(across_z(column[k * rows : (k + 1) * rows].astype(jnp.bfloat16), k))
    return total


def document_bounds(segments):
    seq_count, blocks, span_len = segments.shape
    length = blocks * span_len
    numbers = lax.iota(jnp.int32, length // min(512, length) + 2)
    flat = segments.reshape(seq_count, length)
    below = jnp.sum((flat[:, :, None] < numbers).astype(jnp.int32), axis=1)
    here = flat[:, :, None] == numbers[:-1]
    starts = jnp.sum(jnp.where(here, below[:, None, :-1], 0), axis=2)
    ends = jnp.sum(jnp.where(here, below[:, None, 1:], 0), axis=2)
    return starts.reshape(segments.shape), ends.reshape(segments.shape)


def query_bounds(bounds, place, tile):
    near = [lax.dynamic_index_in_dim(bounds, place ^ k, 1, keepdims=False) for k in range(2)]
    near = jnp.stack(near, axis=0)
    return near.reshape(near.shape[0], near.shape[1], -1, tile)


def gelu_both(values):
    slope = float(np.sqrt(2.0 / np.pi))
    square = values * values
    curve = jnp.tanh(slope * values * (1.0 + 0.044715 * square))
    half = 0.5 * (1.0 + curve)
    rise = half + 0.5 * values * (1.0 - curve * curve) * (slope * (1.0 + 3 * 0.044715 * square))
    return values * half, rise


def joined(block):
    return jnp.concatenate([block, mate(block)], axis=0)


def halves_added(block):
    half = block.shape[0] // 2
    return block[:half] + mate(block[half:])


def norm_back(grad, rows, scale, gain):
    weighted = grad * gain
    inner = jnp.mean(rows * weighted, axis=-1, keepdims=True)
    return scale * weighted - rows * (scale * scale * scale) * inner, jnp.sum(grad * rows * scale, axis=0)


def dot_on(left, right, left_dim, right_dim):
    return lax.dot_general(left, right, (((left_dim,), (right_dim,)), ((), ())), preferred_element_type=jnp.float32)


def pair_body(
    inputs,
    segments,
    bucket_table,
    norm_gain,
    w_query,
    w_key,
    w_value,
    w_out,
    rel_bias,
    ff_gain,
    w_in,
    w_down,
    cotangent,
):
    low = jnp.bfloat16
    seq_count, _, part_len, width = inputs.shape
    groups = lax.axis_size("head")
    span_len = part_len * groups
    blocks = lax.axis_size("blk")
    group, place = lax.axis_index("head"), lax.axis_index("blk")
    core, side = place % 2, place // 2
    slots = relative_slots()
    shard = w_query.shape[0]
    chip_rows = 2 * shard
    half_width = groups * HD
    hidden = w_in.shape[1]
    half_hidden = hidden // 2
    down_rows = w_down.shape[0]

    def by_core(first, second):
        return jnp.where(core == 0, first, second)

    def head_columns(weight, which):
        return weight.reshape(shard, groups, 2, HD)[:, :, which]

    def cut(which):
        key_value = jnp.stack([head_columns(w_key, which), head_columns(w_value, which)], axis=2).reshape(shard, -1)
        query = head_columns(w_query, which).reshape(shard, -1)
        hidden_in = w_in.reshape(shard, -1, 2, down_rows)[:, :, which].reshape(shard, -1)
        return jnp.concatenate([key_value, query, hidden_in], axis=1)

    first_cut, second_cut = cut(0), cut(1)
    gains = jnp.concatenate([norm_gain, ff_gain, rel_bias, jnp.zeros((128 - 5 * shard // 2,), low)])
    gains = jnp.pad(gains[None, :], ((0, shard - 1), (0, 0)))
    kept = jnp.concatenate([by_core(first_cut, second_cut), gains], axis=1)
    given = mate(jnp.concatenate([by_core(second_cut, first_cut), gains], axis=1))
    chip_cut = jnp.concatenate([by_core(kept, given), by_core(given, kept)], axis=0)
    edge_kv, edge_q, edge_in = 2 * half_width, 3 * half_width, 3 * half_width + half_hidden
    gain_rows = jnp.stack([chip_cut[0, edge_in:], chip_cut[shard, edge_in:]], axis=0)
    gain_rows = jnp.pad(gain_rows, ((0, 14), (0, width - 128)))
    payload_kv = jnp.concatenate([chip_cut[:, :edge_kv], gain_rows], axis=0)
    cut_q = chip_cut[:, edge_kv:edge_q]
    payload_q = jnp.concatenate([cut_q[:shard], cut_q[shard:]], axis=1)
    cut_in = chip_cut[:, edge_q:edge_in]
    swap = [(b, (b % 2) * 2 + b // 2) for b in range(blocks)]
    payload_in = jnp.concatenate([cut_in[:, :width], cut_in[:, width:], lax.ppermute(w_out, "blk", swap)], axis=0)

    every = (0, width)
    lay_kv = ((0, chip_rows, 0, every, (every, 0, None)), (chip_rows, 16, 1, (0, 128), ((0, 128), 0, None)))
    lay_q = (
        (0, shard, 0, (0, half_width), ((0, half_width), 0, chip_rows)),
        (0, shard, 0, (half_width, half_width), ((0, half_width), shard, chip_rows)),
    )
    lay_in = (
        (0, chip_rows, 0, every, ((0, width), 0, None)),
        (chip_rows, chip_rows, 0, every, ((width, width), 0, None)),
        (2 * chip_rows, shard, 1, every, (every, 0, None)),
    )
    lay_down = ((0, down_rows, 0, every, (every, 0, None)),)
    kv_w, gain_w = spread_out("whole_kv", slots, payload_kv, (lay_kv, ((width, width), (16 * CHIPS, 128))))
    (query_w,) = spread_out("whole_q", slots, payload_q, (lay_q, ((width, half_width),)))
    in_w, out_w = spread_out("whole_in", slots, payload_in, (lay_in, ((width, half_hidden), (half_width, width))))
    (down_w,) = spread_out("whole_down", slots, w_down, (lay_down, ((half_hidden, width),)))

    gain_w = gain_w.reshape(CHIPS, 16, 128)[:, :2].astype(jnp.float32)
    gain_one = gain_w[:, :, :shard].reshape(-1)
    gain_two = gain_w[:, :, shard : 2 * shard].reshape(-1)
    rel_table = gain_w[:, :, 2 * shard : 5 * shard // 2].reshape(HEADS, BUCKETS)
    rel_here = lax.dynamic_index_in_dim(rel_table, 2 * group + core, 0, keepdims=False)

    bucket_hot = bucket_table[:, None] == lax.iota(jnp.int32, BUCKETS)[None, :]
    by_offset = jnp.sum(jnp.where(bucket_hot, rel_here[None, :], 0.0), axis=1)
    places = strip_places()
    place_hot = jnp.asarray(places.reshape(-1))[:, None] == lax.iota(jnp.int32, 2 * MAXREL + 1)[None, :]
    place_hot = place_hot.astype(jnp.float32)
    waves = jnp.dot(place_hot, by_offset, precision=lax.Precision.HIGHEST)
    waves = waves.reshape(places.shape[0], 1, places.shape[1])
    far_bias = jnp.stack([by_offset[0], by_offset[-1]])
    bias = bias_strip(far_bias, waves)
    starts, ends = document_bounds(segments)
    starts, ends = query_bounds(starts, place, TQ), query_bounds(ends, place, TQ)
    edges = jnp.stack([starts[..., 0], starts[..., -1], ends[..., 0], ends[..., -1]], axis=-1).reshape(-1)
    base = (place ^ lax.iota(jnp.int32, blocks)) * span_len

    token_rows = inputs.reshape(-1, width).astype(jnp.float32)
    scale_one = lax.rsqrt(jnp.mean(token_rows * token_rows, axis=-1, keepdims=True) + EPS)
    first_in = joined((token_rows * scale_one * gain_one).astype(low))
    tokens = first_in.shape[0]

    def exchanged(block):
        return lax.all_to_all(block, "head", split_axis=0, concat_axis=0, tiled=True)

    key_value = exchanged(dot_on(kv_w, first_in, 0, 1).astype(low).reshape(groups, 2 * HD, tokens))
    queries = exchanged(dot_on(query_w, first_in, 0, 1).astype(low).reshape(groups, HD, tokens))
    kvs = [key_value, across_x(key_value)]
    attended, attended_low, lse = attend(base, edges, far_bias, queries, kvs, starts, ends, bias)
    attn_cols = exchanged(attended_low).reshape(half_width, tokens)

    hidden_one = token_rows + halves_added(dot_on(attn_cols, out_w, 0, 0))
    scale_two = lax.rsqrt(jnp.mean(hidden_one * hidden_one, axis=-1, keepdims=True) + EPS)
    second_in = joined((hidden_one * scale_two * gain_two).astype(low))
    activated, rise = gelu_both(dot_on(second_in, in_w, 1, 0))
    activated = activated.astype(low)
    layer_out = (hidden_one + halves_added(dot_on(activated, down_w, 1, 0))).astype(low).reshape(inputs.shape)

    incoming_low = cotangent.reshape(-1, width)
    incoming = joined(incoming_low)
    up_grad = (dot_on(incoming, down_w, 1, 1) * rise).astype(low)
    second_grad = halves_added(dot_on(up_grad, in_w, 1, 1))
    hidden_part, grad_gain_two = norm_back(second_grad, hidden_one, scale_two, gain_two)
    hidden_grad = incoming_low.astype(jnp.float32) + hidden_part
    branch = joined(hidden_grad.astype(low))
    grad_cols = dot_on(out_w, branch, 1, 1).astype(low).reshape(groups, HD, tokens)
    grad_heads = exchanged(grad_cols)

    whole_down = dot_on(activated, incoming, 0, 0).astype(low)
    grad_down = drawn_in("parts_down", slots, (whole_down,), lay_down, down_rows, width)
    whole_in = dot_on(second_in, up_grad, 0, 0).astype(low)
    whole_out = dot_on(attn_cols, branch, 1, 0).astype(low)
    in_sum = drawn_in("parts_in", slots, (whole_in, whole_out), lay_in, 2 * chip_rows + shard, width)

    query_grad, kv_grads, band, sides = attend_back(
        base, edges, far_bias, queries, grad_heads, attended, lse, kvs, starts, ends, bias
    )
    kv_grad = (kv_grads[0].astype(jnp.float32) + across_x(kv_grads[1]).astype(jnp.float32)).astype(low)
    kv_cols = exchanged(kv_grad).reshape(2 * half_width, tokens)
    query_cols = exchanged(query_grad).reshape(half_width, tokens)
    first_grad = halves_added(dot_on(kv_cols, kv_w, 0, 1) + dot_on(query_cols, query_w, 0, 1))
    input_part, grad_gain_one = norm_back(first_grad, token_rows, scale_one, gain_one)
    input_grad = (hidden_grad + input_part).astype(low).reshape(inputs.shape)

    whole_kv = dot_on(first_in, kv_cols, 0, 1).astype(low)
    kv_sum = drawn_in("parts_kv", slots, (whole_kv,), lay_kv[:1], chip_rows, width)
    whole_q = dot_on(first_in, query_cols, 0, 1).astype(low)
    gain_grads = jnp.stack([grad_gain_one.reshape(CHIPS, -1), grad_gain_two.reshape(CHIPS, -1)], axis=1)
    gain_grads = jnp.pad(gain_grads.astype(low), ((0, 0), (0, 14), (0, 128 - chip_rows))).reshape(-1, 128)
    lay_last = lay_q + ((shard, 16, 1, (0, 128), ((0, 128), 0, None)),)
    q_sum = drawn_in("parts_q", slots, (whole_q, gain_grads), lay_last, shard + 16, width)

    def rows_of(block, which):
        return block[which * shard : (which + 1) * shard]

    q_rows = jnp.concatenate([q_sum[:shard, :half_width], q_sum[:shard, half_width:]], axis=0)
    in_rows = jnp.concatenate([in_sum[:chip_rows], in_sum[chip_rows : 2 * chip_rows]], axis=1)
    gain_sum = jnp.pad(q_sum[shard : shard + 2, :128], ((0, shard - 2), (0, 0)))

    def traded(block):
        mine = by_core(rows_of(block, 0), rows_of(block, 1))
        other = mate(by_core(rows_of(block, 1), rows_of(block, 0)))
        return by_core(mine, other), by_core(other, mine)

    kv_pair = jnp.stack(traded(kv_sum), axis=0).reshape(2, shard, groups, 2, HD)
    q_pair = jnp.stack(traded(q_rows), axis=0).reshape(2, shard, groups, HD)
    in_pair = jnp.stack(traded(in_rows), axis=0).reshape(2, shard, -1, down_rows)
    grad_query = q_pair.transpose(1, 2, 0, 3).reshape(shard, -1)
    grad_key = kv_pair[:, :, :, 0].transpose(1, 2, 0, 3).reshape(shard, -1)
    grad_value = kv_pair[:, :, :, 1].transpose(1, 2, 0, 3).reshape(shard, -1)
    grad_in = in_pair.transpose(1, 2, 0, 3).reshape(shard, -1)
    back_swap = [(b, (b % 2) * 2 + b // 2) for b in range(blocks)]
    grad_out = lax.ppermute(in_sum[2 * chip_rows :], "blk", back_swap)
    gain_sum = gain_sum + mate(gain_sum)
    gain_mine = by_core(gain_sum[:2, :shard], gain_sum[:2, shard : 2 * shard])

    near_sums, far_sums = band_sums_of(band, sides)
    offset_sums = jnp.dot(near_sums.reshape(-1), place_hot, precision=lax.Precision.HIGHEST)
    far_sums = jnp.sum(far_sums, axis=1)
    end_hot = lax.iota(jnp.int32, 2 * MAXREL + 1)
    offset_sums = offset_sums + jnp.where(end_hot == 0, far_sums[0], 0.0) + jnp.where(end_hot == 2 * MAXREL, far_sums[1], 0.0)
    rel_grad = jnp.sum(jnp.where(bucket_hot, offset_sums[:, None], 0.0), axis=0)
    rel_grad = jnp.pad(rel_grad[None, :], ((0, 7), (0, 128 - BUCKETS)))
    from_mate, from_x, from_corner = mate(rel_grad), across_x(rel_grad), trade(rel_grad, "blk", 3)
    rel_sum = jnp.where(core == side, rel_grad + from_x, from_mate + from_corner)[0]
    rel_mine = by_core(rel_sum[: BUCKETS // 2], rel_sum[BUCKETS // 2 : BUCKETS])

    return (
        layer_out,
        input_grad,
        gain_mine[0],
        grad_query,
        grad_key,
        grad_value,
        grad_out,
        rel_mine,
        gain_mine[1],
        grad_in,
        grad_down,
    )


def solution(mesh):
    placed = (
        P(None, "blk", "head", None),
        P(),
        P(),
        P(("head", "blk")),
        P(("head", "blk"), None),
        P(("head", "blk"), None),
        P(("head", "blk"), None),
        P(("head", "blk"), None),
        P(("head", "blk")),
        P(("head", "blk")),
        P(("head", "blk"), None),
        P(("head", "blk"), None),
        P(None, "blk", "head", None),
    )
    n_head, n_blk = mesh.shape["head"], mesh.shape["blk"]
    paired = HEADS == 2 * n_head and (n_head, n_blk) == (8, 4)
    return jax.shard_map(
        pair_body if paired else ring_body,
        mesh=mesh,
        in_specs=placed,
        out_specs=(
            P(None, "blk", "head", None),
            P(None, "blk", "head", None),
            P(("head", "blk")),
            P(("head", "blk"), None),
            P(("head", "blk"), None),
            P(("head", "blk"), None),
            P(("head", "blk"), None),
            P(("head", "blk")),
            P(("head", "blk")),
            P(("head", "blk"), None),
            P(("head", "blk"), None),
        ),
        check_vma=False,
    )
```

```python
import functools

import jax
import jax.numpy as jnp
import numpy as np
from jax import lax
from jax.experimental import pallas as pl
from jax.experimental.pallas import tpu as pltpu
from jax.sharding import PartitionSpec as P

HEADS = 16
HD = 64
BUCKETS = 32
MAXREL = 128
EPS = 1e-06
FLOOR = -1e30


def from_behind(block, axis, distance):
    devices = range(lax.axis_size(axis))
    route = [((i - distance) % len(devices), i) for i in devices]
    return lax.ppermute(block, axis, route)


def rms_scale(token_rows, gain_vector):
    return (
        token_rows
        * lax.rsqrt(jnp.mean(token_rows * token_rows, axis=-1, keepdims=True) + EPS)
        * gain_vector
    )


def smooth(values):
    return jax.nn.gelu(values, approximate=True)


def band_layout(span_len):
    tile_side = min(128, span_len)
    reach = MAXREL // tile_side + 2
    return (tile_side, span_len // tile_side, reach)


def band_tables(bucket_table, rel_here, span_len):
    tile_side, _, reach = band_layout(span_len)
    kinds = 2 * reach + 1
    gaps = lax.iota(jnp.int32, kinds) - reach
    rows_in = lax.iota(jnp.int32, tile_side)
    offsets = gaps[:, None, None] * tile_side + rows_in[None, None, :] - rows_in[None, :, None]
    lookup = jnp.clip(offsets, -MAXREL, MAXREL) + MAXREL
    bucket = jnp.take(bucket_table, lookup.reshape(-1), axis=0)
    onehot = (bucket[:, None] == lax.iota(jnp.int32, BUCKETS)[None, :]).astype(jnp.float32)
    band_bias = jnp.dot(rel_here, onehot.T, precision=lax.Precision.HIGHEST)
    return (band_bias.reshape(rel_here.shape[0], kinds, tile_side, tile_side), onehot)


def band_index(block_gap, span_len):
    _, tiles, reach = band_layout(span_len)
    row_tile = lax.iota(jnp.int32, tiles)[:, None, None, None]
    col_tile = lax.iota(jnp.int32, tiles)[None, None, :, None]
    return jnp.clip(block_gap * tiles + col_tile - row_tile, -reach, reach) + reach


def bias_tile(band_bias, block_gap, span_len):
    heads_count, kinds, tile_side, _ = band_bias.shape
    tiles = span_len // tile_side
    which = band_index(block_gap, span_len)
    result = jnp.zeros((heads_count, tiles, tile_side, tiles, tile_side), jnp.float32)
    for kind in range(kinds):
        result = jnp.where(which[None] == kind, band_bias[:, kind][:, None, :, None, :], result)
    return result.reshape(heads_count, span_len, span_len)


def band_sums(tile_sum, block_gap, span_len):
    tile_side, tiles, reach = band_layout(span_len)
    heads_count = tile_sum.shape[0]
    split_sum = tile_sum.reshape(heads_count, tiles, tile_side, tiles, tile_side)
    which = band_index(block_gap, span_len)
    parts = []
    for kind in range(2 * reach + 1):
        parts.append(jnp.sum(jnp.where(which[None] == kind, split_sum, 0.0), axis=(1, 3)))
    return jnp.stack(parts, axis=1).reshape(heads_count, -1)


def pass_grads(key_grad, value_grad):
    return (
        from_behind(key_grad.astype(jnp.bfloat16), "blk", 1).astype(key_grad.dtype),
        from_behind(value_grad.astype(jnp.bfloat16), "blk", 1).astype(value_grad.dtype),
    )


def ring_body(
    inputs,
    segments,
    bucket_table,
    norm_gain,
    w_query,
    w_key,
    w_value,
    w_out,
    rel_bias,
    ff_gain,
    w_in,
    w_down,
    cotangent,
):
    seq_count, _, part_len, width = inputs.shape
    cycle_size = lax.axis_size("blk")
    head_groups = lax.axis_size("head")
    heads_here = HEADS // head_groups
    span_len = part_len * head_groups
    cycle_place = lax.axis_index("blk")
    head_place = lax.axis_index("head")
    gathered = (
        lax.all_gather(norm_gain, ("head", "blk"), axis=0, tiled=True),
        lax.all_gather(w_query, ("head", "blk"), axis=0, tiled=True),
        lax.all_gather(w_key, ("head", "blk"), axis=0, tiled=True),
        lax.all_gather(w_value, ("head", "blk"), axis=0, tiled=True),
        lax.all_gather(w_out, ("head", "blk"), axis=0, tiled=True),
        lax.all_gather(rel_bias, ("head", "blk"), axis=0, tiled=True),
        lax.all_gather(ff_gain, ("head", "blk"), axis=0, tiled=True),
        lax.all_gather(w_in, ("head", "blk"), axis=0, tiled=True),
        lax.all_gather(w_down, ("head", "blk"), axis=0, tiled=True),
    )
    gain_one, query_w, key_w, value_w, out_w, rel_flat, gain_two, in_w, down_w = gathered
    token_rows = inputs.reshape(-1, width).astype(jnp.float32)
    normed, norm_one_back = jax.vjp(rms_scale, token_rows, gain_one.astype(jnp.float32))
    first_in = normed.astype(jnp.bfloat16)

    def project(weight):
        made_rows = jnp.dot(first_in, weight, preferred_element_type=jnp.float32)
        return made_rows.astype(jnp.bfloat16).reshape(seq_count, part_len, -1)

    queries, keys_home, values_home = (
        lax.all_to_all(project(query_w), "head", split_axis=2, concat_axis=1, tiled=True),
        lax.all_to_all(project(key_w), "head", split_axis=2, concat_axis=1, tiled=True),
        lax.all_to_all(project(value_w), "head", split_axis=2, concat_axis=1, tiled=True),
    )
    head_shape = (seq_count, span_len, heads_here, HD)
    queries = queries.reshape(head_shape)
    keys_home = keys_home.reshape(head_shape)
    values_home = values_home.reshape(head_shape)
    rel_table = rel_flat.astype(jnp.float32).reshape(HEADS, BUCKETS)
    rel_here = lax.dynamic_slice_in_dim(rel_table, head_place * heads_here, heads_here, 0)
    band_bias, band_onehot = band_tables(bucket_table, rel_here, span_len)

    def tile_scores(query_rows, key_rows, query_block, key_block):
        query_ids = lax.dynamic_index_in_dim(segments, query_block, 1, keepdims=False)
        key_ids = lax.dynamic_index_in_dim(segments, key_block, 1, keepdims=False)
        plain_scores = (
            jnp.einsum("sihd,sjhd->shij", query_rows, key_rows, preferred_element_type=jnp.float32)
            + bias_tile(band_bias, key_block - query_block, span_len)[None]
        )
        same_doc = query_ids[:, None, :, None] == key_ids[:, None, None, :]
        return jnp.where(same_doc, plain_scores, FLOOR)

    first_scores = tile_scores(queries, keys_home, cycle_place, cycle_place)
    row_max = jnp.max(first_scores, axis=-1)
    first_weights = jnp.exp(first_scores - row_max[..., None])
    row_total = jnp.sum(first_weights, axis=-1)
    summed = jnp.einsum(
        "shij,sjhd->sihd",
        first_weights.astype(jnp.bfloat16),
        values_home,
        preferred_element_type=jnp.float32,
    )

    def forward_turn(cycle_turn, state_now):
        old_max, old_total, old_summed, key_rows, value_rows = state_now
        key_rows, value_rows = from_behind((key_rows, value_rows), "blk", 1)
        source = (cycle_place - cycle_turn) % cycle_size
        scores = tile_scores(queries, key_rows, cycle_place, source)
        new_max = jnp.maximum(old_max, jnp.max(scores, axis=-1))
        shrink = jnp.exp(old_max - new_max)
        weights_now = jnp.exp(scores - new_max[..., None])
        new_total = old_total * shrink + jnp.sum(weights_now, axis=-1)
        new_summed = old_summed * jnp.transpose(shrink, (0, 2, 1))[..., None] + jnp.einsum(
            "shij,sjhd->sihd",
            weights_now.astype(jnp.bfloat16),
            value_rows,
            preferred_element_type=jnp.float32,
        )
        return (new_max, new_total, new_summed, key_rows, value_rows)

    row_max, row_total, summed, _, _ = lax.fori_loop(
        1, cycle_size, forward_turn, (row_max, row_total, summed, keys_home, values_home)
    )
    log_total = row_max + jnp.log(row_total)
    attended = summed / jnp.transpose(row_total, (0, 2, 1))[..., None]
    attended_low = attended.astype(jnp.bfloat16).reshape(seq_count, span_len, heads_here * HD)
    attn_rows = lax.all_to_all(
        attended_low, "head", split_axis=1, concat_axis=2, tiled=True
    ).reshape(-1, HEADS * HD)
    hidden_one = token_rows + jnp.dot(attn_rows, out_w, preferred_element_type=jnp.float32)
    normed_two, norm_two_back = jax.vjp(rms_scale, hidden_one, gain_two.astype(jnp.float32))
    second_in = normed_two.astype(jnp.bfloat16)
    upward = jnp.dot(second_in, in_w, preferred_element_type=jnp.float32)
    activated, smooth_back = jax.vjp(smooth, upward)
    activated_low = activated.astype(jnp.bfloat16)
    layer_rows = hidden_one + jnp.dot(activated_low, down_w, preferred_element_type=jnp.float32)
    layer_out = layer_rows.astype(jnp.bfloat16).reshape(inputs.shape)
    back_query, back_key, back_value, back_out, back_in, back_down = (
        query_w,
        key_w,
        value_w,
        out_w,
        in_w,
        down_w,
    )
    incoming_low = cotangent.reshape(-1, width)
    incoming = incoming_low.astype(jnp.float32)
    grad_down = jnp.dot(activated_low.T, incoming_low, preferred_element_type=jnp.float32)
    (up_grad,) = smooth_back(jnp.dot(incoming_low, back_down.T, preferred_element_type=jnp.float32))
    up_low = up_grad.astype(jnp.bfloat16)
    grad_in = jnp.dot(second_in.T, up_low, preferred_element_type=jnp.float32)
    hidden_part, grad_gain_two = norm_two_back(
        jnp.dot(up_low, back_in.T, preferred_element_type=jnp.float32)
    )
    hidden_grad = incoming + hidden_part
    branch_low = hidden_grad.astype(jnp.bfloat16)
    grad_out = jnp.dot(attn_rows.T, branch_low, preferred_element_type=jnp.float32)
    attn_grad_low = jnp.dot(branch_low, back_out.T, preferred_element_type=jnp.float32).astype(
        jnp.bfloat16
    )
    grad_heads = lax.all_to_all(
        attn_grad_low.reshape(seq_count, part_len, HEADS * HD),
        "head",
        split_axis=2,
        concat_axis=1,
        tiled=True,
    ).reshape(head_shape)
    row_delta = jnp.transpose(
        jnp.sum(grad_heads.astype(jnp.float32) * attended, axis=-1), (0, 2, 1)
    )

    def tile_grads(
        query_rows, grad_rows, log_rows, delta_rows, key_rows, value_rows, query_block, key_block
    ):
        scores = tile_scores(query_rows, key_rows, query_block, key_block)
        probs = jnp.exp(scores - log_rows[..., None])
        value_part = jnp.einsum(
            "shij,sihd->sjhd",
            probs.astype(jnp.bfloat16),
            grad_rows,
            preferred_element_type=jnp.float32,
        )
        prob_grad = jnp.einsum(
            "sihd,sjhd->shij", grad_rows, value_rows, preferred_element_type=jnp.float32
        )
        score_low = (probs * (prob_grad - delta_rows[..., None])).astype(jnp.bfloat16)
        query_part = jnp.einsum(
            "shij,sjhd->sihd", score_low, key_rows, preferred_element_type=jnp.float32
        )
        key_part = jnp.einsum(
            "shij,sihd->sjhd", score_low, query_rows, preferred_element_type=jnp.float32
        )
        tile_sum = jnp.sum(score_low.astype(jnp.float32), axis=0)
        rel_part = jnp.dot(
            band_sums(tile_sum, key_block - query_block, span_len),
            band_onehot,
            precision=lax.Precision.HIGHEST,
        )
        return (query_part, key_part, value_part, rel_part)

    query_grad, key_grad, value_grad, rel_grad = tile_grads(
        queries, grad_heads, log_total, row_delta, keys_home, values_home, cycle_place, cycle_place
    )

    def key_turn(cycle_turn, state_now):
        key_rows, value_rows, key_sum, value_sum, query_sum, rel_sum = state_now
        key_sum, value_sum = pass_grads(key_sum, value_sum)
        key_rows, value_rows = from_behind((key_rows, value_rows), "blk", 1)
        source = (cycle_place - cycle_turn) % cycle_size
        query_part, key_part, value_part, rel_part = tile_grads(
            queries, grad_heads, log_total, row_delta, key_rows, value_rows, cycle_place, source
        )
        return (
            key_rows,
            value_rows,
            key_sum + key_part,
            value_sum + value_part,
            query_sum + query_part,
            rel_sum + rel_part,
        )

    state_first = (keys_home, values_home, key_grad, value_grad, query_grad, rel_grad)
    _, _, key_grad, value_grad, query_grad, rel_grad = lax.fori_loop(
        1, cycle_size, key_turn, state_first
    )
    key_grad, value_grad = pass_grads(key_grad, value_grad)
    block_shape = (seq_count, span_len, heads_here * HD)
    query_rows, key_rows_back, value_rows_back = (
        lax.all_to_all(
            query_grad.astype(jnp.bfloat16).reshape(block_shape),
            "head",
            split_axis=1,
            concat_axis=2,
            tiled=True,
        ),
        lax.all_to_all(
            key_grad.astype(jnp.bfloat16).reshape(block_shape),
            "head",
            split_axis=1,
            concat_axis=2,
            tiled=True,
        ),
        lax.all_to_all(
            value_grad.astype(jnp.bfloat16).reshape(block_shape),
            "head",
            split_axis=1,
            concat_axis=2,
            tiled=True,
        ),
    )
    query_rows = query_rows.reshape(-1, HEADS * HD)
    key_rows_back = key_rows_back.reshape(-1, HEADS * HD)
    value_rows_back = value_rows_back.reshape(-1, HEADS * HD)
    grad_query = jnp.dot(first_in.T, query_rows, preferred_element_type=jnp.float32)
    grad_key = jnp.dot(first_in.T, key_rows_back, preferred_element_type=jnp.float32)
    grad_value = jnp.dot(first_in.T, value_rows_back, preferred_element_type=jnp.float32)
    first_grad = (
        jnp.dot(query_rows, back_query.T, preferred_element_type=jnp.float32)
        + jnp.dot(key_rows_back, back_key.T, preferred_element_type=jnp.float32)
        + jnp.dot(value_rows_back, back_value.T, preferred_element_type=jnp.float32)
    )
    input_part, grad_gain_one = norm_one_back(first_grad)
    input_grad = (hidden_grad + input_part).astype(jnp.bfloat16).reshape(inputs.shape)
    rel_full = lax.dynamic_update_slice_in_dim(
        jnp.zeros((HEADS, BUCKETS), jnp.float32), rel_grad, head_place * heads_here, 0
    ).reshape(-1)
    shards = tuple(
        (
            lax.psum_scatter(grad_gain_one, ("head", "blk"), scatter_dimension=0, tiled=True),
            lax.psum_scatter(grad_query, ("head", "blk"), scatter_dimension=0, tiled=True),
            lax.psum_scatter(grad_key, ("head", "blk"), scatter_dimension=0, tiled=True),
            lax.psum_scatter(grad_value, ("head", "blk"), scatter_dimension=0, tiled=True),
            lax.psum_scatter(grad_out, ("head", "blk"), scatter_dimension=0, tiled=True),
            lax.psum_scatter(rel_full, ("head", "blk"), scatter_dimension=0, tiled=True),
            lax.psum_scatter(grad_gain_two, ("head", "blk"), scatter_dimension=0, tiled=True),
            lax.psum_scatter(grad_in, ("head", "blk"), scatter_dimension=0, tiled=True),
            lax.psum_scatter(grad_down, ("head", "blk"), scatter_dimension=0, tiled=True),
        )
    )
    return (
        layer_out,
        input_grad,
        shards[0],
        shards[1],
        shards[2],
        shards[3],
        shards[4],
        shards[5],
        shards[6],
        shards[7],
        shards[8],
    )


TQ = 512
KT = 512
MARGIN = 256
AUG = 80
NT = (((1,), (1,)), ((), ()))


def nn(left, right):
    return jnp.dot(left, right, preferred_element_type=jnp.float32)


def flipped(block):
    return block.astype(jnp.float32).T.astype(jnp.bfloat16)


def ones_row(width):
    first = lax.broadcasted_iota(jnp.int32, (AUG - HD, width), 0) == 0
    return jnp.where(first, 1.0, 0.0).astype(jnp.bfloat16)


def pieces_of(seq_count, part_len, groups):
    for seq in range(seq_count):
        for near in range(2):
            for source in range(groups):
                yield seq, near, source, slice((near * seq_count + seq) * part_len, (near * seq_count + seq + 1) * part_len)


def lanes_of(ref, tile_at, per_tile, part_len, lane_base):
    parts = [ref[tile_at * per_tile + k, :HD, pl.ds(lane_base, part_len)] for k in range(per_tile)]
    return parts[0] if per_tile == 1 else jnp.concatenate(parts, axis=1)


def tile_class(edge_ref, row, key_at, query_at):
    first_start, last_start, first_end, last_end = (edge_ref[row * 4 + k] for k in range(4))
    touched = (key_at + KT > first_start) & (key_at < last_end)
    gap = key_at - query_at
    whole = (key_at >= last_start) & (key_at + KT <= first_end)
    plain = whole & ((gap + KT <= -MAXREL + 1) | (gap >= TQ + MAXREL - 1))
    strip_at = jnp.clip(gap, -(KT + MARGIN), TQ + MARGIN) + KT + MARGIN
    return touched, plain, gap, pl.ds(pl.multiple_of(strip_at, 256), KT)


def masked(scores, bias, key_at, start_row, end_row):
    places = lax.broadcasted_iota(jnp.int32, scores.shape, 0) + key_at
    return jnp.where((places >= start_row) & (places < end_row), scores + bias, FLOOR)


def attend_kernel(chips, base_ref, edge_ref, far_ref, *refs):
    kv_refs, q_ref = refs[:chips], refs[0]
    start_ref, end_ref, bias_ref, o_ref, ob_ref, lse_ref, k_rows, v_aug, top_ref, acc_ref = refs[chips:]
    groups, _, span = q_ref.shape
    blocks, seq_count, span_len, _ = k_rows.shape
    part_len = span_len // groups
    per_tile = TQ // part_len
    tiles, key_tiles = span_len // TQ, span_len // KT
    per_key = KT // part_len
    for far in range(chips):
        for seq, near, source, lanes in pieces_of(seq_count, part_len, groups):
            block = 2 * far + near
            k_rows[block, seq, source * part_len : (source + 1) * part_len, :] = flipped(kv_refs[far][source, HD : 2 * HD, lanes])
            at = source % per_key * part_len
            v_aug[block, seq, source // per_key, :HD, at : at + part_len] = kv_refs[far][source, 2 * HD :, lanes]
    for block in range(blocks):
        for seq in range(seq_count):
            for tile in range(key_tiles):
                v_aug[block, seq, tile, HD:, :] = ones_row(KT)

    for seq in range(seq_count):
        for near in range(2):
            lane_base = (near * seq_count + seq) * part_len

            def query_tile(tile, _, seq=seq, near=near, lane_base=lane_base):
                query_at = base_ref[near] + tile * TQ
                row = (near * seq_count + seq) * tiles + tile
                queries = lanes_of(q_ref, tile, per_tile, part_len, lane_base)
                top_ref[...] = jnp.full_like(top_ref, FLOOR)
                acc_ref[...] = jnp.zeros_like(acc_ref)
                start_row = start_ref[near, seq, pl.ds(tile, 1), :]
                end_row = end_ref[near, seq, pl.ds(tile, 1), :]

                def take(scores, shift, block, key_tile):
                    old_top = top_ref[0:1, :]
                    new_top = jnp.maximum(old_top, jnp.max(scores, axis=0, keepdims=True) + shift)
                    weights = jnp.exp(scores - (new_top - shift))
                    acc_ref[...] = acc_ref[...] * jnp.exp(old_top - new_top) + nn(
                        v_aug[block, seq, key_tile], weights.astype(jnp.bfloat16)
                    )
                    top_ref[0:1, :] = new_top

                def key_step(step, _):
                    block, key_tile = step // key_tiles, step % key_tiles
                    key_at = base_ref[block] + key_tile * KT
                    touched, plain, gap, strip = tile_class(edge_ref, row, key_at, query_at)

                    def raw():
                        keys = k_rows[block, seq, pl.ds(pl.multiple_of(key_tile * KT, KT), KT), :]
                        return nn(keys, queries)

                    @pl.when(touched & plain)
                    def _():
                        take(raw(), jnp.where(gap < 0, far_ref[0], far_ref[1]), block, key_tile)

                    @pl.when(touched & jnp.logical_not(plain))
                    def _():
                        take(masked(raw(), bias_ref[strip, :], key_at, start_row, end_row), 0.0, block, key_tile)

                    return 0

                lax.fori_loop(0, blocks * key_tiles, key_step, 0)
                total = acc_ref[HD : HD + 1, :]
                outs = acc_ref[:HD, :] / total
                lse_ref[near, seq, pl.ds(tile, 1), :] = top_ref[0:1, :] + jnp.log(total)
                for k in range(per_tile):
                    part = outs[:, k * part_len : (k + 1) * part_len]
                    o_ref[tile * per_tile + k, :, lane_base : lane_base + part_len] = part
                    ob_ref[tile * per_tile + k, :, lane_base : lane_base + part_len] = part.astype(jnp.bfloat16)
                return 0

            lax.fori_loop(0, tiles, query_tile, 0)


def attend_back_kernel(chips, carried, base_ref, edge_ref, far_ref, g_ref, o_ref, lse_ref, *refs):
    kv_refs, q_ref, refs = refs[:chips], refs[0], refs[chips:]
    start_ref, end_ref, bias_ref, *refs = refs
    if carried:
        old_band_ref, old_sides_ref, *refs = refs
    made_refs, refs = refs[:chips], refs[chips:]
    dq_ref = made_refs[0]
    band_ref, sides_ref, k_rows, v_rows, k_aug, dk_acc, dv_acc, dq_acc = refs
    groups, _, span = q_ref.shape
    blocks, seq_count, span_len, _ = k_rows.shape
    part_len = span_len // groups
    per_tile = TQ // part_len
    tiles, key_tiles = span_len // TQ, span_len // KT
    per_key = KT // part_len
    for far in range(chips):
        for seq, near, source, lanes in pieces_of(seq_count, part_len, groups):
            block = 2 * far + near
            rows = slice(source * part_len, (source + 1) * part_len)
            piece = kv_refs[far][source, HD : 2 * HD, lanes]
            k_rows[block, seq, rows, :] = flipped(piece)
            v_rows[block, seq, rows, :] = flipped(kv_refs[far][source, 2 * HD :, lanes])
            at = source % per_key * part_len
            k_aug[block, seq, source // per_key, :HD, at : at + part_len] = piece
    for block in range(blocks):
        for seq in range(seq_count):
            for tile in range(key_tiles):
                k_aug[block, seq, tile, HD:, :] = ones_row(KT)
    dk_acc[...] = jnp.zeros_like(dk_acc)
    dv_acc[...] = jnp.zeros_like(dv_acc)
    band_ref[...] = old_band_ref[...] if carried else jnp.zeros_like(band_ref)
    sides_ref[...] = old_sides_ref[...] if carried else jnp.zeros_like(sides_ref)

    for seq in range(seq_count):
        for near in range(2):
            lane_base = (near * seq_count + seq) * part_len

            def query_tile(tile, _, seq=seq, near=near, lane_base=lane_base):
                query_at = base_ref[near] + tile * TQ
                row = (near * seq_count + seq) * tiles + tile
                queries = lanes_of(q_ref, tile, per_tile, part_len, lane_base)
                grads = lanes_of(g_ref, tile, per_tile, part_len, lane_base)
                outs = lanes_of(o_ref, tile, per_tile, part_len, lane_base)
                delta = jnp.sum(grads.astype(jnp.float32) * outs, axis=0, keepdims=True)
                query_rows, grad_rows = flipped(queries), flipped(grads)
                lse = lse_ref[near, seq, pl.ds(tile, 1), :]
                start_row = start_ref[near, seq, pl.ds(tile, 1), :]
                end_row = end_ref[near, seq, pl.ds(tile, 1), :]
                dq_acc[...] = jnp.zeros_like(dq_acc)

                def take(scores, shift, block, key_tile):
                    rows = pl.ds(pl.multiple_of(key_tile * KT, KT), KT)
                    probs = jnp.exp(scores - (lse - shift))
                    score_grad = probs * (nn(v_rows[block, seq, rows, :], grads) - delta)
                    score_low = score_grad.astype(jnp.bfloat16)
                    dv_acc[block, seq, rows, :] += nn(probs.astype(jnp.bfloat16), grad_rows)
                    dk_acc[block, seq, rows, :] += nn(score_low, query_rows)
                    made = nn(k_aug[block, seq, key_tile], score_low)
                    dq_acc[...] += made
                    return score_grad, made[HD : HD + 1, :]

                def key_step(step, _):
                    block, key_tile = step // key_tiles, step % key_tiles
                    key_at = base_ref[block] + key_tile * KT
                    touched, plain, gap, strip = tile_class(edge_ref, row, key_at, query_at)

                    def raw():
                        keys = k_rows[block, seq, pl.ds(pl.multiple_of(key_tile * KT, KT), KT), :]
                        return nn(keys, queries)

                    @pl.when(touched & plain)
                    def _():
                        _, sums = take(raw(), jnp.where(gap < 0, far_ref[0], far_ref[1]), block, key_tile)
                        side = (gap > 0).astype(jnp.int32)
                        sides_ref[pl.ds(side, 1), :] += sums

                    @pl.when(touched & jnp.logical_not(plain))
                    def _():
                        whole_grad, _ = take(
                            masked(raw(), bias_ref[strip, :], key_at, start_row, end_row), 0.0, block, key_tile
                        )
                        band_ref[strip, :] += whole_grad

                    return 0

                lax.fori_loop(0, blocks * key_tiles, key_step, 0)
                for k in range(per_tile):
                    part = dq_acc[:HD, k * part_len : (k + 1) * part_len].astype(jnp.bfloat16)
                    dq_ref[tile * per_tile + k, :HD, lane_base : lane_base + part_len] = part
                return 0

            lax.fori_loop(0, tiles, query_tile, 0)
    for far in range(chips):
        for seq, near, source, lanes in pieces_of(seq_count, part_len, groups):
            block = 2 * far + near
            rows = slice(source * part_len, (source + 1) * part_len)
            top = 0 if far else HD
            made_refs[far][source, top : top + HD, lanes] = dk_acc[block, seq, rows, :].T.astype(jnp.bfloat16)
            made_refs[far][source, top + HD : top + 2 * HD, lanes] = dv_acc[block, seq, rows, :].T.astype(jnp.bfloat16)


def strip_places():
    width = TQ + 128
    lane = np.arange(width)
    lane = np.where(lane < TQ, lane, lane - width)
    offset = 128 * (np.arange(TQ // 128 + 2)[:, None] - 1) - lane[None, :]
    return np.clip(offset, -MAXREL, MAXREL) + MAXREL


def strip_kernel(far_ref, wave_ref, strip_ref):
    near_blocks, _, width = wave_ref.shape
    first = KT + MARGIN - 128
    strip_ref[:first, :] = jnp.full((first, TQ), far_ref[0], jnp.float32)
    for k in range(near_blocks):
        spread = jnp.broadcast_to(wave_ref[k], (128, width))
        turned = pltpu.roll(spread, 0, 1, stride=1, stride_axis=0)
        strip_ref[first + 128 * k : first + 128 * (k + 1), :] = turned[:, :TQ]
    last = first + 128 * near_blocks
    strip_ref[last:, :] = jnp.full((strip_ref.shape[0] - last, TQ), far_ref[1], jnp.float32)


def bias_strip(far_bias, waves):
    return pl.pallas_call(
        strip_kernel,
        name="bias_strip",
        out_shape=jax.ShapeDtypeStruct((2 * KT + 2 * MARGIN + TQ, TQ), jnp.float32),
        in_specs=[SMEM, VMEM],
        out_specs=VMEM,
        compiler_params=pltpu.CompilerParams(vmem_limit_bytes=32 * 2**20),
    )(far_bias, waves)


def band_kernel(band_ref, sides_ref, near_ref, far_ref):
    near_blocks, _, width = near_ref.shape
    first = KT + MARGIN - 128
    last = first + 128 * near_blocks
    left = jnp.sum(band_ref[:first, :], axis=0, keepdims=True) + sides_ref[0:1, :]
    right = jnp.sum(band_ref[last:, :], axis=0, keepdims=True) + sides_ref[1:2, :]
    far_ref[...] = jnp.concatenate([left, right, jnp.zeros((6, TQ), jnp.float32)], axis=0)
    for k in range(near_blocks):
        rows = band_ref[first + 128 * k : first + 128 * (k + 1), :]
        spread = jnp.concatenate([rows, jnp.zeros((128, width - TQ), jnp.float32)], axis=1)
        row = lax.broadcasted_iota(jnp.int32, spread.shape, 0)
        for step in (1, 2, 4):
            spread = jnp.where((row & step) != 0, pltpu.roll(spread, width - step, 1), spread)
        total = spread[:8, :]
        for at in range(8, 128, 8):
            total = total + pltpu.roll(spread[at : at + 8, :], width - at, 1)
        near_ref[k] = jnp.sum(total, axis=0, keepdims=True)


def band_sums_of(band, sides):
    return pl.pallas_call(
        band_kernel,
        name="band_sums",
        out_shape=(
            jax.ShapeDtypeStruct((TQ // 128 + 2, 1, TQ + 128), jnp.float32),
            jax.ShapeDtypeStruct((8, TQ), jnp.float32),
        ),
        in_specs=[VMEM, VMEM],
        out_specs=(VMEM, VMEM),
        compiler_params=pltpu.CompilerParams(vmem_limit_bytes=32 * 2**20),
    )(band, sides)


SMEM = pl.BlockSpec(memory_space=pltpu.SMEM)
VMEM = pl.BlockSpec(memory_space=pltpu.VMEM)


def attend(base, edges, far_bias, kvs, starts, ends, bias):
    chips = len(kvs)
    groups, _, span = kvs[0].shape
    shape = (groups, HD, span)
    _, seq_count, tiles, _ = starts.shape
    blocks, span_len = 2 * chips, tiles * TQ
    return pl.pallas_call(
        functools.partial(attend_kernel, chips),
        name="attend",
        out_shape=(
            jax.ShapeDtypeStruct(shape, jnp.float32),
            jax.ShapeDtypeStruct(shape, jnp.bfloat16),
            jax.ShapeDtypeStruct(starts.shape, jnp.float32),
        ),
        in_specs=[SMEM] * 3 + [VMEM] * (chips + 3),
        out_specs=(VMEM,) * 3,
        scratch_shapes=[
            pltpu.VMEM((blocks, seq_count, span_len, HD), jnp.bfloat16),
            pltpu.VMEM((blocks, seq_count, span_len // KT, AUG, KT), jnp.bfloat16),
            pltpu.VMEM((8, TQ), jnp.float32),
            pltpu.VMEM((AUG, TQ), jnp.float32),
        ],
        cost_estimate=pl.CostEstimate(flops=1, transcendentals=0, bytes_accessed=1),
        compiler_params=pltpu.CompilerParams(vmem_limit_bytes=48 * 2**20),
    )(base, edges, far_bias, *kvs, starts, ends, bias)


def attend_back(base, edges, far_bias, g, o, lse, kvs, starts, ends, bias, sums=()):
    chips = len(kvs)
    groups, _, span = g.shape
    _, seq_count, tiles, _ = starts.shape
    blocks, span_len = 2 * chips, tiles * TQ
    made = pl.pallas_call(
        functools.partial(attend_back_kernel, chips, bool(sums)),
        name="attend_back",
        out_shape=(jax.ShapeDtypeStruct(kvs[0].shape, jnp.bfloat16),)
        + (jax.ShapeDtypeStruct((groups, 2 * HD, span), jnp.bfloat16),) * (chips - 1)
        + (jax.ShapeDtypeStruct(bias.shape, jnp.float32), jax.ShapeDtypeStruct((8, TQ), jnp.float32)),
        in_specs=[SMEM] * 3 + [VMEM] * (3 + chips + 3 + len(sums)),
        out_specs=(VMEM,) * (2 + chips),
        scratch_shapes=[
            pltpu.VMEM((blocks, seq_count, span_len, HD), jnp.bfloat16),
            pltpu.VMEM((blocks, seq_count, span_len, HD), jnp.bfloat16),
            pltpu.VMEM((blocks, seq_count, span_len // KT, AUG, KT), jnp.bfloat16),
            pltpu.VMEM((blocks, seq_count, span_len, HD), jnp.float32),
            pltpu.VMEM((blocks, seq_count, span_len, HD), jnp.float32),
            pltpu.VMEM((AUG, TQ), jnp.float32),
        ],
        cost_estimate=pl.CostEstimate(flops=1, transcendentals=0, bytes_accessed=1),
        compiler_params=pltpu.CompilerParams(vmem_limit_bytes=56 * 2**20),
    )(base, edges, far_bias, g, o, lse, *kvs, starts, ends, bias, *sums)
    return made[0], made[1:chips], made[-2:]


def trade(block, axis, bit):
    size = lax.axis_size(axis)
    return lax.ppermute(block, axis, [(i, i ^ bit) for i in range(size)])


def mate(block):
    return trade(block, "blk", 1)


def across_x(block):
    return trade(block, "blk", 2)


def across_y(block):
    return trade(block, "head", 1)


def across_z(block, distance):
    return trade(block, "head", 2 * distance)


def copy_kernel(plan, slots_ref, *arrays):
    for source, source_rows, target, target_rows, count in plan:
        views = []
        for which, (slot, scale, first, columns) in ((source, source_rows), (target, target_rows)):
            begin = first if slot is None else pl.multiple_of(slots_ref[slot] * scale, 8) + first
            views.append(arrays[which].at[pl.ds(begin, count), pl.ds(columns[0], columns[1])])
        views[1][...] = views[0][...]


def moved(name, slots, sources, shapes, plan):
    outs = tuple(jax.ShapeDtypeStruct(shape, sources[0].dtype) for shape in shapes)
    return pl.pallas_call(
        functools.partial(copy_kernel, plan),
        name=name,
        out_shape=outs,
        in_specs=[SMEM] + [VMEM] * len(sources),
        out_specs=(VMEM,) * len(outs),
        compiler_params=pltpu.CompilerParams(vmem_limit_bytes=40 * 2**20),
    )(slots, *sources)


DEPTH = 4
CHIPS = 16


def turn_of(k):
    return k % DEPTH, k // DEPTH // 2, k // DEPTH % 2


def slot_table():
    n_blk = lax.axis_size("blk")
    group, place = lax.axis_index("head"), lax.axis_index("blk")
    groups = group ^ jnp.asarray([2 * turn_of(k)[0] + turn_of(k)[1] for k in range(CHIPS)], jnp.int32)
    sides = (place // 2) ^ jnp.asarray([turn_of(k)[2] for k in range(CHIPS)], jnp.int32)
    chips = groups * (n_blk // 2) + sides
    return jnp.concatenate([chips, groups, 2 * chips + place % 2, 2 * chips + 1 - place % 2])


CHIP, GROUP, DEVICE, MATE = 0, CHIPS, 2 * CHIPS, 3 * CHIPS


def after(block, *earlier):
    return lax.optimization_barrier((block, earlier))[0]


def beside(made, *sent):
    return lax.optimization_barrier((made, *sent))


def wide(block):
    return block.astype(jnp.float32)


def placed(name, slots, blocks, layout, shapes, order):
    plan = []
    for k, (which, at) in enumerate(order):
        for first, count, whole, take, target in layout:
            plan.append((which, (None, 0, at + first, take), len(blocks) + whole, target(k), count))
    return moved(name, slots, blocks, shapes, tuple(plan))


def parted(name, slots, wholes, layout, shapes, order):
    plan = []
    for k, (which, at) in enumerate(order):
        for first, count, whole, take, target in layout:
            plan.append((whole, target(k), len(wholes) + which, (None, 0, at + first, take), count))
    return moved(name, slots, wholes, shapes, tuple(plan))


def grouped(rows):
    order = []
    for k in range(CHIPS):
        group, z = k // DEPTH, k % DEPTH
        order.append((group, z * rows) if group < 3 else (3 + z // 2, z % 2 * rows))
    return order


def gather_z(payload, *earlier):
    payload = after(payload, *earlier) if earlier else payload
    return [payload] + [across_z(payload, k) for k in range(1, DEPTH)]


def gather_xy(own, *earlier):
    own = jnp.concatenate(own, axis=0)
    own = after(own, *earlier) if earlier else own
    return own, across_x(own), across_y(own)


def gather_corner(blocks, *earlier):
    own, by_x, by_y = blocks
    half = own.shape[0] // 2
    low, high = by_x[:half], by_y[half:]
    if earlier:
        low, high = after(low, *earlier), after(high, *earlier)
    return own, by_x, by_y, across_y(low), across_x(high)


def sum_corner(name, slots, wholes, layout, rows, width):
    full, half = DEPTH * rows, DEPTH // 2 * rows
    shapes = ((full, width),) * 3 + ((half, width),) * 2
    own, by_x, by_y, low, high = parted(name, slots, wholes, layout, shapes, grouped(rows))
    return own, by_x, by_y, across_y(low), across_x(high)


def sum_xy(blocks, *earlier):
    own, by_x, by_y, low, high = blocks
    half = low.shape[0]
    if earlier:
        low, high = after(low, *earlier), after(high, *earlier)
    by_x = jnp.concatenate([(wide(by_x[:half]) + wide(low)).astype(by_x.dtype), by_x[half:]], axis=0)
    by_y = jnp.concatenate([by_y[:half], (wide(by_y[half:]) + wide(high)).astype(by_y.dtype)], axis=0)
    return own, across_x(by_x), across_y(by_y)


def sum_z(blocks, *earlier):
    own, by_x, by_y = blocks
    by_x = after(by_x, *earlier) if earlier else by_x
    return column_sum(wide(own) + wide(by_x) + wide(by_y), own.dtype)


def column_sum(column, kind):
    rows = column.shape[0] // DEPTH
    total = column[:rows]
    for k in range(1, DEPTH):
        total = total + wide(across_z(column[k * rows : (k + 1) * rows].astype(kind), k))
    return total


def halves_kernel(core_ref, in_ref, out_ref, down_ref, in_w_ref, out_w_ref, down_w_ref):
    devices, rows, width = out_ref.shape
    for d in range(devices):
        here = pl.ds(d * rows, rows)
        for j in range(in_ref.shape[1] // rows):
            in_w_ref[here, j * width : (j + 1) * width] = in_ref[d, j * rows : (j + 1) * rows, :]
        out_w_ref[here, :] = out_ref[d]
    chips, _, rows, _ = down_ref.shape
    for chip in range(chips):
        down_w_ref[pl.ds(chip * rows, rows), :] = down_ref[chip, 0]


def own_halves(core, whole, down_rows, shard):
    devices, rows, width = whole.shape
    steps, chips = 4, devices // 2
    in_rows = (rows - down_rows - shard) // 2
    in_at, out_at = down_rows // in_rows, (rows - shard) // shard
    shapes = ((devices * shard, in_rows // shard * width), (devices * shard, width), (chips * down_rows, width))
    return pl.pallas_call(
        halves_kernel,
        name="own_halves",
        grid_spec=pltpu.PrefetchScalarGridSpec(
            num_scalar_prefetch=1,
            grid=(steps,),
            in_specs=[
                pl.BlockSpec((devices // steps, in_rows, width), lambda i, core_ref: (i, in_at + core_ref[0], 0)),
                pl.BlockSpec((devices // steps, shard, width), lambda i, core_ref: (i, out_at, 0)),
                pl.BlockSpec((chips // steps, 1, down_rows, width), lambda i, core_ref: (i, core_ref[0], 0, 0)),
            ],
            out_specs=[pl.BlockSpec((shape[0] // steps, shape[1]), lambda i, core_ref: (i, 0)) for shape in shapes],
        ),
        out_shape=[jax.ShapeDtypeStruct(shape, whole.dtype) for shape in shapes],
        compiler_params=pltpu.CompilerParams(vmem_limit_bytes=32 * 2**20),
    )(core.reshape(1), whole, whole, whole.reshape(chips, 2, rows, width))


def document_bounds(segments):
    seq_count, blocks, span_len = segments.shape
    length = blocks * span_len
    numbers = lax.iota(jnp.int32, length // min(512, length) + 2)
    flat = segments.reshape(seq_count, length)
    below = jnp.sum((flat[:, :, None] < numbers).astype(jnp.int32), axis=1)
    here = flat[:, :, None] == numbers[:-1]
    starts = jnp.sum(jnp.where(here, below[:, None, :-1], 0), axis=2)
    ends = jnp.sum(jnp.where(here, below[:, None, 1:], 0), axis=2)
    return starts.reshape(segments.shape), ends.reshape(segments.shape)


def query_bounds(bounds, place, tile):
    near = [lax.dynamic_index_in_dim(bounds, place ^ k, 1, keepdims=False) for k in (0, 2)]
    near = jnp.stack(near, axis=0)
    return near.reshape(near.shape[0], near.shape[1], -1, tile)


def gelu_both(values):
    slope = float(np.sqrt(2.0 / np.pi))
    square = values * values
    curve = jnp.tanh(slope * values * (1.0 + 0.044715 * square))
    half = 0.5 * (1.0 + curve)
    rise = half + 0.5 * values * (1.0 - curve * curve) * (slope * (1.0 + 3 * 0.044715 * square))
    return values * half, rise


def joined(block):
    return jnp.concatenate([block, mate(block)], axis=0)


def halves_added(block):
    half = block.shape[0] // 2
    return block[:half] + mate(block[half:])


def norm_back(grad, rows, scale, gain):
    weighted = grad * gain
    inner = jnp.mean(rows * weighted, axis=-1, keepdims=True)
    return scale * weighted - rows * (scale * scale * scale) * inner


def dot_on(left, right, left_dim, right_dim):
    return lax.dot_general(left, right, (((left_dim,), (right_dim,)), ((), ())), preferred_element_type=jnp.float32)


def pair_body(
    inputs,
    segments,
    bucket_table,
    norm_gain,
    w_query,
    w_key,
    w_value,
    w_out,
    rel_bias,
    ff_gain,
    w_in,
    w_down,
    cotangent,
):
    low = jnp.bfloat16
    seq_count, _, part_len, width = inputs.shape
    groups = lax.axis_size("head")
    span_len = part_len * groups
    blocks = lax.axis_size("blk")
    group, place = lax.axis_index("head"), lax.axis_index("blk")
    core, side = place % 2, place // 2
    slots = slot_table()
    shard = w_query.shape[0]
    chip_rows = 2 * shard
    head_cols = 3 * HD
    first_cols = groups * head_cols
    half_width = groups * HD
    half_hidden = w_in.shape[1] // 2
    down_rows = w_down.shape[0]
    half_out = half_width // 2
    tokens = seq_count * part_len

    def by_core(first, second):
        return jnp.where(core == 0, first, second)

    def by_side(first, second):
        return jnp.where(side == 0, first, second)

    def exchanged(block):
        return lax.all_to_all(block, "head", split_axis=0, concat_axis=0, tiled=True)

    every, first_every = (0, width), (0, first_cols)
    gains = jnp.concatenate([norm_gain, ff_gain, rel_bias, jnp.zeros((128 - 5 * shard // 2,), low)])
    gains_near = mate(gains[None, :])[0]
    gains = jnp.stack([by_core(gains, gains_near), by_core(gains_near, gains)], axis=0)
    gains = jnp.pad(gains, ((0, 14), (0, 0)))
    lay_gain = ((0, 16, 0, (0, 128), lambda k: (CHIP + k, 16, 0, (0, 128))),)
    gain_blocks = gather_corner(gather_xy(gather_z(gains)))

    def head_columns(weight, which):
        return weight.reshape(shard, groups, 2, HD)[:, :, which]

    def cut(which):
        return jnp.stack([head_columns(w, which) for w in (w_query, w_key, w_value)], axis=2).reshape(shard, -1)

    first_cut, second_cut = cut(0), cut(1)
    chunks = [by_side(first_cut, second_cut), across_x(by_side(second_cut, first_cut))]
    first_blocks, pace = [], None
    for chunk in chunks:
        own = jnp.concatenate(gather_z(chunk), axis=0)
        pace = own
        both = jnp.concatenate([own, across_y(own)], axis=0)
        first_blocks += [both, mate(both)]
    plan = []
    for k in range(CHIPS):
        z, y, x = turn_of(k)
        for far, slot in enumerate((DEVICE, MATE)):
            source = (None, 0, (DEPTH * y + z) * shard, first_every)
            plan.append((2 * x + far, source, 4, (slot + k, shard, 0, first_every), shard))
    (first_w,) = moved("whole_first", slots, first_blocks, ((width, first_cols),), tuple(plan))

    def hidden_columns(which):
        return w_in.reshape(shard, -1, 2, down_rows)[:, :, which].reshape(shard, -1, width)

    payload_in = jnp.stack([hidden_columns(0), hidden_columns(1)], axis=0).transpose(0, 2, 1, 3).reshape(-1, width)
    in_rows = 2 * chip_rows + shard
    payload = jnp.concatenate([w_down, payload_in, w_out], axis=0)
    whole = lax.all_gather(payload, ("head", "blk"), axis=0, tiled=False)
    in_w, out_w, down_w = own_halves(core, whole, down_rows, shard)

    lay_in = (
        (0, chip_rows, 0, every, lambda k: (CHIP + k, chip_rows, 0, (0, width))),
        (chip_rows, chip_rows, 0, every, lambda k: (CHIP + k, chip_rows, 0, (width, width))),
        (2 * chip_rows, shard, 1, every, lambda k: (CHIP + k, shard, 0, every)),
    )
    lay_down = ((0, down_rows, 0, every, lambda k: (CHIP + k, down_rows, 0, every)),)

    (gain_w,) = placed("whole_gain", slots, gain_blocks, lay_gain, ((16 * CHIPS, 128),), grouped(16))
    gain_w = wide(gain_w.reshape(CHIPS, 16, 128)[:, :2])
    gain_one = gain_w[:, :, :shard].reshape(-1)
    gain_two = gain_w[:, :, shard : 2 * shard].reshape(-1)
    rel_table = gain_w[:, :, 2 * shard : 5 * shard // 2].reshape(HEADS, BUCKETS)
    rel_here = lax.dynamic_index_in_dim(rel_table, 2 * group + side, 0, keepdims=False)

    bucket_hot = bucket_table[:, None] == lax.iota(jnp.int32, BUCKETS)[None, :]
    by_offset = jnp.sum(jnp.where(bucket_hot, rel_here[None, :], 0.0), axis=1)
    places = strip_places()
    place_hot = jnp.asarray(places.reshape(-1))[:, None] == lax.iota(jnp.int32, 2 * MAXREL + 1)[None, :]
    place_hot = place_hot.astype(jnp.float32)
    waves = jnp.dot(place_hot, by_offset, precision=lax.Precision.HIGHEST)
    waves = waves.reshape(places.shape[0], 1, places.shape[1])
    far_bias = jnp.stack([by_offset[0], by_offset[-1]])
    bias = bias_strip(far_bias, waves)
    starts, ends = document_bounds(segments)
    starts, ends = query_bounds(starts, place, TQ), query_bounds(ends, place, TQ)
    edges = jnp.stack([starts[..., 0], starts[..., -1], ends[..., 0], ends[..., -1]], axis=-1)
    base = (place ^ jnp.asarray([0, 2, 1, 3], jnp.int32)) * span_len

    input_rows = inputs.reshape(tokens, width)
    both_rows = wide(jnp.concatenate([input_rows, across_x(input_rows)], axis=0))
    both_scale = lax.rsqrt(jnp.mean(both_rows * both_rows, axis=-1, keepdims=True) + EPS)
    token_rows, scale_one = both_rows[:tokens], both_scale[:tokens]
    first_in = (both_rows * both_scale * gain_one).astype(low).reshape(2, seq_count, part_len, width)
    first_in = [first_in[:, seq].reshape(2 * part_len, width) for seq in range(seq_count)]

    made = [dot_on(first_w, rows, 0, 1).astype(low) for rows in first_in]
    bounds = [(starts[:, seq : seq + 1], ends[:, seq : seq + 1], bias) for seq in range(seq_count)]
    edges = [edges[:, seq].reshape(-1) for seq in range(seq_count)]
    attended, heads, attn_cols = [], [], [None] * seq_count
    sent = exchanged(made[0].reshape(groups, head_cols, 2 * part_len))
    for seq in range(seq_count):
        heads.append([sent, mate(sent)])
        done = attend(base, edges[seq], far_bias, heads[seq], *bounds[seq])
        if seq + 1 < seq_count:
            done, sent = beside(done, exchanged(made[seq + 1].reshape(groups, head_cols, 2 * part_len)))
        else:
            done, attn_cols[seq - 1] = beside(done, attn_cols[seq - 1])
        attended.append(done)
        attn_cols[seq] = exchanged(done[1])
    attn_cols = [block.reshape(half_width, 2 * part_len) for block in attn_cols]
    attn_near = [block[:, :part_len] for block in attn_cols]
    attn_far = [across_x(block[:, part_len:]) for block in attn_cols]
    attn_near, attn_far = jnp.concatenate(attn_near, axis=1), jnp.concatenate(attn_far, axis=1)

    def by_head(near, far):
        near, far = near.reshape(groups, 1, HD, -1), far.reshape(groups, 1, HD, -1)
        return jnp.concatenate([by_side(near, far), by_side(far, near)], axis=1).reshape(2 * half_width, -1)

    attn_cols = by_head(attn_near, attn_far)
    hidden_one = token_rows + dot_on(attn_cols, out_w, 0, 0)
    scale_two = lax.rsqrt(jnp.mean(hidden_one * hidden_one, axis=-1, keepdims=True) + EPS)
    second_in = joined((hidden_one * scale_two * gain_two).astype(low))
    activated, rise = gelu_both(dot_on(second_in, in_w, 1, 0))
    activated = activated.astype(low)
    layer_out = (hidden_one + halves_added(dot_on(activated, down_w, 1, 0))).astype(low).reshape(inputs.shape)

    incoming_low = cotangent.reshape(tokens, width)
    incoming = joined(incoming_low)
    up_grad = (dot_on(incoming, down_w, 1, 1) * rise).astype(low)
    whole_down = dot_on(activated, incoming, 0, 0).astype(low)
    down_parts = sum_corner("parts_down", slots, (whole_down,), lay_down, down_rows, width)
    second_grad = dot_on(up_grad, in_w, 1, 1)
    second_grad = halves_added(second_grad)
    hidden_part = norm_back(second_grad, hidden_one, scale_two, gain_two)
    gain_terms = second_grad * hidden_one * scale_two
    hidden_grad = wide(incoming_low) + hidden_part
    branch, down_parts = beside(hidden_grad.astype(low), down_parts)
    down_parts = sum_xy(down_parts)
    grad_cols = dot_on(out_w, branch, 1, 1).astype(low)
    grad_cols = grad_cols.reshape(groups, 2, HD, tokens)
    grad_far = across_x(by_side(grad_cols[:, 1], grad_cols[:, 0]))
    grad_near = by_side(grad_cols[:, 0], grad_cols[:, 1])

    whole_in = dot_on(after(second_in, grad_cols), up_grad, 0, 0).astype(low)
    whole_out = dot_on(attn_cols, branch, 1, 0).astype(low).reshape(-1, 2, shard, width)
    out_mine, out_given = by_core(whole_out[:, 0], whole_out[:, 1]), by_core(whole_out[:, 1], whole_out[:, 0])
    whole_out = (wide(out_mine) + wide(mate(out_given))).astype(low).reshape(half_width, width)
    in_parts = sum_corner("parts_in", slots, (whole_in, whole_out), lay_in, in_rows, width)

    lanes = [slice(seq * part_len, (seq + 1) * part_len) for seq in range(seq_count)]
    grads = [block[:, :, lane] for lane in lanes for block in (grad_near, grad_far)]
    grads = exchanged(jnp.concatenate(grads, axis=2))
    grads = [grads[:, :, 2 * part_len * seq : 2 * part_len * (seq + 1)] for seq in range(seq_count)]
    grads[0], down_parts = beside(grads[0], down_parts)
    sums, made, sent = (), [], None
    for seq in range(seq_count):
        outs, _, lse = attended[seq]
        done = attend_back(base, edges[seq], far_bias, grads[seq], outs, lse, heads[seq], *bounds[seq], sums)
        if seq == 0:
            done, in_parts, grad_down = beside(done, in_parts, sum_z(down_parts))
        else:
            done, in_parts, made[0] = beside(done, in_parts, made[0])
        near_grad, (far_grad,), sums = done
        far_grad = wide(mate(far_grad))
        near_grad = jnp.concatenate([near_grad[:, :HD], (wide(near_grad[:, HD:]) + far_grad).astype(low)], axis=1)
        if seq == 0:
            grads[1], near_grad = beside(grads[1], near_grad)
            in_parts = sum_xy(in_parts)
        else:
            in_sum = sum_z(in_parts, near_grad)
        made.append(exchanged(near_grad))
    made = [block.reshape(first_cols, 2 * part_len) for block in made]
    whole_first = sum(dot_on(first_in[seq], made[seq], 0, 1) for seq in range(seq_count))
    first_grads = [dot_on(block, first_w, 0, 1) for block in made]
    band, sides = sums

    ones = lax.broadcasted_iota(jnp.int32, (2 * tokens, 128), 1)
    terms = jnp.stack([grad.reshape(2, part_len, width) for grad in first_grads], axis=1).reshape(2 * tokens, width)
    terms = (terms * both_rows * both_scale).astype(low)
    gain_cols = dot_on(terms, (ones == 0).astype(low), 0, 0)
    gain_cols = gain_cols + dot_on(gain_terms.astype(low), (ones[:tokens] == 1).astype(low), 0, 0)
    whole_first = jnp.concatenate([whole_first.astype(low), gain_cols.astype(low)], axis=1)
    plan, all_cols = [], (0, first_cols + 128)
    for k in range(CHIPS):
        z, y, x = turn_of(k)
        at = (None, 0, (DEPTH * y + z) * shard, all_cols)
        plan.append((0, (MATE + k, shard, 0, all_cols), 1 + 3 * x, at, shard))
        at = (None, 0, z * shard, all_cols)
        plan.append((0, (DEVICE + k, shard, 0, all_cols), 2 + 3 * x + y, at, shard))
    column = DEPTH * shard
    shapes = ((2 * column, all_cols[1]), (column, all_cols[1]), (column, all_cols[1])) * 2
    parts = moved("parts_first", slots, (whole_first,), shapes, tuple(plan))
    first_sums, pace = [None, None], None
    for x in (1, 0):
        given, near, by_y = parts[3 * x : 3 * x + 3]
        got = mate(given)
        by_y = across_y((wide(by_y) + wide(got[column:])).astype(low))
        total = column_sum(wide(near) + wide(got[:column]) + wide(by_y), low)
        first_sums[x] = across_x(total) if x else total
        pace = got if pace is None else pace

    near_part = jnp.concatenate([grad[:part_len] for grad in first_grads], axis=0)
    far_part = jnp.concatenate([grad[part_len:] for grad in first_grads], axis=0).astype(low)
    first_grad = near_part + wide(across_x(after(far_part, pace)))
    input_part = norm_back(first_grad, token_rows, scale_one, gain_one)
    input_grad = (hidden_grad + input_part).astype(low).reshape(inputs.shape)

    gain_mine = first_sums[0][:, first_cols : first_cols + 2] + first_sums[1][:, first_cols : first_cols + 2]
    first_sums = [block[:, :first_cols] for block in first_sums]
    first_pair = [by_side(*first_sums), by_side(*first_sums[::-1])]
    first_pair = [block.reshape(shard, groups, 3, HD) for block in first_pair]
    grad_query, grad_key, grad_value = (
        jnp.stack([block[:, :, which] for block in first_pair], axis=2).reshape(shard, -1) for which in range(3)
    )

    hidden_rows = jnp.concatenate([in_sum[:chip_rows], in_sum[chip_rows : 2 * chip_rows]], axis=1)
    mine = by_core(hidden_rows[:shard], hidden_rows[shard:])
    other = mate(by_core(hidden_rows[shard:], hidden_rows[:shard]))
    in_pair = [block.reshape(shard, -1, down_rows) for block in (by_core(mine, other), by_core(other, mine))]
    grad_in = jnp.stack(in_pair, axis=2).reshape(shard, -1)
    grad_out = in_sum[2 * chip_rows :]

    near_sums, far_sums = band_sums_of(after(band, pace), sides)
    offset_sums = jnp.dot(near_sums.reshape(-1), place_hot, precision=lax.Precision.HIGHEST)
    far_sums = jnp.sum(far_sums, axis=1)
    end_hot = lax.iota(jnp.int32, 2 * MAXREL + 1)
    offset_sums = offset_sums + jnp.where(end_hot == 0, far_sums[0], 0.0)
    offset_sums = offset_sums + jnp.where(end_hot == 2 * MAXREL, far_sums[1], 0.0)
    rel_grad = jnp.sum(jnp.where(bucket_hot, offset_sums[:, None], 0.0), axis=0)
    rel_grad = jnp.pad(rel_grad[None, :], ((0, 7), (0, 128 - BUCKETS)))
    rel_sum = (rel_grad + mate(rel_grad))[0]
    rel_mine = by_core(rel_sum[: BUCKETS // 2], rel_sum[BUCKETS // 2 : BUCKETS])

    return (
        layer_out,
        input_grad,
        gain_mine[:, 0],
        grad_query,
        grad_key,
        grad_value,
        grad_out,
        rel_mine,
        gain_mine[:, 1],
        grad_in,
        grad_down,
    )


def solution(mesh):
    placed = (
        P(None, "blk", "head", None),
        P(),
        P(),
        P(("head", "blk")),
        P(("head", "blk"), None),
        P(("head", "blk"), None),
        P(("head", "blk"), None),
        P(("head", "blk"), None),
        P(("head", "blk")),
        P(("head", "blk")),
        P(("head", "blk"), None),
        P(("head", "blk"), None),
        P(None, "blk", "head", None),
    )
    n_head, n_blk = mesh.shape["head"], mesh.shape["blk"]
    paired = HEADS == 2 * n_head and (n_head, n_blk) == (8, 4)
    return jax.shard_map(
        pair_body if paired else ring_body,
        mesh=mesh,
        in_specs=placed,
        out_specs=(
            P(None, "blk", "head", None),
            P(None, "blk", "head", None),
            P(("head", "blk")),
            P(("head", "blk"), None),
            P(("head", "blk"), None),
            P(("head", "blk"), None),
            P(("head", "blk"), None),
            P(("head", "blk")),
            P(("head", "blk")),
            P(("head", "blk"), None),
            P(("head", "blk"), None),
        ),
        check_vma=False,
    )
```

```python
import functools

import jax
import jax.numpy as jnp
import numpy as np
from jax import lax
from jax.experimental import pallas as pl
from jax.experimental.pallas import tpu as pltpu
from jax.sharding import PartitionSpec as P

HEADS = 16
HD = 64
BUCKETS = 32
MAXREL = 128
EPS = 1e-06
FLOOR = -1e30


def from_behind(block, axis, distance):
    devices = range(lax.axis_size(axis))
    route = [((i - distance) % len(devices), i) for i in devices]
    return lax.ppermute(block, axis, route)


def rms_scale(token_rows, gain_vector):
    return (
        token_rows
        * lax.rsqrt(jnp.mean(token_rows * token_rows, axis=-1, keepdims=True) + EPS)
        * gain_vector
    )


def smooth(values):
    return jax.nn.gelu(values, approximate=True)


def band_layout(span_len):
    tile_side = min(128, span_len)
    reach = MAXREL // tile_side + 2
    return (tile_side, span_len // tile_side, reach)


def band_tables(bucket_table, rel_here, span_len):
    tile_side, _, reach = band_layout(span_len)
    kinds = 2 * reach + 1
    gaps = lax.iota(jnp.int32, kinds) - reach
    rows_in = lax.iota(jnp.int32, tile_side)
    offsets = gaps[:, None, None] * tile_side + rows_in[None, None, :] - rows_in[None, :, None]
    lookup = jnp.clip(offsets, -MAXREL, MAXREL) + MAXREL
    bucket = jnp.take(bucket_table, lookup.reshape(-1), axis=0)
    onehot = (bucket[:, None] == lax.iota(jnp.int32, BUCKETS)[None, :]).astype(jnp.float32)
    band_bias = jnp.dot(rel_here, onehot.T, precision=lax.Precision.HIGHEST)
    return (band_bias.reshape(rel_here.shape[0], kinds, tile_side, tile_side), onehot)


def band_index(block_gap, span_len):
    _, tiles, reach = band_layout(span_len)
    row_tile = lax.iota(jnp.int32, tiles)[:, None, None, None]
    col_tile = lax.iota(jnp.int32, tiles)[None, None, :, None]
    return jnp.clip(block_gap * tiles + col_tile - row_tile, -reach, reach) + reach


def bias_tile(band_bias, block_gap, span_len):
    heads_count, kinds, tile_side, _ = band_bias.shape
    tiles = span_len // tile_side
    which = band_index(block_gap, span_len)
    result = jnp.zeros((heads_count, tiles, tile_side, tiles, tile_side), jnp.float32)
    for kind in range(kinds):
        result = jnp.where(which[None] == kind, band_bias[:, kind][:, None, :, None, :], result)
    return result.reshape(heads_count, span_len, span_len)


def band_sums(tile_sum, block_gap, span_len):
    tile_side, tiles, reach = band_layout(span_len)
    heads_count = tile_sum.shape[0]
    split_sum = tile_sum.reshape(heads_count, tiles, tile_side, tiles, tile_side)
    which = band_index(block_gap, span_len)
    parts = []
    for kind in range(2 * reach + 1):
        parts.append(jnp.sum(jnp.where(which[None] == kind, split_sum, 0.0), axis=(1, 3)))
    return jnp.stack(parts, axis=1).reshape(heads_count, -1)


def pass_grads(key_grad, value_grad):
    return (
        from_behind(key_grad.astype(jnp.bfloat16), "blk", 1).astype(key_grad.dtype),
        from_behind(value_grad.astype(jnp.bfloat16), "blk", 1).astype(value_grad.dtype),
    )


def ring_body(
    inputs,
    segments,
    bucket_table,
    norm_gain,
    w_query,
    w_key,
    w_value,
    w_out,
    rel_bias,
    ff_gain,
    w_in,
    w_down,
    cotangent,
):
    seq_count, _, part_len, width = inputs.shape
    cycle_size = lax.axis_size("blk")
    head_groups = lax.axis_size("head")
    heads_here = HEADS // head_groups
    span_len = part_len * head_groups
    cycle_place = lax.axis_index("blk")
    head_place = lax.axis_index("head")
    gathered = (
        lax.all_gather(norm_gain, ("head", "blk"), axis=0, tiled=True),
        lax.all_gather(w_query, ("head", "blk"), axis=0, tiled=True),
        lax.all_gather(w_key, ("head", "blk"), axis=0, tiled=True),
        lax.all_gather(w_value, ("head", "blk"), axis=0, tiled=True),
        lax.all_gather(w_out, ("head", "blk"), axis=0, tiled=True),
        lax.all_gather(rel_bias, ("head", "blk"), axis=0, tiled=True),
        lax.all_gather(ff_gain, ("head", "blk"), axis=0, tiled=True),
        lax.all_gather(w_in, ("head", "blk"), axis=0, tiled=True),
        lax.all_gather(w_down, ("head", "blk"), axis=0, tiled=True),
    )
    gain_one, query_w, key_w, value_w, out_w, rel_flat, gain_two, in_w, down_w = gathered
    token_rows = inputs.reshape(-1, width).astype(jnp.float32)
    normed, norm_one_back = jax.vjp(rms_scale, token_rows, gain_one.astype(jnp.float32))
    first_in = normed.astype(jnp.bfloat16)

    def project(weight):
        made_rows = jnp.dot(first_in, weight, preferred_element_type=jnp.float32)
        return made_rows.astype(jnp.bfloat16).reshape(seq_count, part_len, -1)

    queries, keys_home, values_home = (
        lax.all_to_all(project(query_w), "head", split_axis=2, concat_axis=1, tiled=True),
        lax.all_to_all(project(key_w), "head", split_axis=2, concat_axis=1, tiled=True),
        lax.all_to_all(project(value_w), "head", split_axis=2, concat_axis=1, tiled=True),
    )
    head_shape = (seq_count, span_len, heads_here, HD)
    queries = queries.reshape(head_shape)
    keys_home = keys_home.reshape(head_shape)
    values_home = values_home.reshape(head_shape)
    rel_table = rel_flat.astype(jnp.float32).reshape(HEADS, BUCKETS)
    rel_here = lax.dynamic_slice_in_dim(rel_table, head_place * heads_here, heads_here, 0)
    band_bias, band_onehot = band_tables(bucket_table, rel_here, span_len)

    def tile_scores(query_rows, key_rows, query_block, key_block):
        query_ids = lax.dynamic_index_in_dim(segments, query_block, 1, keepdims=False)
        key_ids = lax.dynamic_index_in_dim(segments, key_block, 1, keepdims=False)
        plain_scores = (
            jnp.einsum("sihd,sjhd->shij", query_rows, key_rows, preferred_element_type=jnp.float32)
            + bias_tile(band_bias, key_block - query_block, span_len)[None]
        )
        same_doc = query_ids[:, None, :, None] == key_ids[:, None, None, :]
        return jnp.where(same_doc, plain_scores, FLOOR)

    first_scores = tile_scores(queries, keys_home, cycle_place, cycle_place)
    row_max = jnp.max(first_scores, axis=-1)
    first_weights = jnp.exp(first_scores - row_max[..., None])
    row_total = jnp.sum(first_weights, axis=-1)
    summed = jnp.einsum(
        "shij,sjhd->sihd",
        first_weights.astype(jnp.bfloat16),
        values_home,
        preferred_element_type=jnp.float32,
    )

    def forward_turn(cycle_turn, state_now):
        old_max, old_total, old_summed, key_rows, value_rows = state_now
        key_rows, value_rows = from_behind((key_rows, value_rows), "blk", 1)
        source = (cycle_place - cycle_turn) % cycle_size
        scores = tile_scores(queries, key_rows, cycle_place, source)
        new_max = jnp.maximum(old_max, jnp.max(scores, axis=-1))
        shrink = jnp.exp(old_max - new_max)
        weights_now = jnp.exp(scores - new_max[..., None])
        new_total = old_total * shrink + jnp.sum(weights_now, axis=-1)
        new_summed = old_summed * jnp.transpose(shrink, (0, 2, 1))[..., None] + jnp.einsum(
            "shij,sjhd->sihd",
            weights_now.astype(jnp.bfloat16),
            value_rows,
            preferred_element_type=jnp.float32,
        )
        return (new_max, new_total, new_summed, key_rows, value_rows)

    row_max, row_total, summed, _, _ = lax.fori_loop(
        1, cycle_size, forward_turn, (row_max, row_total, summed, keys_home, values_home)
    )
    log_total = row_max + jnp.log(row_total)
    attended = summed / jnp.transpose(row_total, (0, 2, 1))[..., None]
    attended_low = attended.astype(jnp.bfloat16).reshape(seq_count, span_len, heads_here * HD)
    attn_rows = lax.all_to_all(
        attended_low, "head", split_axis=1, concat_axis=2, tiled=True
    ).reshape(-1, HEADS * HD)
    hidden_one = token_rows + jnp.dot(attn_rows, out_w, preferred_element_type=jnp.float32)
    normed_two, norm_two_back = jax.vjp(rms_scale, hidden_one, gain_two.astype(jnp.float32))
    second_in = normed_two.astype(jnp.bfloat16)
    upward = jnp.dot(second_in, in_w, preferred_element_type=jnp.float32)
    activated, smooth_back = jax.vjp(smooth, upward)
    activated_low = activated.astype(jnp.bfloat16)
    layer_rows = hidden_one + jnp.dot(activated_low, down_w, preferred_element_type=jnp.float32)
    layer_out = layer_rows.astype(jnp.bfloat16).reshape(inputs.shape)
    back_query, back_key, back_value, back_out, back_in, back_down = (
        query_w,
        key_w,
        value_w,
        out_w,
        in_w,
        down_w,
    )
    incoming_low = cotangent.reshape(-1, width)
    incoming = incoming_low.astype(jnp.float32)
    grad_down = jnp.dot(activated_low.T, incoming_low, preferred_element_type=jnp.float32)
    (up_grad,) = smooth_back(jnp.dot(incoming_low, back_down.T, preferred_element_type=jnp.float32))
    up_low = up_grad.astype(jnp.bfloat16)
    grad_in = jnp.dot(second_in.T, up_low, preferred_element_type=jnp.float32)
    hidden_part, grad_gain_two = norm_two_back(
        jnp.dot(up_low, back_in.T, preferred_element_type=jnp.float32)
    )
    hidden_grad = incoming + hidden_part
    branch_low = hidden_grad.astype(jnp.bfloat16)
    grad_out = jnp.dot(attn_rows.T, branch_low, preferred_element_type=jnp.float32)
    attn_grad_low = jnp.dot(branch_low, back_out.T, preferred_element_type=jnp.float32).astype(
        jnp.bfloat16
    )
    grad_heads = lax.all_to_all(
        attn_grad_low.reshape(seq_count, part_len, HEADS * HD),
        "head",
        split_axis=2,
        concat_axis=1,
        tiled=True,
    ).reshape(head_shape)
    row_delta = jnp.transpose(
        jnp.sum(grad_heads.astype(jnp.float32) * attended, axis=-1), (0, 2, 1)
    )

    def tile_grads(
        query_rows, grad_rows, log_rows, delta_rows, key_rows, value_rows, query_block, key_block
    ):
        scores = tile_scores(query_rows, key_rows, query_block, key_block)
        probs = jnp.exp(scores - log_rows[..., None])
        value_part = jnp.einsum(
            "shij,sihd->sjhd",
            probs.astype(jnp.bfloat16),
            grad_rows,
            preferred_element_type=jnp.float32,
        )
        prob_grad = jnp.einsum(
            "sihd,sjhd->shij", grad_rows, value_rows, preferred_element_type=jnp.float32
        )
        score_low = (probs * (prob_grad - delta_rows[..., None])).astype(jnp.bfloat16)
        query_part = jnp.einsum(
            "shij,sjhd->sihd", score_low, key_rows, preferred_element_type=jnp.float32
        )
        key_part = jnp.einsum(
            "shij,sihd->sjhd", score_low, query_rows, preferred_element_type=jnp.float32
        )
        tile_sum = jnp.sum(score_low.astype(jnp.float32), axis=0)
        rel_part = jnp.dot(
            band_sums(tile_sum, key_block - query_block, span_len),
            band_onehot,
            precision=lax.Precision.HIGHEST,
        )
        return (query_part, key_part, value_part, rel_part)

    query_grad, key_grad, value_grad, rel_grad = tile_grads(
        queries, grad_heads, log_total, row_delta, keys_home, values_home, cycle_place, cycle_place
    )

    def key_turn(cycle_turn, state_now):
        key_rows, value_rows, key_sum, value_sum, query_sum, rel_sum = state_now
        key_sum, value_sum = pass_grads(key_sum, value_sum)
        key_rows, value_rows = from_behind((key_rows, value_rows), "blk", 1)
        source = (cycle_place - cycle_turn) % cycle_size
        query_part, key_part, value_part, rel_part = tile_grads(
            queries, grad_heads, log_total, row_delta, key_rows, value_rows, cycle_place, source
        )
        return (
            key_rows,
            value_rows,
            key_sum + key_part,
            value_sum + value_part,
            query_sum + query_part,
            rel_sum + rel_part,
        )

    state_first = (keys_home, values_home, key_grad, value_grad, query_grad, rel_grad)
    _, _, key_grad, value_grad, query_grad, rel_grad = lax.fori_loop(
        1, cycle_size, key_turn, state_first
    )
    key_grad, value_grad = pass_grads(key_grad, value_grad)
    block_shape = (seq_count, span_len, heads_here * HD)
    query_rows, key_rows_back, value_rows_back = (
        lax.all_to_all(
            query_grad.astype(jnp.bfloat16).reshape(block_shape),
            "head",
            split_axis=1,
            concat_axis=2,
            tiled=True,
        ),
        lax.all_to_all(
            key_grad.astype(jnp.bfloat16).reshape(block_shape),
            "head",
            split_axis=1,
            concat_axis=2,
            tiled=True,
        ),
        lax.all_to_all(
            value_grad.astype(jnp.bfloat16).reshape(block_shape),
            "head",
            split_axis=1,
            concat_axis=2,
            tiled=True,
        ),
    )
    query_rows = query_rows.reshape(-1, HEADS * HD)
    key_rows_back = key_rows_back.reshape(-1, HEADS * HD)
    value_rows_back = value_rows_back.reshape(-1, HEADS * HD)
    grad_query = jnp.dot(first_in.T, query_rows, preferred_element_type=jnp.float32)
    grad_key = jnp.dot(first_in.T, key_rows_back, preferred_element_type=jnp.float32)
    grad_value = jnp.dot(first_in.T, value_rows_back, preferred_element_type=jnp.float32)
    first_grad = (
        jnp.dot(query_rows, back_query.T, preferred_element_type=jnp.float32)
        + jnp.dot(key_rows_back, back_key.T, preferred_element_type=jnp.float32)
        + jnp.dot(value_rows_back, back_value.T, preferred_element_type=jnp.float32)
    )
    input_part, grad_gain_one = norm_one_back(first_grad)
    input_grad = (hidden_grad + input_part).astype(jnp.bfloat16).reshape(inputs.shape)
    rel_full = lax.dynamic_update_slice_in_dim(
        jnp.zeros((HEADS, BUCKETS), jnp.float32), rel_grad, head_place * heads_here, 0
    ).reshape(-1)
    shards = tuple(
        (
            lax.psum_scatter(grad_gain_one, ("head", "blk"), scatter_dimension=0, tiled=True),
            lax.psum_scatter(grad_query, ("head", "blk"), scatter_dimension=0, tiled=True),
            lax.psum_scatter(grad_key, ("head", "blk"), scatter_dimension=0, tiled=True),
            lax.psum_scatter(grad_value, ("head", "blk"), scatter_dimension=0, tiled=True),
            lax.psum_scatter(grad_out, ("head", "blk"), scatter_dimension=0, tiled=True),
            lax.psum_scatter(rel_full, ("head", "blk"), scatter_dimension=0, tiled=True),
            lax.psum_scatter(grad_gain_two, ("head", "blk"), scatter_dimension=0, tiled=True),
            lax.psum_scatter(grad_in, ("head", "blk"), scatter_dimension=0, tiled=True),
            lax.psum_scatter(grad_down, ("head", "blk"), scatter_dimension=0, tiled=True),
        )
    )
    return (
        layer_out,
        input_grad,
        shards[0],
        shards[1],
        shards[2],
        shards[3],
        shards[4],
        shards[5],
        shards[6],
        shards[7],
        shards[8],
    )


TQ = 512
KT = 512
MARGIN = 256
AUG = 80
NT = (((1,), (1,)), ((), ()))


def nn(left, right):
    return jnp.dot(left, right, preferred_element_type=jnp.float32)


def flipped(block):
    return block.astype(jnp.float32).T.astype(jnp.bfloat16)


def ones_row(width):
    first = lax.broadcasted_iota(jnp.int32, (AUG - HD, width), 0) == 0
    return jnp.where(first, 1.0, 0.0).astype(jnp.bfloat16)


def pieces_of(seq_count, part_len, groups):
    for seq in range(seq_count):
        for near in range(2):
            for source in range(groups):
                yield seq, near, source, slice((near * seq_count + seq) * part_len, (near * seq_count + seq + 1) * part_len)


def lanes_of(ref, tile_at, per_tile, part_len, lane_base):
    parts = [ref[tile_at * per_tile + k, :HD, pl.ds(lane_base, part_len)] for k in range(per_tile)]
    return parts[0] if per_tile == 1 else jnp.concatenate(parts, axis=1)


def tile_class(edge_ref, row, key_at, query_at):
    first_start, last_start, first_end, last_end = (edge_ref[row * 4 + k] for k in range(4))
    touched = (key_at + KT > first_start) & (key_at < last_end)
    gap = key_at - query_at
    whole = (key_at >= last_start) & (key_at + KT <= first_end)
    plain = whole & ((gap + KT <= -MAXREL + 1) | (gap >= TQ + MAXREL - 1))
    strip_at = jnp.clip(gap, -(KT + MARGIN), TQ + MARGIN) + KT + MARGIN
    return touched, plain, gap, pl.ds(pl.multiple_of(strip_at, 256), KT)


def masked(scores, bias, key_at, start_row, end_row):
    places = lax.broadcasted_iota(jnp.int32, scores.shape, 0) + key_at
    return jnp.where((places >= start_row) & (places < end_row), scores + bias, FLOOR)


def attend_kernel(chips, base_ref, edge_ref, far_ref, *refs):
    kv_refs, q_ref = refs[:chips], refs[0]
    start_ref, end_ref, bias_ref, o_ref, ob_ref, lse_ref, k_rows, v_aug, top_ref, acc_ref = refs[chips:]
    groups, _, span = q_ref.shape
    blocks, seq_count, span_len, _ = k_rows.shape
    part_len = span_len // groups
    per_tile = TQ // part_len
    tiles, key_tiles = span_len // TQ, span_len // KT
    per_key = KT // part_len
    for far in range(chips):
        for seq, near, source, lanes in pieces_of(seq_count, part_len, groups):
            block = 2 * far + near
            k_rows[block, seq, source * part_len : (source + 1) * part_len, :] = flipped(kv_refs[far][source, HD : 2 * HD, lanes])
            at = source % per_key * part_len
            v_aug[block, seq, source // per_key, :HD, at : at + part_len] = kv_refs[far][source, 2 * HD :, lanes]
    for block in range(blocks):
        for seq in range(seq_count):
            for tile in range(key_tiles):
                v_aug[block, seq, tile, HD:, :] = ones_row(KT)

    for seq in range(seq_count):
        for near in range(2):
            lane_base = (near * seq_count + seq) * part_len

            def query_tile(tile, _, seq=seq, near=near, lane_base=lane_base):
                query_at = base_ref[near] + tile * TQ
                row = (near * seq_count + seq) * tiles + tile
                queries = lanes_of(q_ref, tile, per_tile, part_len, lane_base)
                top_ref[...] = jnp.full_like(top_ref, FLOOR)
                acc_ref[...] = jnp.zeros_like(acc_ref)
                start_row = start_ref[near, seq, pl.ds(tile, 1), :]
                end_row = end_ref[near, seq, pl.ds(tile, 1), :]

                def take(scores, shift, block, key_tile):
                    old_top = top_ref[0:1, :]
                    new_top = jnp.maximum(old_top, jnp.max(scores, axis=0, keepdims=True) + shift)
                    weights = jnp.exp(scores - (new_top - shift))
                    acc_ref[...] = acc_ref[...] * jnp.exp(old_top - new_top) + nn(
                        v_aug[block, seq, key_tile], weights.astype(jnp.bfloat16)
                    )
                    top_ref[0:1, :] = new_top

                def key_step(step, _):
                    block, key_tile = step // key_tiles, step % key_tiles
                    key_at = base_ref[block] + key_tile * KT
                    touched, plain, gap, strip = tile_class(edge_ref, row, key_at, query_at)

                    def raw():
                        keys = k_rows[block, seq, pl.ds(pl.multiple_of(key_tile * KT, KT), KT), :]
                        return nn(keys, queries)

                    @pl.when(touched & plain)
                    def _():
                        take(raw(), jnp.where(gap < 0, far_ref[0], far_ref[1]), block, key_tile)

                    @pl.when(touched & jnp.logical_not(plain))
                    def _():
                        take(masked(raw(), bias_ref[strip, :], key_at, start_row, end_row), 0.0, block, key_tile)

                    return 0

                lax.fori_loop(0, blocks * key_tiles, key_step, 0)
                total = acc_ref[HD : HD + 1, :]
                outs = acc_ref[:HD, :] / total
                lse_ref[near, seq, pl.ds(tile, 1), :] = top_ref[0:1, :] + jnp.log(total)
                for k in range(per_tile):
                    part = outs[:, k * part_len : (k + 1) * part_len]
                    o_ref[tile * per_tile + k, :, lane_base : lane_base + part_len] = part
                    ob_ref[2 * (tile * per_tile + k) + (near ^ base_ref[blocks])] = part.astype(jnp.bfloat16)
                return 0

            lax.fori_loop(0, tiles, query_tile, 0)


def attend_back_kernel(chips, carried, g_base, base_ref, edge_ref, far_ref, g_ref, o_ref, lse_ref, *refs):
    kv_refs, q_ref, refs = refs[:chips], refs[0], refs[chips:]
    start_ref, end_ref, bias_ref, *refs = refs
    if carried:
        old_band_ref, old_sides_ref, *refs = refs
    made_refs, refs = refs[:chips], refs[chips:]
    dq_ref = made_refs[0]
    band_ref, sides_ref, k_rows, v_rows, k_aug, dk_acc, dv_acc, dq_acc = refs
    groups, _, span = q_ref.shape
    blocks, seq_count, span_len, _ = k_rows.shape
    part_len = span_len // groups
    per_tile = TQ // part_len
    tiles, key_tiles = span_len // TQ, span_len // KT
    per_key = KT // part_len
    for far in range(chips):
        for seq, near, source, lanes in pieces_of(seq_count, part_len, groups):
            block = 2 * far + near
            rows = slice(source * part_len, (source + 1) * part_len)
            piece = kv_refs[far][source, HD : 2 * HD, lanes]
            k_rows[block, seq, rows, :] = flipped(piece)
            v_rows[block, seq, rows, :] = flipped(kv_refs[far][source, 2 * HD :, lanes])
            at = source % per_key * part_len
            k_aug[block, seq, source // per_key, :HD, at : at + part_len] = piece
    for block in range(blocks):
        for seq in range(seq_count):
            for tile in range(key_tiles):
                k_aug[block, seq, tile, HD:, :] = ones_row(KT)
    dk_acc[...] = jnp.zeros_like(dk_acc)
    dv_acc[...] = jnp.zeros_like(dv_acc)
    band_ref[...] = old_band_ref[...] if carried else jnp.zeros_like(band_ref)
    sides_ref[...] = old_sides_ref[...] if carried else jnp.zeros_like(sides_ref)

    for seq in range(seq_count):
        for near in range(2):
            lane_base = (near * seq_count + seq) * part_len

            def query_tile(tile, _, seq=seq, near=near, lane_base=lane_base):
                query_at = base_ref[near] + tile * TQ
                row = (near * seq_count + seq) * tiles + tile
                queries = lanes_of(q_ref, tile, per_tile, part_len, lane_base)
                first = 2 * tile * per_tile + (near ^ base_ref[blocks])
                grads = [g_ref[first + 2 * k, :, g_base : g_base + part_len] for k in range(per_tile)]
                grads = jnp.concatenate(grads, axis=1)
                outs = lanes_of(o_ref, tile, per_tile, part_len, lane_base)
                delta = jnp.sum(grads.astype(jnp.float32) * outs, axis=0, keepdims=True)
                query_rows, grad_rows = flipped(queries), flipped(grads)
                lse = lse_ref[near, seq, pl.ds(tile, 1), :]
                start_row = start_ref[near, seq, pl.ds(tile, 1), :]
                end_row = end_ref[near, seq, pl.ds(tile, 1), :]
                dq_acc[...] = jnp.zeros_like(dq_acc)

                def take(scores, shift, block, key_tile):
                    rows = pl.ds(pl.multiple_of(key_tile * KT, KT), KT)
                    probs = jnp.exp(scores - (lse - shift))
                    score_grad = probs * (nn(v_rows[block, seq, rows, :], grads) - delta)
                    score_low = score_grad.astype(jnp.bfloat16)
                    dv_acc[block, seq, rows, :] += nn(probs.astype(jnp.bfloat16), grad_rows)
                    dk_acc[block, seq, rows, :] += nn(score_low, query_rows)
                    made = nn(k_aug[block, seq, key_tile], score_low)
                    dq_acc[...] += made
                    return score_grad, made[HD : HD + 1, :]

                def key_step(step, _):
                    block, key_tile = step // key_tiles, step % key_tiles
                    key_at = base_ref[block] + key_tile * KT
                    touched, plain, gap, strip = tile_class(edge_ref, row, key_at, query_at)

                    def raw():
                        keys = k_rows[block, seq, pl.ds(pl.multiple_of(key_tile * KT, KT), KT), :]
                        return nn(keys, queries)

                    @pl.when(touched & plain)
                    def _():
                        _, sums = take(raw(), jnp.where(gap < 0, far_ref[0], far_ref[1]), block, key_tile)
                        side = (gap > 0).astype(jnp.int32)
                        sides_ref[pl.ds(side, 1), :] += sums

                    @pl.when(touched & jnp.logical_not(plain))
                    def _():
                        whole_grad, _ = take(
                            masked(raw(), bias_ref[strip, :], key_at, start_row, end_row), 0.0, block, key_tile
                        )
                        band_ref[strip, :] += whole_grad

                    return 0

                lax.fori_loop(0, blocks * key_tiles, key_step, 0)
                for k in range(per_tile):
                    part = dq_acc[:HD, k * part_len : (k + 1) * part_len].astype(jnp.bfloat16)
                    dq_ref[tile * per_tile + k, :HD, lane_base : lane_base + part_len] = part
                return 0

            lax.fori_loop(0, tiles, query_tile, 0)
    for far in range(chips):
        for seq, near, source, lanes in pieces_of(seq_count, part_len, groups):
            block = 2 * far + near
            rows = slice(source * part_len, (source + 1) * part_len)
            top = 0 if far else HD
            made_refs[far][source, top : top + HD, lanes] = dk_acc[block, seq, rows, :].T.astype(jnp.bfloat16)
            made_refs[far][source, top + HD : top + 2 * HD, lanes] = dv_acc[block, seq, rows, :].T.astype(jnp.bfloat16)


def strip_places():
    width = TQ + 128
    lane = np.arange(width)
    lane = np.where(lane < TQ, lane, lane - width)
    offset = 128 * (np.arange(TQ // 128 + 2)[:, None] - 1) - lane[None, :]
    return np.clip(offset, -MAXREL, MAXREL) + MAXREL


def strip_kernel(far_ref, wave_ref, strip_ref):
    near_blocks, _, width = wave_ref.shape
    first = KT + MARGIN - 128
    strip_ref[:first, :] = jnp.full((first, TQ), far_ref[0], jnp.float32)
    for k in range(near_blocks):
        spread = jnp.broadcast_to(wave_ref[k], (128, width))
        turned = pltpu.roll(spread, 0, 1, stride=1, stride_axis=0)
        strip_ref[first + 128 * k : first + 128 * (k + 1), :] = turned[:, :TQ]
    last = first + 128 * near_blocks
    strip_ref[last:, :] = jnp.full((strip_ref.shape[0] - last, TQ), far_ref[1], jnp.float32)


def bias_strip(far_bias, waves):
    return pl.pallas_call(
        strip_kernel,
        name="bias_strip",
        out_shape=jax.ShapeDtypeStruct((2 * KT + 2 * MARGIN + TQ, TQ), jnp.float32),
        in_specs=[SMEM, VMEM],
        out_specs=VMEM,
        compiler_params=pltpu.CompilerParams(vmem_limit_bytes=32 * 2**20),
    )(far_bias, waves)


def band_kernel(band_ref, sides_ref, near_ref, far_ref):
    near_blocks, _, width = near_ref.shape
    first = KT + MARGIN - 128
    last = first + 128 * near_blocks
    left = jnp.sum(band_ref[:first, :], axis=0, keepdims=True) + sides_ref[0:1, :]
    right = jnp.sum(band_ref[last:, :], axis=0, keepdims=True) + sides_ref[1:2, :]
    far_ref[...] = jnp.concatenate([left, right, jnp.zeros((6, TQ), jnp.float32)], axis=0)
    for k in range(near_blocks):
        rows = band_ref[first + 128 * k : first + 128 * (k + 1), :]
        spread = jnp.concatenate([rows, jnp.zeros((128, width - TQ), jnp.float32)], axis=1)
        row = lax.broadcasted_iota(jnp.int32, spread.shape, 0)
        for step in (1, 2, 4):
            spread = jnp.where((row & step) != 0, pltpu.roll(spread, width - step, 1), spread)
        total = spread[:8, :]
        for at in range(8, 128, 8):
            total = total + pltpu.roll(spread[at : at + 8, :], width - at, 1)
        near_ref[k] = jnp.sum(total, axis=0, keepdims=True)


def band_sums_of(band, sides):
    return pl.pallas_call(
        band_kernel,
        name="band_sums",
        out_shape=(
            jax.ShapeDtypeStruct((TQ // 128 + 2, 1, TQ + 128), jnp.float32),
            jax.ShapeDtypeStruct((8, TQ), jnp.float32),
        ),
        in_specs=[VMEM, VMEM],
        out_specs=(VMEM, VMEM),
        compiler_params=pltpu.CompilerParams(vmem_limit_bytes=32 * 2**20),
    )(band, sides)


SMEM = pl.BlockSpec(memory_space=pltpu.SMEM)
VMEM = pl.BlockSpec(memory_space=pltpu.VMEM)


def attend(base, edges, far_bias, kvs, starts, ends, bias):
    chips = len(kvs)
    groups, _, span = kvs[0].shape
    shape = (groups, HD, span)
    _, seq_count, tiles, _ = starts.shape
    blocks, span_len = 2 * chips, tiles * TQ
    return pl.pallas_call(
        functools.partial(attend_kernel, chips),
        name="attend",
        out_shape=(
            jax.ShapeDtypeStruct(shape, jnp.float32),
            jax.ShapeDtypeStruct((2 * groups, HD, span // 2), jnp.bfloat16),
            jax.ShapeDtypeStruct(starts.shape, jnp.float32),
        ),
        in_specs=[SMEM] * 3 + [VMEM] * (chips + 3),
        out_specs=(VMEM,) * 3,
        scratch_shapes=[
            pltpu.VMEM((blocks, seq_count, span_len, HD), jnp.bfloat16),
            pltpu.VMEM((blocks, seq_count, span_len // KT, AUG, KT), jnp.bfloat16),
            pltpu.VMEM((8, TQ), jnp.float32),
            pltpu.VMEM((AUG, TQ), jnp.float32),
        ],
        cost_estimate=pl.CostEstimate(flops=1, transcendentals=0, bytes_accessed=1),
        compiler_params=pltpu.CompilerParams(vmem_limit_bytes=48 * 2**20),
    )(base, edges, far_bias, *kvs, starts, ends, bias)


def attend_back(base, edges, far_bias, g, seq, o, lse, kvs, starts, ends, bias, sums=()):
    chips = len(kvs)
    groups, _, span = kvs[0].shape
    _, seq_count, tiles, _ = starts.shape
    blocks, span_len = 2 * chips, tiles * TQ
    made = pl.pallas_call(
        functools.partial(attend_back_kernel, chips, bool(sums), seq * span // 2),
        name="attend_back",
        out_shape=(jax.ShapeDtypeStruct(kvs[0].shape, jnp.bfloat16),)
        + (jax.ShapeDtypeStruct((groups, 2 * HD, span), jnp.bfloat16),) * (chips - 1)
        + (jax.ShapeDtypeStruct(bias.shape, jnp.float32), jax.ShapeDtypeStruct((8, TQ), jnp.float32)),
        in_specs=[SMEM] * 3
        + [VMEM] * (3 + chips + 3 + len(sums)),
        out_specs=(VMEM,) * (2 + chips),
        scratch_shapes=[
            pltpu.VMEM((blocks, seq_count, span_len, HD), jnp.bfloat16),
            pltpu.VMEM((blocks, seq_count, span_len, HD), jnp.bfloat16),
            pltpu.VMEM((blocks, seq_count, span_len // KT, AUG, KT), jnp.bfloat16),
            pltpu.VMEM((blocks, seq_count, span_len, HD), jnp.float32),
            pltpu.VMEM((blocks, seq_count, span_len, HD), jnp.float32),
            pltpu.VMEM((AUG, TQ), jnp.float32),
        ],
        cost_estimate=pl.CostEstimate(flops=1, transcendentals=0, bytes_accessed=1),
        compiler_params=pltpu.CompilerParams(vmem_limit_bytes=56 * 2**20),
    )(base, edges, far_bias, g, o, lse, *kvs, starts, ends, bias, *sums)
    return made[0], made[1:chips], made[-2:]


def trade(block, axis, bit):
    size = lax.axis_size(axis)
    return lax.ppermute(block, axis, [(i, i ^ bit) for i in range(size)])


def mate(block):
    return trade(block, "blk", 1)


def across_x(block):
    return trade(block, "blk", 2)


def across_y(block):
    return trade(block, "head", 1)


def across_z(block, distance):
    return trade(block, "head", 2 * distance)


def copy_kernel(plan, slots_ref, *arrays):
    for source, source_rows, target, target_rows, count in plan:
        views = []
        for which, (slot, scale, first, columns) in ((source, source_rows), (target, target_rows)):
            begin = first if slot is None else pl.multiple_of(slots_ref[slot] * scale, 8) + first
            views.append(arrays[which].at[pl.ds(begin, count), pl.ds(columns[0], columns[1])])
        views[1][...] = views[0][...]


def moved(name, slots, sources, shapes, plan):
    outs = tuple(jax.ShapeDtypeStruct(shape, sources[0].dtype) for shape in shapes)
    return pl.pallas_call(
        functools.partial(copy_kernel, plan),
        name=name,
        out_shape=outs,
        in_specs=[SMEM] + [VMEM] * len(sources),
        out_specs=(VMEM,) * len(outs),
        compiler_params=pltpu.CompilerParams(vmem_limit_bytes=40 * 2**20),
    )(slots, *sources)


DEPTH = 4
CHIPS = 16


def turn_of(k):
    return k % DEPTH, k // DEPTH // 2, k // DEPTH % 2


def slot_table():
    n_blk = lax.axis_size("blk")
    group, place = lax.axis_index("head"), lax.axis_index("blk")
    groups = group ^ jnp.asarray([2 * turn_of(k)[0] + turn_of(k)[1] for k in range(CHIPS)], jnp.int32)
    sides = (place // 2) ^ jnp.asarray([turn_of(k)[2] for k in range(CHIPS)], jnp.int32)
    chips = groups * (n_blk // 2) + sides
    return jnp.concatenate([chips, groups, 2 * chips + place % 2, 2 * chips + 1 - place % 2])


CHIP, GROUP, DEVICE, MATE = 0, CHIPS, 2 * CHIPS, 3 * CHIPS


def after(block, *earlier):
    return lax.optimization_barrier((block, earlier))[0]


def beside(made, *sent):
    return lax.optimization_barrier((made, *sent))


def wide(block):
    return block.astype(jnp.float32)


def placed(name, slots, blocks, layout, shapes, order):
    plan = []
    for k, (which, at) in enumerate(order):
        for first, count, whole, take, target in layout:
            plan.append((which, (None, 0, at + first, take), len(blocks) + whole, target(k), count))
    return moved(name, slots, blocks, shapes, tuple(plan))


def parted(name, slots, wholes, layout, shapes, order):
    plan = []
    for k, (which, at) in enumerate(order):
        for first, count, whole, take, target in layout:
            plan.append((whole, target(k), len(wholes) + which, (None, 0, at + first, take), count))
    return moved(name, slots, wholes, shapes, tuple(plan))


def grouped(rows):
    order = []
    for k in range(CHIPS):
        group, z = k // DEPTH, k % DEPTH
        order.append((group, z * rows) if group < 3 else (3 + z // 2, z % 2 * rows))
    return order


def gather_z(payload, *earlier):
    payload = after(payload, *earlier) if earlier else payload
    return [payload] + [across_z(payload, k) for k in range(1, DEPTH)]


def gather_xy(own, *earlier):
    own = jnp.concatenate(own, axis=0)
    own = after(own, *earlier) if earlier else own
    return own, across_x(own), across_y(own)


def gather_corner(blocks, *earlier):
    own, by_x, by_y = blocks
    half = own.shape[0] // 2
    low, high = by_x[:half], by_y[half:]
    if earlier:
        low, high = after(low, *earlier), after(high, *earlier)
    return own, by_x, by_y, across_y(low), across_x(high)


def sum_parts(name, slots, wholes, layout, rows, width):
    full, half = DEPTH * rows, DEPTH // 2 * rows
    shapes = ((full, width),) * 3 + ((half, width),) * 2
    return parted(name, slots, wholes, layout, shapes, grouped(rows))


def sum_corner(blocks):
    own, by_x, by_y, low, high = blocks
    return own, by_x, by_y, across_y(low), across_x(high)


def sum_xy(blocks):
    own, by_x, by_y, low, high = blocks
    half = low.shape[0]
    return own, across_x(added(by_x, low, slice(0, half))), across_y(added(by_y, high, slice(half, 2 * half)))


def column_kernel(firsts, own_ref, *refs):
    rows = own_ref.shape[0] // DEPTH
    parts, outs = refs[:-DEPTH], refs[-DEPTH:]
    for k, out_ref in enumerate(outs):
        total = wide(own_ref[k * rows : (k + 1) * rows])
        for first, part_ref in zip(firsts, parts):
            at = k * rows - first
            if 0 <= at < part_ref.shape[0]:
                total = total + wide(part_ref[at : at + rows])
        out_ref[...] = total.astype(out_ref.dtype)


def column_sent(blocks):
    rows, width = blocks[0].shape[0] // DEPTH, blocks[0].shape[1]
    firsts, at = [], 0
    for block in blocks[1:]:
        firsts.append(at % (DEPTH * rows))
        at += block.shape[0]
    here, *given = pl.pallas_call(
        functools.partial(column_kernel, tuple(firsts)),
        name="column",
        out_shape=[jax.ShapeDtypeStruct((rows, width), jnp.float32)]
        + [jax.ShapeDtypeStruct((rows, width), jnp.bfloat16)] * (DEPTH - 1),
        in_specs=[VMEM] * len(blocks),
        out_specs=[VMEM] * DEPTH,
        compiler_params=pltpu.CompilerParams(vmem_limit_bytes=32 * 2**20),
    )(*blocks)
    return [here] + [across_z(block, k + 1) for k, block in enumerate(given)]


def column_total(blocks):
    here, *met = blocks
    return here + sum(wide(block) for block in met)


def norm_kernel(here_ref, there_ref, gain_ref, rows_ref, scale_ref, *normed_refs):
    seqs, part, _ = here_ref.shape
    for seq in range(seqs):
        for which, ref in enumerate((here_ref, there_ref)):
            rows = wide(ref[seq])
            scale = lax.rsqrt(jnp.mean(rows * rows, axis=-1, keepdims=True) + EPS)
            normed = (rows * scale * gain_ref[...]).astype(here_ref.dtype)
            normed_refs[seq][which * part : (which + 1) * part, :] = normed
            if which == 0:
                rows_ref[seq * part : (seq + 1) * part, :] = rows
                scale_ref[seq * part : (seq + 1) * part, :] = scale


def normed_by_seq(here, there, gain):
    seqs, part, width = here.shape
    shapes = [(seqs * part, width), (seqs * part, 1)]
    return pl.pallas_call(
        norm_kernel,
        name="normed_by_seq",
        out_shape=[jax.ShapeDtypeStruct(shape, jnp.float32) for shape in shapes]
        + [jax.ShapeDtypeStruct((2 * part, width), here.dtype)] * seqs,
        in_specs=[VMEM] * 3,
        out_specs=[VMEM] * (2 + seqs),
    )(here, there, gain.reshape(1, width))


def feed_kernel(rows_ref, grad_ref, in_ref, down_ref, act_ref, up_ref, out_near, out_far, back_near, back_far):
    half = rows_ref.shape[0] // 2
    hidden, step = in_ref.shape[1], 512
    made = back = None
    for at in range(0, hidden, step):
        here = slice(at, at + step)
        values, rise = gelu_both(nn(rows_ref[...], in_ref[:, here]))
        values = values.astype(act_ref.dtype)
        act_ref[:, here] = values
        up = (dot_on(grad_ref[...], down_ref[here, :], 1, 1) * rise).astype(up_ref.dtype)
        up_ref[:, here] = up
        part, part_back = nn(values, down_ref[here, :]), dot_on(up, in_ref[:, here], 1, 1)
        made = part if made is None else made + part
        back = part_back if back is None else back + part_back
    out_near[...], out_far[...] = made[:half], made[half:]
    back_near[...], back_far[...] = back[:half], back[half:]


def feed(rows, grads, in_w, down_w):
    tokens, width = rows.shape
    hidden = jax.ShapeDtypeStruct((tokens, in_w.shape[1]), rows.dtype)
    half = jax.ShapeDtypeStruct((tokens // 2, width), jnp.float32)
    return pl.pallas_call(
        feed_kernel,
        name="feed",
        out_shape=[hidden] * 2 + [half] * 4,
        in_specs=[VMEM] * 4,
        out_specs=[VMEM] * 6,
        cost_estimate=pl.CostEstimate(flops=1, transcendentals=0, bytes_accessed=1),
        compiler_params=pltpu.CompilerParams(vmem_limit_bytes=48 * 2**20),
    )(rows, grads, in_w, down_w)


def first_back_kernel(plan, slots_ref, in_0, made_0, in_1, made_1, *refs):
    *parts, whole_ref = refs
    rows = whole_ref.shape[0]
    step = 256
    for at in range(0, rows, step):
        here = slice(at, at + step)
        product = dot_on(in_0[here], made_0[...], 1, 1) + dot_on(in_1[here], made_1[...], 1, 1)
        whole_ref[here, :] = product.astype(whole_ref.dtype)
    for slot, scale, which, at in plan:
        source = pl.ds(pl.multiple_of(slots_ref[slot] * scale, scale), scale)
        parts[which][at : at + scale, :] = whole_ref[source, :]


def first_back(slots, plan, shapes, ins, made):
    return pl.pallas_call(
        functools.partial(first_back_kernel, plan),
        name="first_back",
        out_shape=[jax.ShapeDtypeStruct(shape, made[0].dtype) for shape in shapes],
        in_specs=[SMEM] + [VMEM] * 4,
        out_specs=[VMEM] * len(shapes),
        scratch_shapes=[pltpu.VMEM((ins[0].shape[0], made[0].shape[0]), made[0].dtype)],
        compiler_params=pltpu.CompilerParams(vmem_limit_bytes=48 * 2**20),
    )(slots, ins[0], made[0], ins[1], made[1])


def last_kernel(first_ref, second_ref, wq_ref, wk_ref, wv_ref, q_ref, k_ref, v_ref, gain_ref):
    groups = first_ref.shape[1] // (3 * HD)
    for g in range(groups):
        for which, out_ref in enumerate((q_ref, k_ref, v_ref)):
            at = (3 * g + which) * HD
            pair = [ref[:, at : at + HD] for ref in (first_ref, second_ref)]
            out_ref[:, 2 * g * HD : 2 * (g + 1) * HD] = jnp.concatenate(pair, axis=1)
    products = sum(wide(w[...]) * grad[...] for w, grad in ((wq_ref, q_ref), (wk_ref, k_ref), (wv_ref, v_ref)))
    gain_ref[...] = jnp.sum(products, axis=1, keepdims=True)


def by_weight(first, second, *weights):
    rows, width = weights[0].shape
    return pl.pallas_call(
        last_kernel,
        name="by_weight",
        out_shape=[jax.ShapeDtypeStruct((rows, width), jnp.float32)] * 3 + [jax.ShapeDtypeStruct((rows, 1), jnp.float32)],
        in_specs=[VMEM] * 5,
        out_specs=[VMEM] * 4,
    )(first, second, *weights)


def halves_kernel(place_ref, in_ref, out_ref, down_ref, in_w_ref, out_w_ref, down_w_ref):
    devices, rows, width = out_ref.shape
    for d in range(devices):
        here = pl.ds(d * rows, rows)
        for j in range(in_ref.shape[1] // rows):
            in_w_ref[here, j * width : (j + 1) * width] = in_ref[d, j * rows : (j + 1) * rows, :]
        out_w_ref[here, :] = out_ref[d]
    chips, _, rows, _ = down_ref.shape
    for chip in range(chips):
        down_w_ref[pl.ds(chip * rows, rows), :] = down_ref[chip, 0]


def own_halves(core, whole, down_rows, shard):
    devices, rows, width = whole.shape
    steps, chips = 4, devices // 2
    in_rows = (rows - down_rows - shard) // 2
    in_at, out_at = down_rows // in_rows, (rows - shard) // shard
    shapes = (
        (devices * shard, in_rows // shard * width),
        (devices * shard, width),
        (chips * down_rows, width),
    )
    return pl.pallas_call(
        halves_kernel,
        name="own_halves",
        grid_spec=pltpu.PrefetchScalarGridSpec(
            num_scalar_prefetch=1,
            grid=(steps,),
            in_specs=[
                pl.BlockSpec((devices // steps, in_rows, width), lambda i, place_ref: (i, in_at + place_ref[0], 0)),
                pl.BlockSpec((devices // steps, shard, width), lambda i, place_ref: (i, out_at, 0)),
                pl.BlockSpec((chips // steps, 1, down_rows, width), lambda i, place_ref: (i, place_ref[0], 0, 0)),
            ],
            out_specs=[pl.BlockSpec((shape[0] // steps, shape[1]), lambda i, place_ref: (i, 0)) for shape in shapes],
        ),
        out_shape=[jax.ShapeDtypeStruct(shape, whole.dtype) for shape in shapes],
        compiler_params=pltpu.CompilerParams(vmem_limit_bytes=32 * 2**20),
    )(core.reshape(1), whole, whole, whole.reshape(chips, 2, rows, width))


def add_kernel(place, whole_ref, part_ref, sum_ref):
    sum_ref[...] = whole_ref[...]
    sum_ref[place] = (wide(whole_ref[place]) + wide(part_ref[...])).astype(sum_ref.dtype)


def added(whole, part, place):
    return pl.pallas_call(
        functools.partial(add_kernel, place),
        name="added",
        out_shape=jax.ShapeDtypeStruct(whole.shape, whole.dtype),
        in_specs=[VMEM] * 2,
        out_specs=VMEM,
        compiler_params=pltpu.CompilerParams(vmem_limit_bytes=32 * 2**20),
    )(whole, part)


def document_bounds(segments):
    seq_count, blocks, span_len = segments.shape
    length = blocks * span_len
    numbers = lax.iota(jnp.int32, length // min(512, length) + 2)
    flat = segments.reshape(seq_count, length)
    below = jnp.sum((flat[:, :, None] < numbers).astype(jnp.int32), axis=1)
    here = flat[:, :, None] == numbers[:-1]
    starts = jnp.sum(jnp.where(here, below[:, None, :-1], 0), axis=2)
    ends = jnp.sum(jnp.where(here, below[:, None, 1:], 0), axis=2)
    return starts.reshape(segments.shape), ends.reshape(segments.shape)


def query_bounds(bounds, place, tile):
    near = [lax.dynamic_index_in_dim(bounds, place ^ k, 1, keepdims=False) for k in (0, 2)]
    near = jnp.stack(near, axis=0)
    return near.reshape(near.shape[0], near.shape[1], -1, tile)


def gelu_both(values):
    slope = float(np.sqrt(2.0 / np.pi))
    square = values * values
    curve = jnp.tanh(slope * values * (1.0 + 0.044715 * square))
    half = 0.5 * (1.0 + curve)
    rise = half + 0.5 * values * (1.0 - curve * curve) * (slope * (1.0 + 3 * 0.044715 * square))
    return values * half, rise


def joined(block):
    return jnp.concatenate([block, mate(block)], axis=0)


def halves_added(block):
    half = block.shape[0] // 2
    return block[:half] + mate(block[half:])


def norm_back(grad, rows, scale, gain):
    weighted = grad * gain
    inner = jnp.mean(rows * weighted, axis=-1, keepdims=True)
    return scale * weighted - rows * (scale * scale * scale) * inner


def dot_on(left, right, left_dim, right_dim):
    return lax.dot_general(left, right, (((left_dim,), (right_dim,)), ((), ())), preferred_element_type=jnp.float32)


def pair_body(
    inputs,
    segments,
    bucket_table,
    norm_gain,
    w_query,
    w_key,
    w_value,
    w_out,
    rel_bias,
    ff_gain,
    w_in,
    w_down,
    cotangent,
):
    low = jnp.bfloat16
    seq_count, _, part_len, width = inputs.shape
    groups = lax.axis_size("head")
    span_len = part_len * groups
    blocks = lax.axis_size("blk")
    group, place = lax.axis_index("head"), lax.axis_index("blk")
    core, side = place % 2, place // 2
    slots = slot_table()
    shard = w_query.shape[0]
    chip_rows = 2 * shard
    head_cols = 3 * HD
    first_cols = groups * head_cols
    half_width = groups * HD
    half_hidden = w_in.shape[1] // 2
    down_rows = w_down.shape[0]
    tokens = seq_count * part_len

    def by_core(first, second):
        return jnp.where(core == 0, first, second)

    def by_side(first, second):
        return jnp.where(side == 0, first, second)

    cores = [[g * blocks + 2 * s + c for g in range(groups) for s in range(blocks // 2)] for c in range(2)]

    def exchanged_all(block):
        return lax.all_to_all(block, ("head", "blk"), split_axis=0, concat_axis=0, tiled=True, axis_index_groups=cores)

    def exchanged(block):
        return lax.all_to_all(block, "head", split_axis=0, concat_axis=0, tiled=True)

    every, first_every = (0, width), (0, first_cols)
    gains = jnp.concatenate([norm_gain, ff_gain, rel_bias, jnp.zeros((128 - 5 * shard // 2,), low)])
    gains = jnp.broadcast_to(jnp.pad(gains[None, :], ((0, 7), (0, 0))), (2 * CHIPS, 8, 128))
    gain_w = lax.all_to_all(gains, ("head", "blk"), split_axis=0, concat_axis=0, tiled=True)
    gain_w = wide(gain_w[:, 0])
    gain_one = gain_w[:, :shard].reshape(-1)
    gain_two = gain_w[:, shard : 2 * shard].reshape(-1)

    input_rows = inputs.reshape(seq_count, part_len, width)
    token_rows, scale_one, *first_in = normed_by_seq(input_rows, across_x(input_rows), gain_one)

    def head_columns(weight, which):
        return weight.reshape(shard, groups, 2, HD)[:, :, which]

    def cut(which):
        return jnp.stack([head_columns(w, which) for w in (w_query, w_key, w_value)], axis=2).reshape(shard, -1)

    first_cut, second_cut = cut(0), cut(1)
    chunks = [by_side(first_cut, second_cut), across_x(by_side(second_cut, first_cut))]
    first_blocks = []
    for at, chunk in enumerate(chunks):
        own = jnp.concatenate(gather_z(chunk), axis=0)
        if at == 0:
            own, chunks[1] = beside(own, chunks[1])
        by_y = across_y(own)
        if at == 1:
            by_y, first_in = beside(by_y, first_in)
        both = jnp.concatenate([own, by_y], axis=0)
        first_blocks += [both, mate(both)]
    plan = []
    for k in range(CHIPS):
        z, y, x = turn_of(k)
        for far, slot in enumerate((DEVICE, MATE)):
            source = (None, 0, (DEPTH * y + z) * shard, first_every)
            plan.append((2 * x + far, source, 4, (slot + k, shard, 0, first_every), shard))
    (first_w,) = moved("whole_first", slots, first_blocks, ((width, first_cols),), tuple(plan))

    def hidden_columns(which):
        return w_in.reshape(shard, -1, 2, down_rows)[:, :, which].reshape(shard, -1, width)

    payload_in = jnp.stack([hidden_columns(0), hidden_columns(1)], axis=0).transpose(0, 2, 1, 3).reshape(-1, width)
    in_rows = 2 * chip_rows + shard
    payload = jnp.concatenate([w_down, payload_in, w_out], axis=0)
    whole = lax.all_gather(payload, ("head", "blk"), axis=0, tiled=False)

    lay_in = (
        (0, chip_rows, 0, every, lambda k: (CHIP + k, chip_rows, 0, (0, width))),
        (chip_rows, chip_rows, 0, every, lambda k: (CHIP + k, chip_rows, 0, (width, width))),
        (2 * chip_rows, shard, 1, every, lambda k: (CHIP + k, shard, 0, every)),
    )
    lay_down = ((0, down_rows, 0, every, lambda k: (CHIP + k, down_rows, 0, every)),)

    rel_table = gain_w[:, 2 * shard : 5 * shard // 2].reshape(HEADS, BUCKETS)
    rel_here = lax.dynamic_index_in_dim(rel_table, 2 * group + side, 0, keepdims=False)

    bucket_hot = bucket_table[:, None] == lax.iota(jnp.int32, BUCKETS)[None, :]
    by_offset = jnp.sum(jnp.where(bucket_hot, rel_here[None, :], 0.0), axis=1)
    places = strip_places()
    place_hot = jnp.asarray(places.reshape(-1))[:, None] == lax.iota(jnp.int32, 2 * MAXREL + 1)[None, :]
    place_hot = place_hot.astype(jnp.float32)
    waves = jnp.dot(place_hot, by_offset, precision=lax.Precision.HIGHEST)
    waves = waves.reshape(places.shape[0], 1, places.shape[1])
    far_bias = jnp.stack([by_offset[0], by_offset[-1]])
    bias = bias_strip(far_bias, waves)
    starts, ends = document_bounds(segments)
    starts, ends = query_bounds(starts, place, TQ), query_bounds(ends, place, TQ)
    edges = jnp.stack([starts[..., 0], starts[..., -1], ends[..., 0], ends[..., -1]], axis=-1)
    base = (place ^ jnp.asarray([0, 2, 1, 3], jnp.int32)) * span_len
    base = jnp.concatenate([base, side.reshape(1)])

    made = [dot_on(first_w, rows, 0, 1).astype(low) for rows in first_in]
    sent = exchanged(made[0].reshape(groups, head_cols, 2 * part_len))
    sent, bias, far_bias, starts, ends, edges = beside(sent, bias, far_bias, starts, ends, edges)
    bounds = [(starts[:, seq : seq + 1], ends[:, seq : seq + 1], bias) for seq in range(seq_count)]
    edges = [edges[:, seq].reshape(-1) for seq in range(seq_count)]
    attended, heads, attn_cols = [], [], [None] * seq_count
    for seq in range(seq_count):
        heads.append([sent, mate(sent)])
        if seq + 1 < seq_count:
            heads[seq][1], made[seq + 1] = beside(heads[seq][1], made[seq + 1])
        done = attend(base, edges[seq], far_bias, heads[seq], *bounds[seq])
        if seq + 1 < seq_count:
            done, sent = beside(done, exchanged(made[seq + 1].reshape(groups, head_cols, 2 * part_len)))
        else:
            done, attn_cols[seq - 1] = beside(done, attn_cols[seq - 1])
        attended.append(done)
        attn_cols[seq] = exchanged_all(done[1])
    attn_cols[1], in_w, out_w, down_w = beside(attn_cols[1], *own_halves(core, whole, down_rows, shard))
    attn_cols = jnp.concatenate([block.reshape(2 * half_width, part_len) for block in attn_cols], axis=1)
    hidden_one = token_rows + dot_on(attn_cols, out_w, 0, 0)
    scale_two = lax.rsqrt(jnp.mean(hidden_one * hidden_one, axis=-1, keepdims=True) + EPS)
    second_in = joined((hidden_one * scale_two * gain_two).astype(low))
    incoming_low = cotangent.reshape(tokens, width)
    incoming = joined(incoming_low)
    activated, up_grad, layer_near, layer_far, back_near, back_far = feed(second_in, incoming, in_w, down_w)
    whole_down = dot_on(activated, incoming, 0, 0).astype(low)
    down_parts = sum_parts("parts_down", slots, (whole_down,), lay_down, down_rows, width)
    second_grad, down_parts = beside(back_near + mate(back_far), down_parts)
    down_parts = sum_corner(down_parts)
    hidden_part = norm_back(second_grad, hidden_one, scale_two, gain_two)
    hidden_grad = wide(incoming_low) + hidden_part
    branch = hidden_grad.astype(low)
    grads = dot_on(out_w, branch, 1, 1).astype(low).reshape(HEADS, HD, tokens)
    late_in, late_branch = after((second_in, branch), grads)
    whole_in = dot_on(late_in, up_grad, 0, 0).astype(low)
    whole_out = dot_on(attn_cols, late_branch, 1, 0).astype(low).reshape(-1, 2, shard, width)
    out_mine, out_given = by_core(whole_out[:, 0], whole_out[:, 1]), by_core(whole_out[:, 1], whole_out[:, 0])
    whole_out = (wide(out_mine) + wide(mate(out_given))).astype(low).reshape(half_width, width)
    in_parts = sum_parts("parts_in", slots, (whole_in, whole_out), lay_in, in_rows, width)
    grads, in_parts, down_parts = beside(exchanged_all(grads), in_parts, down_parts)
    in_parts = sum_corner(in_parts)
    down_parts = sum_xy(down_parts)

    def offset_grads(band, sides, earlier):
        near_sums, far_sums = band_sums_of(after(band, *earlier), sides)
        offset_sums = jnp.dot(near_sums.reshape(-1), place_hot, precision=lax.Precision.HIGHEST)
        far_sums = jnp.sum(far_sums, axis=1)
        end_hot = lax.iota(jnp.int32, 2 * MAXREL + 1)
        offset_sums = offset_sums + jnp.where(end_hot == 0, far_sums[0], 0.0)
        offset_sums = offset_sums + jnp.where(end_hot == 2 * MAXREL, far_sums[1], 0.0)
        return jnp.sum(jnp.where(bucket_hot, offset_sums[:, None], 0.0), axis=0)

    sums, made, sent = (), [], None
    for seq in range(seq_count):
        outs, _, lse = attended[seq]
        done = attend_back(base, edges[seq], far_bias, grads, seq, outs, lse, heads[seq], *bounds[seq], sums)
        if seq == 0:
            done, in_parts, down_parts = beside(done, in_parts, down_parts)
        else:
            done, in_parts, down_sent, made[0] = beside(done, in_parts, down_sent, made[0])
        near_grad, (far_grad,), sums = done
        near_grad = added(near_grad, mate(far_grad), (slice(None), slice(HD, 3 * HD)))
        if seq == 0:
            grads, near_grad = beside(grads, near_grad)
            in_parts = sum_xy(in_parts)
            down_sent = column_sent(down_parts)
        made.append(exchanged(near_grad))
    band, sides = sums
    layer_out = (hidden_one + layer_near + mate(layer_far)).astype(low).reshape(inputs.shape)
    made[1], rel_grad = beside(made[1], offset_grads(band, sides, (near_grad,)))
    made = [block.reshape(first_cols, 2 * part_len) for block in made]
    plan, column = [], 2 * DEPTH * shard
    for k in range(CHIPS):
        z, y, x = turn_of(k)
        plan.append((MATE + k, shard, 0, y * column + (2 * z + x) * shard))
        plan.append((DEVICE + k, shard, 1 + y, (2 * z + x) * shard))
    shapes = ((2 * column, first_cols), (column, first_cols), (column, first_cols))
    given, near, by_y = first_back(slots, tuple(plan), shapes, [block.T for block in first_in], made)
    in_sent = column_sent(after(in_parts, made[1]))
    got = mate(given)
    first_grads = [dot_on(block, first_w, 0, 1) for block in made]
    near_part = jnp.concatenate([grad[:part_len] for grad in first_grads], axis=0)
    far_part = jnp.concatenate([grad[part_len:] for grad in first_grads], axis=0).astype(low)
    by_y = across_y((wide(by_y) + wide(got[column:])).astype(low))
    by_y, far_part = beside(by_y, across_x(after(far_part, got)))
    first_sent = column_sent((near, got[:column], by_y))
    first_sum = column_total(first_sent)
    first_sums = [first_sum[:shard], across_x(first_sum[shard:])]
    in_sum = column_total(after(in_sent, first_sent[0]))
    grad_down = column_total(down_sent)
    first_grad = near_part + wide(far_part)
    input_part = norm_back(first_grad, token_rows, scale_one, gain_one)
    input_grad = (hidden_grad + input_part).astype(low).reshape(inputs.shape)

    grad_query, grad_key, grad_value, norm_sums = by_weight(
        by_side(*first_sums), by_side(*first_sums[::-1]), w_query, w_key, w_value
    )

    hidden_rows = jnp.concatenate([in_sum[:chip_rows], in_sum[chip_rows : 2 * chip_rows]], axis=1)
    mine = by_core(hidden_rows[:shard], hidden_rows[shard:])
    other = mate(by_core(hidden_rows[shard:], hidden_rows[:shard]))
    in_pair = [block.reshape(shard, -1, down_rows) for block in (by_core(mine, other), by_core(other, mine))]
    grad_in = jnp.stack(in_pair, axis=2).reshape(shard, -1)
    grad_out = in_sum[2 * chip_rows :]

    grad_norm_gain = norm_sums[:, 0] / wide(norm_gain)
    grad_ff_gain = jnp.sum(wide(w_in) * grad_in, axis=1) / wide(ff_gain)

    rel_grad = jnp.pad(rel_grad[None, :], ((0, 7), (0, 128 - BUCKETS)))
    rel_sum = (rel_grad + mate(rel_grad))[0]
    rel_mine = by_core(rel_sum[: BUCKETS // 2], rel_sum[BUCKETS // 2 : BUCKETS])

    return (
        layer_out,
        input_grad,
        grad_norm_gain,
        grad_query,
        grad_key,
        grad_value,
        grad_out,
        rel_mine,
        grad_ff_gain,
        grad_in,
        grad_down,
    )


def solution(mesh):
    placed = (
        P(None, "blk", "head", None),
        P(),
        P(),
        P(("head", "blk")),
        P(("head", "blk"), None),
        P(("head", "blk"), None),
        P(("head", "blk"), None),
        P(("head", "blk"), None),
        P(("head", "blk")),
        P(("head", "blk")),
        P(("head", "blk"), None),
        P(("head", "blk"), None),
        P(None, "blk", "head", None),
    )
    n_head, n_blk = mesh.shape["head"], mesh.shape["blk"]
    paired = HEADS == 2 * n_head and (n_head, n_blk) == (8, 4)
    return jax.shard_map(
        pair_body if paired else ring_body,
        mesh=mesh,
        in_specs=placed,
        out_specs=(
            P(None, "blk", "head", None),
            P(None, "blk", "head", None),
            P(("head", "blk")),
            P(("head", "blk"), None),
            P(("head", "blk"), None),
            P(("head", "blk"), None),
            P(("head", "blk"), None),
            P(("head", "blk")),
            P(("head", "blk")),
            P(("head", "blk"), None),
            P(("head", "blk"), None),
        ),
        check_vma=False,
    )
```

```python
import functools

import jax
import jax.numpy as jnp
import numpy as np
from jax import lax
from jax.experimental import pallas as pl
from jax.experimental.pallas import tpu as pltpu
from jax.sharding import PartitionSpec as P

HEADS = 16
HD = 64
BUCKETS = 32
MAXREL = 128
EPS = 1e-06
FLOOR = -1e30


def from_behind(block, axis, distance):
    devices = range(lax.axis_size(axis))
    route = [((i - distance) % len(devices), i) for i in devices]
    return lax.ppermute(block, axis, route)


def rms_scale(token_rows, gain_vector):
    return (
        token_rows
        * lax.rsqrt(jnp.mean(token_rows * token_rows, axis=-1, keepdims=True) + EPS)
        * gain_vector
    )


def smooth(values):
    return jax.nn.gelu(values, approximate=True)


def band_layout(span_len):
    tile_side = min(128, span_len)
    reach = MAXREL // tile_side + 2
    return (tile_side, span_len // tile_side, reach)


def band_tables(bucket_table, rel_here, span_len):
    tile_side, _, reach = band_layout(span_len)
    kinds = 2 * reach + 1
    gaps = lax.iota(jnp.int32, kinds) - reach
    rows_in = lax.iota(jnp.int32, tile_side)
    offsets = gaps[:, None, None] * tile_side + rows_in[None, None, :] - rows_in[None, :, None]
    lookup = jnp.clip(offsets, -MAXREL, MAXREL) + MAXREL
    bucket = jnp.take(bucket_table, lookup.reshape(-1), axis=0)
    onehot = (bucket[:, None] == lax.iota(jnp.int32, BUCKETS)[None, :]).astype(jnp.float32)
    band_bias = jnp.dot(rel_here, onehot.T, precision=lax.Precision.HIGHEST)
    return (band_bias.reshape(rel_here.shape[0], kinds, tile_side, tile_side), onehot)


def band_index(block_gap, span_len):
    _, tiles, reach = band_layout(span_len)
    row_tile = lax.iota(jnp.int32, tiles)[:, None, None, None]
    col_tile = lax.iota(jnp.int32, tiles)[None, None, :, None]
    return jnp.clip(block_gap * tiles + col_tile - row_tile, -reach, reach) + reach


def bias_tile(band_bias, block_gap, span_len):
    heads_count, kinds, tile_side, _ = band_bias.shape
    tiles = span_len // tile_side
    which = band_index(block_gap, span_len)
    result = jnp.zeros((heads_count, tiles, tile_side, tiles, tile_side), jnp.float32)
    for kind in range(kinds):
        result = jnp.where(which[None] == kind, band_bias[:, kind][:, None, :, None, :], result)
    return result.reshape(heads_count, span_len, span_len)


def band_sums(tile_sum, block_gap, span_len):
    tile_side, tiles, reach = band_layout(span_len)
    heads_count = tile_sum.shape[0]
    split_sum = tile_sum.reshape(heads_count, tiles, tile_side, tiles, tile_side)
    which = band_index(block_gap, span_len)
    parts = []
    for kind in range(2 * reach + 1):
        parts.append(jnp.sum(jnp.where(which[None] == kind, split_sum, 0.0), axis=(1, 3)))
    return jnp.stack(parts, axis=1).reshape(heads_count, -1)


def pass_grads(key_grad, value_grad):
    return (
        from_behind(key_grad.astype(jnp.bfloat16), "blk", 1).astype(key_grad.dtype),
        from_behind(value_grad.astype(jnp.bfloat16), "blk", 1).astype(value_grad.dtype),
    )


def ring_body(
    inputs,
    segments,
    bucket_table,
    norm_gain,
    w_query,
    w_key,
    w_value,
    w_out,
    rel_bias,
    ff_gain,
    w_in,
    w_down,
    cotangent,
):
    seq_count, _, part_len, width = inputs.shape
    cycle_size = lax.axis_size("blk")
    head_groups = lax.axis_size("head")
    heads_here = HEADS // head_groups
    span_len = part_len * head_groups
    cycle_place = lax.axis_index("blk")
    head_place = lax.axis_index("head")
    gathered = (
        lax.all_gather(norm_gain, ("head", "blk"), axis=0, tiled=True),
        lax.all_gather(w_query, ("head", "blk"), axis=0, tiled=True),
        lax.all_gather(w_key, ("head", "blk"), axis=0, tiled=True),
        lax.all_gather(w_value, ("head", "blk"), axis=0, tiled=True),
        lax.all_gather(w_out, ("head", "blk"), axis=0, tiled=True),
        lax.all_gather(rel_bias, ("head", "blk"), axis=0, tiled=True),
        lax.all_gather(ff_gain, ("head", "blk"), axis=0, tiled=True),
        lax.all_gather(w_in, ("head", "blk"), axis=0, tiled=True),
        lax.all_gather(w_down, ("head", "blk"), axis=0, tiled=True),
    )
    gain_one, query_w, key_w, value_w, out_w, rel_flat, gain_two, in_w, down_w = gathered
    token_rows = inputs.reshape(-1, width).astype(jnp.float32)
    normed, norm_one_back = jax.vjp(rms_scale, token_rows, gain_one.astype(jnp.float32))
    first_in = normed.astype(jnp.bfloat16)

    def project(weight):
        made_rows = jnp.dot(first_in, weight, preferred_element_type=jnp.float32)
        return made_rows.astype(jnp.bfloat16).reshape(seq_count, part_len, -1)

    queries, keys_home, values_home = (
        lax.all_to_all(project(query_w), "head", split_axis=2, concat_axis=1, tiled=True),
        lax.all_to_all(project(key_w), "head", split_axis=2, concat_axis=1, tiled=True),
        lax.all_to_all(project(value_w), "head", split_axis=2, concat_axis=1, tiled=True),
    )
    head_shape = (seq_count, span_len, heads_here, HD)
    queries = queries.reshape(head_shape)
    keys_home = keys_home.reshape(head_shape)
    values_home = values_home.reshape(head_shape)
    rel_table = rel_flat.astype(jnp.float32).reshape(HEADS, BUCKETS)
    rel_here = lax.dynamic_slice_in_dim(rel_table, head_place * heads_here, heads_here, 0)
    band_bias, band_onehot = band_tables(bucket_table, rel_here, span_len)

    def tile_scores(query_rows, key_rows, query_block, key_block):
        query_ids = lax.dynamic_index_in_dim(segments, query_block, 1, keepdims=False)
        key_ids = lax.dynamic_index_in_dim(segments, key_block, 1, keepdims=False)
        plain_scores = (
            jnp.einsum("sihd,sjhd->shij", query_rows, key_rows, preferred_element_type=jnp.float32)
            + bias_tile(band_bias, key_block - query_block, span_len)[None]
        )
        same_doc = query_ids[:, None, :, None] == key_ids[:, None, None, :]
        return jnp.where(same_doc, plain_scores, FLOOR)

    first_scores = tile_scores(queries, keys_home, cycle_place, cycle_place)
    row_max = jnp.max(first_scores, axis=-1)
    first_weights = jnp.exp(first_scores - row_max[..., None])
    row_total = jnp.sum(first_weights, axis=-1)
    summed = jnp.einsum(
        "shij,sjhd->sihd",
        first_weights.astype(jnp.bfloat16),
        values_home,
        preferred_element_type=jnp.float32,
    )

    def forward_turn(cycle_turn, state_now):
        old_max, old_total, old_summed, key_rows, value_rows = state_now
        key_rows, value_rows = from_behind((key_rows, value_rows), "blk", 1)
        source = (cycle_place - cycle_turn) % cycle_size
        scores = tile_scores(queries, key_rows, cycle_place, source)
        new_max = jnp.maximum(old_max, jnp.max(scores, axis=-1))
        shrink = jnp.exp(old_max - new_max)
        weights_now = jnp.exp(scores - new_max[..., None])
        new_total = old_total * shrink + jnp.sum(weights_now, axis=-1)
        new_summed = old_summed * jnp.transpose(shrink, (0, 2, 1))[..., None] + jnp.einsum(
            "shij,sjhd->sihd",
            weights_now.astype(jnp.bfloat16),
            value_rows,
            preferred_element_type=jnp.float32,
        )
        return (new_max, new_total, new_summed, key_rows, value_rows)

    row_max, row_total, summed, _, _ = lax.fori_loop(
        1, cycle_size, forward_turn, (row_max, row_total, summed, keys_home, values_home)
    )
    log_total = row_max + jnp.log(row_total)
    attended = summed / jnp.transpose(row_total, (0, 2, 1))[..., None]
    attended_low = attended.astype(jnp.bfloat16).reshape(seq_count, span_len, heads_here * HD)
    attn_rows = lax.all_to_all(
        attended_low, "head", split_axis=1, concat_axis=2, tiled=True
    ).reshape(-1, HEADS * HD)
    hidden_one = token_rows + jnp.dot(attn_rows, out_w, preferred_element_type=jnp.float32)
    normed_two, norm_two_back = jax.vjp(rms_scale, hidden_one, gain_two.astype(jnp.float32))
    second_in = normed_two.astype(jnp.bfloat16)
    upward = jnp.dot(second_in, in_w, preferred_element_type=jnp.float32)
    activated, smooth_back = jax.vjp(smooth, upward)
    activated_low = activated.astype(jnp.bfloat16)
    layer_rows = hidden_one + jnp.dot(activated_low, down_w, preferred_element_type=jnp.float32)
    layer_out = layer_rows.astype(jnp.bfloat16).reshape(inputs.shape)
    back_query, back_key, back_value, back_out, back_in, back_down = (
        query_w,
        key_w,
        value_w,
        out_w,
        in_w,
        down_w,
    )
    incoming_low = cotangent.reshape(-1, width)
    incoming = incoming_low.astype(jnp.float32)
    grad_down = jnp.dot(activated_low.T, incoming_low, preferred_element_type=jnp.float32)
    (up_grad,) = smooth_back(jnp.dot(incoming_low, back_down.T, preferred_element_type=jnp.float32))
    up_low = up_grad.astype(jnp.bfloat16)
    grad_in = jnp.dot(second_in.T, up_low, preferred_element_type=jnp.float32)
    hidden_part, grad_gain_two = norm_two_back(
        jnp.dot(up_low, back_in.T, preferred_element_type=jnp.float32)
    )
    hidden_grad = incoming + hidden_part
    branch_low = hidden_grad.astype(jnp.bfloat16)
    grad_out = jnp.dot(attn_rows.T, branch_low, preferred_element_type=jnp.float32)
    attn_grad_low = jnp.dot(branch_low, back_out.T, preferred_element_type=jnp.float32).astype(
        jnp.bfloat16
    )
    grad_heads = lax.all_to_all(
        attn_grad_low.reshape(seq_count, part_len, HEADS * HD),
        "head",
        split_axis=2,
        concat_axis=1,
        tiled=True,
    ).reshape(head_shape)
    row_delta = jnp.transpose(
        jnp.sum(grad_heads.astype(jnp.float32) * attended, axis=-1), (0, 2, 1)
    )

    def tile_grads(
        query_rows, grad_rows, log_rows, delta_rows, key_rows, value_rows, query_block, key_block
    ):
        scores = tile_scores(query_rows, key_rows, query_block, key_block)
        probs = jnp.exp(scores - log_rows[..., None])
        value_part = jnp.einsum(
            "shij,sihd->sjhd",
            probs.astype(jnp.bfloat16),
            grad_rows,
            preferred_element_type=jnp.float32,
        )
        prob_grad = jnp.einsum(
            "sihd,sjhd->shij", grad_rows, value_rows, preferred_element_type=jnp.float32
        )
        score_low = (probs * (prob_grad - delta_rows[..., None])).astype(jnp.bfloat16)
        query_part = jnp.einsum(
            "shij,sjhd->sihd", score_low, key_rows, preferred_element_type=jnp.float32
        )
        key_part = jnp.einsum(
            "shij,sihd->sjhd", score_low, query_rows, preferred_element_type=jnp.float32
        )
        tile_sum = jnp.sum(score_low.astype(jnp.float32), axis=0)
        rel_part = jnp.dot(
            band_sums(tile_sum, key_block - query_block, span_len),
            band_onehot,
            precision=lax.Precision.HIGHEST,
        )
        return (query_part, key_part, value_part, rel_part)

    query_grad, key_grad, value_grad, rel_grad = tile_grads(
        queries, grad_heads, log_total, row_delta, keys_home, values_home, cycle_place, cycle_place
    )

    def key_turn(cycle_turn, state_now):
        key_rows, value_rows, key_sum, value_sum, query_sum, rel_sum = state_now
        key_sum, value_sum = pass_grads(key_sum, value_sum)
        key_rows, value_rows = from_behind((key_rows, value_rows), "blk", 1)
        source = (cycle_place - cycle_turn) % cycle_size
        query_part, key_part, value_part, rel_part = tile_grads(
            queries, grad_heads, log_total, row_delta, key_rows, value_rows, cycle_place, source
        )
        return (
            key_rows,
            value_rows,
            key_sum + key_part,
            value_sum + value_part,
            query_sum + query_part,
            rel_sum + rel_part,
        )

    state_first = (keys_home, values_home, key_grad, value_grad, query_grad, rel_grad)
    _, _, key_grad, value_grad, query_grad, rel_grad = lax.fori_loop(
        1, cycle_size, key_turn, state_first
    )
    key_grad, value_grad = pass_grads(key_grad, value_grad)
    block_shape = (seq_count, span_len, heads_here * HD)
    query_rows, key_rows_back, value_rows_back = (
        lax.all_to_all(
            query_grad.astype(jnp.bfloat16).reshape(block_shape),
            "head",
            split_axis=1,
            concat_axis=2,
            tiled=True,
        ),
        lax.all_to_all(
            key_grad.astype(jnp.bfloat16).reshape(block_shape),
            "head",
            split_axis=1,
            concat_axis=2,
            tiled=True,
        ),
        lax.all_to_all(
            value_grad.astype(jnp.bfloat16).reshape(block_shape),
            "head",
            split_axis=1,
            concat_axis=2,
            tiled=True,
        ),
    )
    query_rows = query_rows.reshape(-1, HEADS * HD)
    key_rows_back = key_rows_back.reshape(-1, HEADS * HD)
    value_rows_back = value_rows_back.reshape(-1, HEADS * HD)
    grad_query = jnp.dot(first_in.T, query_rows, preferred_element_type=jnp.float32)
    grad_key = jnp.dot(first_in.T, key_rows_back, preferred_element_type=jnp.float32)
    grad_value = jnp.dot(first_in.T, value_rows_back, preferred_element_type=jnp.float32)
    first_grad = (
        jnp.dot(query_rows, back_query.T, preferred_element_type=jnp.float32)
        + jnp.dot(key_rows_back, back_key.T, preferred_element_type=jnp.float32)
        + jnp.dot(value_rows_back, back_value.T, preferred_element_type=jnp.float32)
    )
    input_part, grad_gain_one = norm_one_back(first_grad)
    input_grad = (hidden_grad + input_part).astype(jnp.bfloat16).reshape(inputs.shape)
    rel_full = lax.dynamic_update_slice_in_dim(
        jnp.zeros((HEADS, BUCKETS), jnp.float32), rel_grad, head_place * heads_here, 0
    ).reshape(-1)
    shards = tuple(
        (
            lax.psum_scatter(grad_gain_one, ("head", "blk"), scatter_dimension=0, tiled=True),
            lax.psum_scatter(grad_query, ("head", "blk"), scatter_dimension=0, tiled=True),
            lax.psum_scatter(grad_key, ("head", "blk"), scatter_dimension=0, tiled=True),
            lax.psum_scatter(grad_value, ("head", "blk"), scatter_dimension=0, tiled=True),
            lax.psum_scatter(grad_out, ("head", "blk"), scatter_dimension=0, tiled=True),
            lax.psum_scatter(rel_full, ("head", "blk"), scatter_dimension=0, tiled=True),
            lax.psum_scatter(grad_gain_two, ("head", "blk"), scatter_dimension=0, tiled=True),
            lax.psum_scatter(grad_in, ("head", "blk"), scatter_dimension=0, tiled=True),
            lax.psum_scatter(grad_down, ("head", "blk"), scatter_dimension=0, tiled=True),
        )
    )
    return (
        layer_out,
        input_grad,
        shards[0],
        shards[1],
        shards[2],
        shards[3],
        shards[4],
        shards[5],
        shards[6],
        shards[7],
        shards[8],
    )


TQ = 512
KT = 512
MARGIN = 256
AUG = 80
NT = (((1,), (1,)), ((), ()))


def nn(left, right):
    return jnp.dot(left, right, preferred_element_type=jnp.float32)


def flipped(block):
    return block.astype(jnp.float32).T.astype(jnp.bfloat16)


def ones_row(width):
    first = lax.broadcasted_iota(jnp.int32, (AUG - HD, width), 0) == 0
    return jnp.where(first, 1.0, 0.0).astype(jnp.bfloat16)


def pieces_of(seq_count, part_len, groups):
    for seq in range(seq_count):
        for near in range(2):
            for source in range(groups):
                yield seq, near, source, slice((near * seq_count + seq) * part_len, (near * seq_count + seq + 1) * part_len)


def lanes_of(ref, tile_at, per_tile, part_len, lane_base):
    parts = [ref[tile_at * per_tile + k, :HD, pl.ds(lane_base, part_len)] for k in range(per_tile)]
    return parts[0] if per_tile == 1 else jnp.concatenate(parts, axis=1)


def tile_class(edge_ref, row, key_at, query_at):
    first_start, last_start, first_end, last_end = (edge_ref[row * 4 + k] for k in range(4))
    touched = (key_at + KT > first_start) & (key_at < last_end)
    gap = key_at - query_at
    whole = (key_at >= last_start) & (key_at + KT <= first_end)
    plain = whole & ((gap + KT <= -MAXREL + 1) | (gap >= TQ + MAXREL - 1))
    strip_at = jnp.clip(gap, -(KT + MARGIN), TQ + MARGIN) + KT + MARGIN
    return touched, plain, gap, pl.ds(pl.multiple_of(strip_at, 256), KT)


def masked(scores, bias, key_at, start_row, end_row):
    places = lax.broadcasted_iota(jnp.int32, scores.shape, 0) + key_at
    return jnp.where((places >= start_row) & (places < end_row), scores + bias, FLOOR)


def attend_kernel(chips, base_ref, edge_ref, far_ref, *refs):
    kv_refs, q_ref = refs[:chips], refs[0]
    start_ref, end_ref, bias_ref, o_ref, ob_ref, lse_ref, k_rows, v_aug, top_ref, acc_ref = refs[chips:]
    groups, _, span = q_ref.shape
    blocks, seq_count, span_len, _ = k_rows.shape
    part_len = span_len // groups
    per_tile = TQ // part_len
    tiles, key_tiles = span_len // TQ, span_len // KT
    per_key = KT // part_len
    for far in range(chips):
        for seq, near, source, lanes in pieces_of(seq_count, part_len, groups):
            block = 2 * far + near
            k_rows[block, seq, source * part_len : (source + 1) * part_len, :] = flipped(kv_refs[far][source, HD : 2 * HD, lanes])
            at = source % per_key * part_len
            v_aug[block, seq, source // per_key, :HD, at : at + part_len] = kv_refs[far][source, 2 * HD :, lanes]
    for block in range(blocks):
        for seq in range(seq_count):
            for tile in range(key_tiles):
                v_aug[block, seq, tile, HD:, :] = ones_row(KT)

    for seq in range(seq_count):
        for near in range(2):
            lane_base = (near * seq_count + seq) * part_len

            def query_tile(tile, _, seq=seq, near=near, lane_base=lane_base):
                query_at = base_ref[near] + tile * TQ
                row = (near * seq_count + seq) * tiles + tile
                queries = lanes_of(q_ref, tile, per_tile, part_len, lane_base)
                top_ref[...] = jnp.full_like(top_ref, FLOOR)
                acc_ref[...] = jnp.zeros_like(acc_ref)
                start_row = start_ref[near, seq, pl.ds(tile, 1), :]
                end_row = end_ref[near, seq, pl.ds(tile, 1), :]

                def take(scores, shift, block, key_tile):
                    old_top = top_ref[0:1, :]
                    new_top = jnp.maximum(old_top, jnp.max(scores, axis=0, keepdims=True) + shift)
                    weights = jnp.exp(scores - (new_top - shift))
                    acc_ref[...] = acc_ref[...] * jnp.exp(old_top - new_top) + nn(
                        v_aug[block, seq, key_tile], weights.astype(jnp.bfloat16)
                    )
                    top_ref[0:1, :] = new_top

                def key_step(step, _):
                    block, key_tile = step // key_tiles, step % key_tiles
                    key_at = base_ref[block] + key_tile * KT
                    touched, plain, gap, strip = tile_class(edge_ref, row, key_at, query_at)

                    def raw():
                        keys = k_rows[block, seq, pl.ds(pl.multiple_of(key_tile * KT, KT), KT), :]
                        return nn(keys, queries)

                    @pl.when(touched & plain)
                    def _():
                        take(raw(), jnp.where(gap < 0, far_ref[0], far_ref[1]), block, key_tile)

                    @pl.when(touched & jnp.logical_not(plain))
                    def _():
                        take(masked(raw(), bias_ref[strip, :], key_at, start_row, end_row), 0.0, block, key_tile)

                    return 0

                lax.fori_loop(0, blocks * key_tiles, key_step, 0)
                total = acc_ref[HD : HD + 1, :]
                outs = acc_ref[:HD, :] / total
                lse_ref[near, seq, pl.ds(tile, 1), :] = top_ref[0:1, :] + jnp.log(total)
                for k in range(per_tile):
                    part = outs[:, k * part_len : (k + 1) * part_len]
                    o_ref[tile * per_tile + k, :, lane_base : lane_base + part_len] = part
                    ob_ref[2 * (tile * per_tile + k) + (near ^ base_ref[blocks])] = part.astype(jnp.bfloat16)
                return 0

            lax.fori_loop(0, tiles, query_tile, 0)


def attend_back_kernel(chips, carried, g_base, base_ref, edge_ref, far_ref, g_ref, o_ref, lse_ref, *refs):
    kv_refs, q_ref, refs = refs[:chips], refs[0], refs[chips:]
    start_ref, end_ref, bias_ref, *refs = refs
    if carried:
        old_band_ref, old_sides_ref, *refs = refs
    made_refs, refs = refs[:chips], refs[chips:]
    dq_ref = made_refs[0]
    band_ref, sides_ref, k_rows, v_rows, k_aug, dk_acc, dv_acc, dq_acc = refs
    groups, _, span = q_ref.shape
    blocks, seq_count, span_len, _ = k_rows.shape
    part_len = span_len // groups
    per_tile = TQ // part_len
    tiles, key_tiles = span_len // TQ, span_len // KT
    per_key = KT // part_len
    for far in range(chips):
        for seq, near, source, lanes in pieces_of(seq_count, part_len, groups):
            block = 2 * far + near
            rows = slice(source * part_len, (source + 1) * part_len)
            piece = kv_refs[far][source, HD : 2 * HD, lanes]
            k_rows[block, seq, rows, :] = flipped(piece)
            v_rows[block, seq, rows, :] = flipped(kv_refs[far][source, 2 * HD :, lanes])
            at = source % per_key * part_len
            k_aug[block, seq, source // per_key, :HD, at : at + part_len] = piece
    for block in range(blocks):
        for seq in range(seq_count):
            for tile in range(key_tiles):
                k_aug[block, seq, tile, HD:, :] = ones_row(KT)
    dk_acc[...] = jnp.zeros_like(dk_acc)
    dv_acc[...] = jnp.zeros_like(dv_acc)
    band_ref[...] = old_band_ref[...] if carried else jnp.zeros_like(band_ref)
    sides_ref[...] = old_sides_ref[...] if carried else jnp.zeros_like(sides_ref)

    for seq in range(seq_count):
        for near in range(2):
            lane_base = (near * seq_count + seq) * part_len

            def query_tile(tile, _, seq=seq, near=near, lane_base=lane_base):
                query_at = base_ref[near] + tile * TQ
                row = (near * seq_count + seq) * tiles + tile
                queries = lanes_of(q_ref, tile, per_tile, part_len, lane_base)
                first = 2 * tile * per_tile + (near ^ base_ref[blocks])
                grads = [g_ref[first + 2 * k, :, g_base : g_base + part_len] for k in range(per_tile)]
                grads = jnp.concatenate(grads, axis=1)
                outs = lanes_of(o_ref, tile, per_tile, part_len, lane_base)
                delta = jnp.sum(grads.astype(jnp.float32) * outs, axis=0, keepdims=True)
                query_rows, grad_rows = flipped(queries), flipped(grads)
                lse = lse_ref[near, seq, pl.ds(tile, 1), :]
                start_row = start_ref[near, seq, pl.ds(tile, 1), :]
                end_row = end_ref[near, seq, pl.ds(tile, 1), :]
                dq_acc[...] = jnp.zeros_like(dq_acc)

                def take(scores, shift, block, key_tile):
                    rows = pl.ds(pl.multiple_of(key_tile * KT, KT), KT)
                    probs = jnp.exp(scores - (lse - shift))
                    score_grad = probs * (nn(v_rows[block, seq, rows, :], grads) - delta)
                    score_low = score_grad.astype(jnp.bfloat16)
                    dv_acc[block, seq, rows, :] += nn(probs.astype(jnp.bfloat16), grad_rows)
                    dk_acc[block, seq, rows, :] += nn(score_low, query_rows)
                    made = nn(k_aug[block, seq, key_tile], score_low)
                    dq_acc[...] += made
                    return score_grad, made[HD : HD + 1, :]

                def key_step(step, _):
                    block, key_tile = step // key_tiles, step % key_tiles
                    key_at = base_ref[block] + key_tile * KT
                    touched, plain, gap, strip = tile_class(edge_ref, row, key_at, query_at)

                    def raw():
                        keys = k_rows[block, seq, pl.ds(pl.multiple_of(key_tile * KT, KT), KT), :]
                        return nn(keys, queries)

                    @pl.when(touched & plain)
                    def _():
                        _, sums = take(raw(), jnp.where(gap < 0, far_ref[0], far_ref[1]), block, key_tile)
                        side = (gap > 0).astype(jnp.int32)
                        sides_ref[pl.ds(side, 1), :] += sums

                    @pl.when(touched & jnp.logical_not(plain))
                    def _():
                        whole_grad, _ = take(
                            masked(raw(), bias_ref[strip, :], key_at, start_row, end_row), 0.0, block, key_tile
                        )
                        band_ref[strip, :] += whole_grad

                    return 0

                lax.fori_loop(0, blocks * key_tiles, key_step, 0)
                for k in range(per_tile):
                    part = dq_acc[:HD, k * part_len : (k + 1) * part_len].astype(jnp.bfloat16)
                    dq_ref[tile * per_tile + k, :HD, lane_base : lane_base + part_len] = part
                return 0

            lax.fori_loop(0, tiles, query_tile, 0)
    for far in range(chips):
        for seq, near, source, lanes in pieces_of(seq_count, part_len, groups):
            block = 2 * far + near
            rows = slice(source * part_len, (source + 1) * part_len)
            top = 0 if far else HD
            made_refs[far][source, top : top + HD, lanes] = dk_acc[block, seq, rows, :].T.astype(jnp.bfloat16)
            made_refs[far][source, top + HD : top + 2 * HD, lanes] = dv_acc[block, seq, rows, :].T.astype(jnp.bfloat16)


def strip_places():
    width = TQ + 128
    lane = np.arange(width)
    lane = np.where(lane < TQ, lane, lane - width)
    offset = 128 * (np.arange(TQ // 128 + 2)[:, None] - 1) - lane[None, :]
    return np.clip(offset, -MAXREL, MAXREL) + MAXREL


def strip_kernel(far_ref, wave_ref, strip_ref):
    near_blocks, _, width = wave_ref.shape
    first = KT + MARGIN - 128
    strip_ref[:first, :] = jnp.full((first, TQ), far_ref[0], jnp.float32)
    for k in range(near_blocks):
        spread = jnp.broadcast_to(wave_ref[k], (128, width))
        turned = pltpu.roll(spread, 0, 1, stride=1, stride_axis=0)
        strip_ref[first + 128 * k : first + 128 * (k + 1), :] = turned[:, :TQ]
    last = first + 128 * near_blocks
    strip_ref[last:, :] = jnp.full((strip_ref.shape[0] - last, TQ), far_ref[1], jnp.float32)


def bias_strip(far_bias, waves):
    return pl.pallas_call(
        strip_kernel,
        name="bias_strip",
        out_shape=jax.ShapeDtypeStruct((2 * KT + 2 * MARGIN + TQ, TQ), jnp.float32),
        in_specs=[SMEM, VMEM],
        out_specs=VMEM,
        compiler_params=pltpu.CompilerParams(vmem_limit_bytes=32 * 2**20),
    )(far_bias, waves)


def band_kernel(band_ref, sides_ref, near_ref, far_ref):
    near_blocks, _, width = near_ref.shape
    first = KT + MARGIN - 128
    last = first + 128 * near_blocks
    left = jnp.sum(band_ref[:first, :], axis=0, keepdims=True) + sides_ref[0:1, :]
    right = jnp.sum(band_ref[last:, :], axis=0, keepdims=True) + sides_ref[1:2, :]
    far_ref[...] = jnp.concatenate([left, right, jnp.zeros((6, TQ), jnp.float32)], axis=0)
    for k in range(near_blocks):
        rows = band_ref[first + 128 * k : first + 128 * (k + 1), :]
        spread = jnp.concatenate([rows, jnp.zeros((128, width - TQ), jnp.float32)], axis=1)
        row = lax.broadcasted_iota(jnp.int32, spread.shape, 0)
        for step in (1, 2, 4):
            spread = jnp.where((row & step) != 0, pltpu.roll(spread, width - step, 1), spread)
        total = spread[:8, :]
        for at in range(8, 128, 8):
            total = total + pltpu.roll(spread[at : at + 8, :], width - at, 1)
        near_ref[k] = jnp.sum(total, axis=0, keepdims=True)


def band_sums_of(band, sides):
    return pl.pallas_call(
        band_kernel,
        name="band_sums",
        out_shape=(
            jax.ShapeDtypeStruct((TQ // 128 + 2, 1, TQ + 128), jnp.float32),
            jax.ShapeDtypeStruct((8, TQ), jnp.float32),
        ),
        in_specs=[VMEM, VMEM],
        out_specs=(VMEM, VMEM),
        compiler_params=pltpu.CompilerParams(vmem_limit_bytes=32 * 2**20),
    )(band, sides)


SMEM = pl.BlockSpec(memory_space=pltpu.SMEM)
VMEM = pl.BlockSpec(memory_space=pltpu.VMEM)


def attend(base, edges, far_bias, kvs, starts, ends, bias):
    chips = len(kvs)
    groups, _, span = kvs[0].shape
    shape = (groups, HD, span)
    _, seq_count, tiles, _ = starts.shape
    blocks, span_len = 2 * chips, tiles * TQ
    return pl.pallas_call(
        functools.partial(attend_kernel, chips),
        name="attend",
        out_shape=(
            jax.ShapeDtypeStruct(shape, jnp.float32),
            jax.ShapeDtypeStruct((2 * groups, HD, span // 2), jnp.bfloat16),
            jax.ShapeDtypeStruct(starts.shape, jnp.float32),
        ),
        in_specs=[SMEM] * 3 + [VMEM] * (chips + 3),
        out_specs=(VMEM,) * 3,
        scratch_shapes=[
            pltpu.VMEM((blocks, seq_count, span_len, HD), jnp.bfloat16),
            pltpu.VMEM((blocks, seq_count, span_len // KT, AUG, KT), jnp.bfloat16),
            pltpu.VMEM((8, TQ), jnp.float32),
            pltpu.VMEM((AUG, TQ), jnp.float32),
        ],
        cost_estimate=pl.CostEstimate(flops=1, transcendentals=0, bytes_accessed=1),
        compiler_params=pltpu.CompilerParams(vmem_limit_bytes=48 * 2**20),
    )(base, edges, far_bias, *kvs, starts, ends, bias)


def attend_back(base, edges, far_bias, g, seq, o, lse, kvs, starts, ends, bias, sums=()):
    chips = len(kvs)
    groups, _, span = kvs[0].shape
    _, seq_count, tiles, _ = starts.shape
    blocks, span_len = 2 * chips, tiles * TQ
    made = pl.pallas_call(
        functools.partial(attend_back_kernel, chips, bool(sums), seq * span // 2),
        name="attend_back",
        out_shape=(jax.ShapeDtypeStruct(kvs[0].shape, jnp.bfloat16),)
        + (jax.ShapeDtypeStruct((groups, 2 * HD, span), jnp.bfloat16),) * (chips - 1)
        + (jax.ShapeDtypeStruct(bias.shape, jnp.float32), jax.ShapeDtypeStruct((8, TQ), jnp.float32)),
        in_specs=[SMEM] * 3
        + [VMEM] * (3 + chips + 3 + len(sums)),
        out_specs=(VMEM,) * (2 + chips),
        scratch_shapes=[
            pltpu.VMEM((blocks, seq_count, span_len, HD), jnp.bfloat16),
            pltpu.VMEM((blocks, seq_count, span_len, HD), jnp.bfloat16),
            pltpu.VMEM((blocks, seq_count, span_len // KT, AUG, KT), jnp.bfloat16),
            pltpu.VMEM((blocks, seq_count, span_len, HD), jnp.float32),
            pltpu.VMEM((blocks, seq_count, span_len, HD), jnp.float32),
            pltpu.VMEM((AUG, TQ), jnp.float32),
        ],
        cost_estimate=pl.CostEstimate(flops=1, transcendentals=0, bytes_accessed=1),
        compiler_params=pltpu.CompilerParams(vmem_limit_bytes=56 * 2**20),
    )(base, edges, far_bias, g, o, lse, *kvs, starts, ends, bias, *sums)
    return made[0], made[1:chips], made[-2:]


def trade(block, axis, bit):
    size = lax.axis_size(axis)
    return lax.ppermute(block, axis, [(i, i ^ bit) for i in range(size)])


def mate(block):
    return trade(block, "blk", 1)


def across_x(block):
    return trade(block, "blk", 2)


def across_y(block):
    return trade(block, "head", 1)


def across_z(block, distance):
    return trade(block, "head", 2 * distance)


def whole_block(array):
    return pl.BlockSpec(array.shape, lambda i: (0,) * len(array.shape))


def copy_kernel(plan, slots_ref, *arrays):
    for source, source_rows, target, target_rows, count in plan:
        views = []
        for which, (slot, scale, first, columns) in ((source, source_rows), (target, target_rows)):
            begin = first if slot is None else pl.multiple_of(slots_ref[slot] * scale, 8) + first
            views.append(arrays[which].at[pl.ds(begin, count), pl.ds(columns[0], columns[1])])
        views[1][...] = views[0][...]


def moved(name, slots, sources, shapes, plan):
    outs = tuple(pltpu.HBM(shape, sources[0].dtype) for shape in shapes)
    return pl.pallas_call(
        functools.partial(copy_kernel, plan),
        name=name,
        grid=(1,),
        out_shape=outs,
        in_specs=[SMEM] + [whole_block(block) for block in sources],
        out_specs=tuple(whole_block(block) for block in outs),
        compiler_params=pltpu.CompilerParams(vmem_limit_bytes=48 * 2**20),
    )(slots, *sources)


DEPTH = 4
CHIPS = 16


def turn_of(k):
    return k % DEPTH, k // DEPTH // 2, k // DEPTH % 2


def slot_table():
    n_blk = lax.axis_size("blk")
    group, place = lax.axis_index("head"), lax.axis_index("blk")
    groups = group ^ jnp.asarray([2 * turn_of(k)[0] + turn_of(k)[1] for k in range(CHIPS)], jnp.int32)
    sides = (place // 2) ^ jnp.asarray([turn_of(k)[2] for k in range(CHIPS)], jnp.int32)
    chips = groups * (n_blk // 2) + sides
    return jnp.concatenate([chips, groups, 2 * chips + place % 2, 2 * chips + 1 - place % 2])


CHIP, GROUP, DEVICE, MATE = 0, CHIPS, 2 * CHIPS, 3 * CHIPS


def after(block, *earlier):
    return lax.optimization_barrier((block, earlier))[0]


def beside(made, *sent):
    return lax.optimization_barrier((made, *sent))


def wide(block):
    return block.astype(jnp.float32)


def placed(name, slots, blocks, layout, shapes, order):
    plan = []
    for k, (which, at) in enumerate(order):
        for first, count, whole, take, target in layout:
            plan.append((which, (None, 0, at + first, take), len(blocks) + whole, target(k), count))
    return moved(name, slots, blocks, shapes, tuple(plan))


def parted(name, slots, wholes, layout, shapes, order):
    plan = []
    for k, (which, at) in enumerate(order):
        for first, count, whole, take, target in layout:
            plan.append((whole, target(k), len(wholes) + which, (None, 0, at + first, take), count))
    return moved(name, slots, wholes, shapes, tuple(plan))


def grouped(rows):
    order = []
    for k in range(CHIPS):
        group, z = k // DEPTH, k % DEPTH
        order.append((group, z * rows) if group < 3 else (3 + z // 2, z % 2 * rows))
    return order


def gather_z(payload, *earlier):
    payload = after(payload, *earlier) if earlier else payload
    return [payload] + [across_z(payload, k) for k in range(1, DEPTH)]


def gather_xy(own, *earlier):
    own = jnp.concatenate(own, axis=0)
    own = after(own, *earlier) if earlier else own
    return own, across_x(own), across_y(own)


def gather_corner(blocks, *earlier):
    own, by_x, by_y = blocks
    half = own.shape[0] // 2
    low, high = by_x[:half], by_y[half:]
    if earlier:
        low, high = after(low, *earlier), after(high, *earlier)
    return own, by_x, by_y, across_y(low), across_x(high)


def sum_parts(name, slots, wholes, layout, rows, width):
    full, half = DEPTH * rows, DEPTH // 2 * rows
    shapes = ((full, width),) * 3 + ((half, width),) * 2
    return parted(name, slots, wholes, layout, shapes, grouped(rows))


def sum_corner(blocks):
    own, by_x, by_y, low, high = blocks
    return own, by_x, by_y, across_y(low), across_x(high)


def sum_xy(blocks):
    own, by_x, by_y, low, high = blocks
    half = low.shape[0]
    return own, across_x(added(by_x, low, slice(0, half))), across_y(added(by_y, high, slice(half, 2 * half)))


def column_kernel(*refs):
    groups, outs = refs[:-DEPTH], refs[-DEPTH:]
    first = 0
    for at in range(0, len(groups), 3):
        rows = groups[at].shape[0] // DEPTH
        for k, out_ref in enumerate(outs):
            here = slice(k * rows, (k + 1) * rows)
            total = sum(wide(ref[here]) for ref in groups[at : at + 3])
            out_ref[first : first + rows, :] = total.astype(out_ref.dtype)
        first += rows


def column_sent(*groups):
    rows, width = sum(group[0].shape[0] for group in groups) // DEPTH, groups[0][0].shape[1]
    blocks = [block for group in groups for block in group]
    here, *given = pl.pallas_call(
        column_kernel,
        name="column",
        out_shape=[jax.ShapeDtypeStruct((rows, width), jnp.float32)]
        + [jax.ShapeDtypeStruct((rows, width), jnp.bfloat16)] * (DEPTH - 1),
        in_specs=[VMEM] * len(blocks),
        out_specs=[VMEM] * DEPTH,
        compiler_params=pltpu.CompilerParams(vmem_limit_bytes=32 * 2**20),
    )(*blocks)
    return [here] + [across_z(block, k + 1) for k, block in enumerate(given)]


def column_total(blocks):
    here, *met = blocks
    return here + sum(wide(block) for block in met)


def norm_kernel(here_ref, there_ref, gain_ref, rows_ref, scale_ref, *normed_refs):
    seqs, part, _ = here_ref.shape
    for seq in range(seqs):
        for which, ref in enumerate((here_ref, there_ref)):
            rows = wide(ref[seq])
            scale = lax.rsqrt(jnp.mean(rows * rows, axis=-1, keepdims=True) + EPS)
            normed = (rows * scale * gain_ref[...]).astype(here_ref.dtype)
            normed_refs[seq][which * part : (which + 1) * part, :] = normed
            if which == 0:
                rows_ref[seq * part : (seq + 1) * part, :] = rows
                scale_ref[seq * part : (seq + 1) * part, :] = scale


def normed_by_seq(here, there, gain):
    seqs, part, width = here.shape
    shapes = [(seqs * part, width), (seqs * part, 1)]
    return pl.pallas_call(
        norm_kernel,
        name="normed_by_seq",
        out_shape=[jax.ShapeDtypeStruct(shape, jnp.float32) for shape in shapes]
        + [jax.ShapeDtypeStruct((2 * part, width), here.dtype)] * seqs,
        in_specs=[VMEM] * 3,
        out_specs=[VMEM] * (2 + seqs),
    )(here, there, gain.reshape(1, width))


def feed_kernel(rows_ref, grad_ref, in_ref, down_ref, act_ref, up_ref, out_near, out_far, back_near, back_far):
    half = rows_ref.shape[0] // 2
    values, rise = gelu_both(nn(rows_ref[...], in_ref[...]))
    values = values.astype(act_ref.dtype)
    act_ref[...] = values
    up = (dot_on(grad_ref[...], down_ref[...], 1, 1) * rise).astype(up_ref.dtype)
    up_ref[...] = up
    made, back = nn(values, down_ref[...]), dot_on(up, in_ref[...], 1, 1)
    parts = ((out_near, made[:half]), (out_far, made[half:]), (back_near, back[:half]), (back_far, back[half:]))

    @pl.when(pl.program_id(0) == 0)
    def _():
        for ref, part in parts:
            ref[...] = part

    @pl.when(pl.program_id(0) > 0)
    def _():
        for ref, part in parts:
            ref[...] += part


def feed(rows, grads, in_w, down_w):
    tokens, width = rows.shape
    hidden, step = in_w.shape[1], 512
    whole = pl.BlockSpec((tokens, width), lambda i: (0, 0))
    half = pl.BlockSpec((tokens // 2, width), lambda i: (0, 0))
    units = pl.BlockSpec((tokens, step), lambda i: (0, i))
    return pl.pallas_call(
        feed_kernel,
        name="feed",
        grid=(hidden // step,),
        out_shape=[pltpu.HBM((tokens, hidden), rows.dtype)] * 2
        + [pltpu.HBM((tokens // 2, width), jnp.float32)] * 4,
        in_specs=[
            whole,
            whole,
            pl.BlockSpec((width, step), lambda i: (0, i)),
            pl.BlockSpec((step, width), lambda i: (i, 0)),
        ],
        out_specs=[units] * 2 + [half] * 4,
        cost_estimate=pl.CostEstimate(flops=1, transcendentals=0, bytes_accessed=1),
        compiler_params=pltpu.CompilerParams(vmem_limit_bytes=32 * 2**20),
    )(rows, grads, in_w, down_w)


def weight_grad_kernel(left_ref, right_ref, out_ref):
    out_ref[...] = dot_on(left_ref[...], right_ref[...], 0, 0).astype(out_ref.dtype)


def weight_grad(left, right):
    tokens, rows = left.shape
    cols, step = right.shape[1], 512
    left, right = (pltpu.with_memory_space_constraint(block, pltpu.HBM) for block in (left, right))
    return pl.pallas_call(
        weight_grad_kernel,
        name="weight_grad",
        grid=(rows // step,),
        out_shape=jax.ShapeDtypeStruct((rows, cols), left.dtype),
        in_specs=[pl.BlockSpec((tokens, step), lambda i: (0, i)), pl.BlockSpec((tokens, cols), lambda i: (0, 0))],
        out_specs=pl.BlockSpec((step, cols), lambda i: (i, 0)),
        cost_estimate=pl.CostEstimate(flops=1, transcendentals=0, bytes_accessed=1),
        compiler_params=pltpu.CompilerParams(vmem_limit_bytes=32 * 2**20),
    )(left, right)


def first_back_kernel(plan, slots_ref, in_0, made_0, in_1, made_1, *refs):
    *parts, whole_ref = refs
    rows = whole_ref.shape[0]
    step = 256
    for at in range(0, rows, step):
        here = slice(at, at + step)
        product = dot_on(in_0[here], made_0[...], 1, 1) + dot_on(in_1[here], made_1[...], 1, 1)
        whole_ref[here, :] = product.astype(whole_ref.dtype)
    for slot, scale, which, at in plan:
        source = pl.ds(pl.multiple_of(slots_ref[slot] * scale, scale), scale)
        parts[which][at : at + scale, :] = whole_ref[source, :]


def first_back(slots, plan, shapes, ins, made):
    outs = [pltpu.HBM(shape, made[0].dtype) for shape in shapes]
    sources = (ins[0], made[0], ins[1], made[1])
    sources = [pltpu.with_memory_space_constraint(block, pltpu.HBM) for block in sources]
    return pl.pallas_call(
        functools.partial(first_back_kernel, plan),
        name="first_back",
        grid=(1,),
        out_shape=outs,
        in_specs=[SMEM] + [whole_block(block) for block in sources],
        out_specs=[whole_block(block) for block in outs],
        scratch_shapes=[pltpu.VMEM((ins[0].shape[0], made[0].shape[0]), made[0].dtype)],
        compiler_params=pltpu.CompilerParams(vmem_limit_bytes=48 * 2**20),
    )(slots, *sources)


def last_kernel(first_ref, second_ref, wq_ref, wk_ref, wv_ref, q_ref, k_ref, v_ref, gain_ref):
    groups = first_ref.shape[1] // (3 * HD)
    for g in range(groups):
        for which, out_ref in enumerate((q_ref, k_ref, v_ref)):
            at = (3 * g + which) * HD
            pair = [ref[:, at : at + HD] for ref in (first_ref, second_ref)]
            out_ref[:, 2 * g * HD : 2 * (g + 1) * HD] = jnp.concatenate(pair, axis=1)
    products = sum(wide(w[...]) * grad[...] for w, grad in ((wq_ref, q_ref), (wk_ref, k_ref), (wv_ref, v_ref)))
    gain_ref[...] = jnp.sum(products, axis=1, keepdims=True)


def by_weight(first, second, *weights):
    rows, width = weights[0].shape
    return pl.pallas_call(
        last_kernel,
        name="by_weight",
        out_shape=[jax.ShapeDtypeStruct((rows, width), jnp.float32)] * 3 + [jax.ShapeDtypeStruct((rows, 1), jnp.float32)],
        in_specs=[VMEM] * 5,
        out_specs=[VMEM] * 4,
    )(first, second, *weights)


def halves_kernel(place_ref, in_ref, out_ref, *refs):
    *down_refs, in_w_ref, out_w_ref, down_w_ref = refs
    devices, rows, width = out_ref.shape
    for d in range(devices):
        here = pl.ds(d * rows, rows)
        for j in range(in_ref.shape[1] // rows):
            in_w_ref[here, j * width : (j + 1) * width] = in_ref[d, j * rows : (j + 1) * rows, :]
        out_w_ref[here, :] = out_ref[d]
    rows = down_refs[0].shape[1]
    for chip, down_ref in enumerate(down_refs):
        down_w_ref[pl.ds(chip * rows, rows), :] = down_ref[0]


def own_halves(core, whole, down_rows, shard):
    devices, rows, width = whole.shape
    steps, chips = 4, devices // 2
    in_rows = (rows - down_rows - shard) // 2
    in_at, out_at = down_rows // in_rows, (rows - shard) // shard
    shapes = (
        (devices * shard, in_rows // shard * width),
        (devices * shard, width),
        (chips * down_rows, width),
    )
    return pl.pallas_call(
        halves_kernel,
        name="own_halves",
        grid_spec=pltpu.PrefetchScalarGridSpec(
            num_scalar_prefetch=1,
            grid=(steps,),
            in_specs=[
                pl.BlockSpec((devices // steps, in_rows, width), lambda i, place_ref: (i, in_at + place_ref[0], 0)),
                pl.BlockSpec((devices // steps, shard, width), lambda i, place_ref: (i, out_at, 0)),
            ]
            + [
                pl.BlockSpec(
                    (1, down_rows, width), lambda i, place_ref, j=j: (2 * (i * chips // steps + j) + place_ref[0], 0, 0)
                )
                for j in range(chips // steps)
            ],
            out_specs=[pl.BlockSpec((shape[0] // steps, shape[1]), lambda i, place_ref: (i, 0)) for shape in shapes],
        ),
        out_shape=[pltpu.HBM(shape, whole.dtype) for shape in shapes],
        compiler_params=pltpu.CompilerParams(vmem_limit_bytes=32 * 2**20),
    )(core.reshape(1), *[whole] * (2 + chips // steps))


def add_kernel(place, whole_ref, part_ref, sum_ref):
    sum_ref[...] = whole_ref[...]
    sum_ref[place] = (wide(whole_ref[place]) + wide(part_ref[...])).astype(sum_ref.dtype)


def added(whole, part, place):
    return pl.pallas_call(
        functools.partial(add_kernel, place),
        name="added",
        out_shape=jax.ShapeDtypeStruct(whole.shape, whole.dtype),
        in_specs=[VMEM] * 2,
        out_specs=VMEM,
        compiler_params=pltpu.CompilerParams(vmem_limit_bytes=32 * 2**20),
    )(whole, part)


def document_bounds(segments):
    seq_count, blocks, span_len = segments.shape
    length = blocks * span_len
    numbers = lax.iota(jnp.int32, length // min(512, length) + 2)
    flat = segments.reshape(seq_count, length)
    below = jnp.sum((flat[:, :, None] < numbers).astype(jnp.int32), axis=1)
    here = flat[:, :, None] == numbers[:-1]
    starts = jnp.sum(jnp.where(here, below[:, None, :-1], 0), axis=2)
    ends = jnp.sum(jnp.where(here, below[:, None, 1:], 0), axis=2)
    return starts.reshape(segments.shape), ends.reshape(segments.shape)


def query_bounds(bounds, place, tile):
    near = [lax.dynamic_index_in_dim(bounds, place ^ k, 1, keepdims=False) for k in (0, 2)]
    near = jnp.stack(near, axis=0)
    return near.reshape(near.shape[0], near.shape[1], -1, tile)


def gelu_both(values):
    slope = float(np.sqrt(2.0 / np.pi))
    square = values * values
    curve = jnp.tanh(slope * values * (1.0 + 0.044715 * square))
    half = 0.5 * (1.0 + curve)
    rise = half + 0.5 * values * (1.0 - curve * curve) * (slope * (1.0 + 3 * 0.044715 * square))
    return values * half, rise


def joined(block):
    return jnp.concatenate([block, mate(block)], axis=0)


def halves_added(block):
    half = block.shape[0] // 2
    return block[:half] + mate(block[half:])


def norm_back(grad, rows, scale, gain):
    weighted = grad * gain
    inner = jnp.mean(rows * weighted, axis=-1, keepdims=True)
    return scale * weighted - rows * (scale * scale * scale) * inner


def dot_on(left, right, left_dim, right_dim):
    return lax.dot_general(left, right, (((left_dim,), (right_dim,)), ((), ())), preferred_element_type=jnp.float32)


def pair_body(
    inputs,
    segments,
    bucket_table,
    norm_gain,
    w_query,
    w_key,
    w_value,
    w_out,
    rel_bias,
    ff_gain,
    w_in,
    w_down,
    cotangent,
):
    low = jnp.bfloat16
    seq_count, _, part_len, width = inputs.shape
    groups = lax.axis_size("head")
    span_len = part_len * groups
    blocks = lax.axis_size("blk")
    group, place = lax.axis_index("head"), lax.axis_index("blk")
    core, side = place % 2, place // 2
    slots = slot_table()
    shard = w_query.shape[0]
    chip_rows = 2 * shard
    head_cols = 3 * HD
    first_cols = groups * head_cols
    half_width = groups * HD
    half_hidden = w_in.shape[1] // 2
    down_rows = w_down.shape[0]
    tokens = seq_count * part_len

    def all_rows(pieces):
        return jnp.concatenate(pieces, axis=0)

    turned = segments[1, -1, -1] < segments[0, -1, -1]

    def in_order(block):
        return jnp.where(turned, block[::-1], block)

    inputs, cotangent, segments = in_order(inputs), in_order(cotangent), in_order(segments)

    def by_core(first, second):
        return jnp.where(core == 0, first, second)

    def by_side(first, second):
        return jnp.where(side == 0, first, second)

    cores = [[g * blocks + 2 * s + c for g in range(groups) for s in range(blocks // 2)] for c in range(2)]

    def exchanged_all(block):
        return lax.all_to_all(block, ("head", "blk"), split_axis=0, concat_axis=0, tiled=True, axis_index_groups=cores)

    def exchanged(block):
        return lax.all_to_all(block, "head", split_axis=0, concat_axis=0, tiled=True)

    every, first_every = (0, width), (0, first_cols)
    def head_columns(weight, which):
        return weight.reshape(shard, groups, 2, HD)[:, :, which]

    def cut(which):
        return jnp.stack([head_columns(w, which) for w in (w_query, w_key, w_value)], axis=2).reshape(shard, -1)

    first_cut, second_cut = cut(0), cut(1)
    chunks = [by_side(first_cut, second_cut), across_x(by_side(second_cut, first_cut))]
    gains = jnp.concatenate([norm_gain, ff_gain, rel_bias, jnp.zeros((128 - 5 * shard // 2,), low)])
    gains = jnp.broadcast_to(jnp.pad(gains[None, :], ((0, 7), (0, 0))), (2 * CHIPS, 8, 128))
    gain_w = lax.all_to_all(after(gains, chunks[1]), ("head", "blk"), split_axis=0, concat_axis=0, tiled=True)
    gain_w = wide(gain_w[:, 0])
    gain_one = gain_w[:, :shard].reshape(-1)
    gain_two = gain_w[:, shard : 2 * shard].reshape(-1)

    input_rows = inputs.reshape(seq_count, part_len, width)
    token_rows, scale_one, *first_in = normed_by_seq(input_rows, across_x(input_rows), gain_one)

    first_blocks = []
    for at, chunk in enumerate(chunks):
        own = jnp.concatenate(gather_z(chunk), axis=0)
        if at == 0:
            own, chunks[1] = beside(own, chunks[1])
        by_y = across_y(own)
        if at == 1:
            by_y, first_in = beside(by_y, first_in)
        both = jnp.concatenate([own, by_y], axis=0)
        first_blocks += [both, mate(both)]
    plan = []
    for k in range(CHIPS):
        z, y, x = turn_of(k)
        for far, slot in enumerate((DEVICE, MATE)):
            source = (None, 0, (DEPTH * y + z) * shard, first_every)
            plan.append((2 * x + far, source, 4, (slot + k, shard, 0, first_every), shard))
    (first_w,) = moved("whole_first", slots, first_blocks, ((width, first_cols),), tuple(plan))

    def hidden_columns(which):
        return w_in.reshape(shard, -1, 2, down_rows)[:, :, which].reshape(shard, -1, width)

    payload_in = jnp.stack([hidden_columns(0), hidden_columns(1)], axis=0).transpose(0, 2, 1, 3).reshape(-1, width)
    in_rows = 2 * chip_rows + shard
    payload = jnp.concatenate([w_down, payload_in, w_out], axis=0)
    whole = lax.all_gather(payload, ("head", "blk"), axis=0, tiled=False)
    whole = pltpu.with_memory_space_constraint(whole, pltpu.HBM)

    lay_in = (
        (0, chip_rows, 0, every, lambda k: (CHIP + k, chip_rows, 0, (0, width))),
        (chip_rows, chip_rows, 0, every, lambda k: (CHIP + k, chip_rows, 0, (width, width))),
        (2 * chip_rows, shard, 1, every, lambda k: (CHIP + k, shard, 0, every)),
    )
    lay_down = ((0, down_rows, 0, every, lambda k: (CHIP + k, down_rows, 0, every)),)

    rel_table = gain_w[:, 2 * shard : 5 * shard // 2].reshape(HEADS, BUCKETS)
    rel_here = lax.dynamic_index_in_dim(rel_table, 2 * group + side, 0, keepdims=False)

    bucket_hot = bucket_table[:, None] == lax.iota(jnp.int32, BUCKETS)[None, :]
    by_offset = jnp.sum(jnp.where(bucket_hot, rel_here[None, :], 0.0), axis=1)
    places = strip_places()
    place_hot = jnp.asarray(places.reshape(-1))[:, None] == lax.iota(jnp.int32, 2 * MAXREL + 1)[None, :]
    place_hot = place_hot.astype(jnp.float32)
    waves = jnp.dot(place_hot, by_offset, precision=lax.Precision.HIGHEST)
    waves = waves.reshape(places.shape[0], 1, places.shape[1])
    far_bias = jnp.stack([by_offset[0], by_offset[-1]])
    bias = bias_strip(far_bias, waves)
    starts, ends = document_bounds(segments)
    starts, ends = query_bounds(starts, place, TQ), query_bounds(ends, place, TQ)
    edges = jnp.stack([starts[..., 0], starts[..., -1], ends[..., 0], ends[..., -1]], axis=-1)
    base = (place ^ jnp.asarray([0, 2, 1, 3], jnp.int32)) * span_len
    base = jnp.concatenate([base, side.reshape(1)])

    made = [dot_on(first_w, rows, 0, 1).astype(low) for rows in first_in]
    sent = exchanged(made[0].reshape(groups, head_cols, 2 * part_len))
    sent, bias, far_bias, starts, ends, edges = beside(sent, bias, far_bias, starts, ends, edges)
    bounds = [(starts[:, seq : seq + 1], ends[:, seq : seq + 1], bias) for seq in range(seq_count)]
    edges = [edges[:, seq].reshape(-1) for seq in range(seq_count)]
    attended, heads, attn_cols = [], [], [None] * seq_count
    for seq in range(seq_count):
        heads.append([sent, mate(sent)])
        if seq + 1 < seq_count:
            heads[seq][1], made[seq + 1] = beside(heads[seq][1], made[seq + 1])
        done = attend(base, edges[seq], far_bias, heads[seq], *bounds[seq])
        if seq + 1 < seq_count:
            done, sent = beside(done, exchanged(made[seq + 1].reshape(groups, head_cols, 2 * part_len)))
        else:
            done, attn_cols[seq - 1] = beside(done, attn_cols[seq - 1])
        attended.append(done)
        attn_cols[seq] = exchanged_all(done[1])
    attn_cols[1], in_w, out_w, down_w = beside(attn_cols[1], *own_halves(core, whole, down_rows, shard))
    attn_cols = jnp.concatenate([block.reshape(2 * half_width, part_len) for block in attn_cols], axis=1)
    hidden_one = token_rows + dot_on(attn_cols, out_w, 0, 0)
    scale_two = lax.rsqrt(jnp.mean(hidden_one * hidden_one, axis=-1, keepdims=True) + EPS)
    second_in = joined((hidden_one * scale_two * gain_two).astype(low))
    incoming_low = cotangent.reshape(tokens, width)
    incoming = joined(incoming_low)
    activated, up_grad, layer_near, layer_far, back_near, back_far = feed(second_in, incoming, in_w, down_w)
    whole_down = weight_grad(activated, incoming)
    down_parts = sum_parts("parts_down", slots, (whole_down,), lay_down, down_rows, width)
    down_parts = sum_corner(down_parts)
    second_grad = back_near + mate(back_far)
    hidden_part = norm_back(second_grad, hidden_one, scale_two, gain_two)
    hidden_grad = wide(incoming_low) + hidden_part
    branch = hidden_grad.astype(low)
    grads = dot_on(out_w, branch, 1, 1).astype(low).reshape(HEADS, HD, tokens)
    late_in, late_branch = after((second_in, branch), grads, down_parts)
    whole_in = weight_grad(late_in, up_grad)
    whole_out = dot_on(attn_cols, late_branch, 1, 0).astype(low).reshape(-1, 2, shard, width)
    out_mine, out_given = by_core(whole_out[:, 0], whole_out[:, 1]), by_core(whole_out[:, 1], whole_out[:, 0])
    whole_out = (wide(out_mine) + wide(mate(out_given))).astype(low).reshape(half_width, width)
    in_parts = sum_parts("parts_in", slots, (whole_in, whole_out), lay_in, in_rows, width)
    grads, in_parts = beside(exchanged_all(grads), in_parts)
    in_parts = sum_corner(in_parts)
    down_parts = sum_xy(down_parts)

    def offset_grads(band, sides, earlier):
        near_sums, far_sums = band_sums_of(after(band, *earlier), sides)
        offset_sums = jnp.dot(near_sums.reshape(-1), place_hot, precision=lax.Precision.HIGHEST)
        far_sums = jnp.sum(far_sums, axis=1)
        end_hot = lax.iota(jnp.int32, 2 * MAXREL + 1)
        offset_sums = offset_sums + jnp.where(end_hot == 0, far_sums[0], 0.0)
        offset_sums = offset_sums + jnp.where(end_hot == 2 * MAXREL, far_sums[1], 0.0)
        return jnp.sum(jnp.where(bucket_hot, offset_sums[:, None], 0.0), axis=0)

    sums, made, sent = (), [], None
    for seq in range(seq_count):
        outs, _, lse = attended[seq]
        done = attend_back(base, edges[seq], far_bias, grads, seq, outs, lse, heads[seq], *bounds[seq], sums)
        if seq == 0:
            done, in_parts, down_parts = beside(done, in_parts, down_parts)
        else:
            done, in_parts, down_sent, made[0] = beside(done, in_parts, down_sent, made[0])
        near_grad, (far_grad,), sums = done
        near_grad = added(near_grad, mate(far_grad), (slice(None), slice(HD, 3 * HD)))
        if seq == 0:
            grads, near_grad = beside(grads, near_grad)
            in_parts = sum_xy(in_parts)
            down_sent = column_sent(down_parts)
        made.append(exchanged(near_grad))
    band, sides = sums
    layer_out = (hidden_one + layer_near + mate(layer_far)).astype(low).reshape(inputs.shape)
    made = [block.reshape(first_cols, 2 * part_len) for block in made]
    first_grads = [dot_on(after(made[0], near_grad), first_w, 0, 1)]
    far_parts = [across_x(first_grads[0][part_len:].astype(low))]
    made[1], rel_grad, far_parts = beside(made[1], offset_grads(band, sides, (near_grad,)), far_parts)
    plan, column = [], 2 * DEPTH * shard
    for k in range(CHIPS):
        z, y, x = turn_of(k)
        plan.append((MATE + k, shard, 0, y * column + (2 * z + x) * shard))
        plan.append((DEVICE + k, shard, 1 + y, (2 * z + x) * shard))
    shapes = ((2 * column, first_cols), (column, first_cols), (column, first_cols))
    given, near, by_y = first_back(slots, tuple(plan), shapes, [block.T for block in first_in], made)
    in_sent = column_sent(after(in_parts, made[1]))
    got = mate(given)
    by_y = across_y((wide(by_y) + wide(got[column:])).astype(low))
    by_y, in_sent = beside(by_y, in_sent)
    first_sent = column_sent((near, got[:column], by_y))
    first_sum = column_total(first_sent)
    first_sums = [first_sum[:shard], across_x(first_sum[shard:])]
    in_sum = column_total(after(in_sent, first_sent[0]))
    grad_down = column_total(down_sent)
    first_grads.append(dot_on(after(made[1], first_sent[0]), first_w, 0, 1))
    far_parts.append(across_x(first_grads[1][part_len:].astype(low)))
    first_grad = all_rows([grad[:part_len] for grad in first_grads]) + wide(all_rows(far_parts))
    input_part = norm_back(first_grad, token_rows, scale_one, gain_one)
    input_grad = (hidden_grad + input_part).astype(low).reshape(inputs.shape)

    grad_query, grad_key, grad_value, norm_sums = by_weight(
        by_side(*first_sums), by_side(*first_sums[::-1]), w_query, w_key, w_value
    )

    hidden_rows = jnp.concatenate([in_sum[:chip_rows], in_sum[chip_rows : 2 * chip_rows]], axis=1)
    mine = by_core(hidden_rows[:shard], hidden_rows[shard:])
    other = mate(by_core(hidden_rows[shard:], hidden_rows[:shard]))
    in_pair = [block.reshape(shard, -1, down_rows) for block in (by_core(mine, other), by_core(other, mine))]
    grad_in = jnp.stack(in_pair, axis=2).reshape(shard, -1)
    grad_out = in_sum[2 * chip_rows :]

    grad_norm_gain = norm_sums[:, 0] / wide(norm_gain)
    grad_ff_gain = jnp.sum(wide(w_in) * grad_in, axis=1) / wide(ff_gain)

    rel_grad = jnp.pad(rel_grad[None, :], ((0, 7), (0, 128 - BUCKETS)))
    rel_sum = (rel_grad + mate(rel_grad))[0]
    rel_mine = by_core(rel_sum[: BUCKETS // 2], rel_sum[BUCKETS // 2 : BUCKETS])

    return (
        in_order(layer_out),
        in_order(input_grad),
        grad_norm_gain,
        grad_query,
        grad_key,
        grad_value,
        grad_out,
        rel_mine,
        grad_ff_gain,
        grad_in,
        grad_down,
    )


def solution(mesh):
    placed = (
        P(None, "blk", "head", None),
        P(),
        P(),
        P(("head", "blk")),
        P(("head", "blk"), None),
        P(("head", "blk"), None),
        P(("head", "blk"), None),
        P(("head", "blk"), None),
        P(("head", "blk")),
        P(("head", "blk")),
        P(("head", "blk"), None),
        P(("head", "blk"), None),
        P(None, "blk", "head", None),
    )
    n_head, n_blk = mesh.shape["head"], mesh.shape["blk"]
    paired = HEADS == 2 * n_head and (n_head, n_blk) == (8, 4)
    return jax.shard_map(
        pair_body if paired else ring_body,
        mesh=mesh,
        in_specs=placed,
        out_specs=(
            P(None, "blk", "head", None),
            P(None, "blk", "head", None),
            P(("head", "blk")),
            P(("head", "blk"), None),
            P(("head", "blk"), None),
            P(("head", "blk"), None),
            P(("head", "blk"), None),
            P(("head", "blk")),
            P(("head", "blk")),
            P(("head", "blk"), None),
            P(("head", "blk"), None),
        ),
        check_vma=False,
    )
```

```python
import functools

import jax
import jax.numpy as jnp
import numpy as np
from jax import lax
from jax.experimental import pallas as pl
from jax.experimental.pallas import tpu as pltpu
from jax.sharding import PartitionSpec as P

HEADS = 16
HD = 64
BUCKETS = 32
MAXREL = 128
EPS = 1e-06
FLOOR = -1e30


def from_behind(block, axis, distance):
    devices = range(lax.axis_size(axis))
    route = [((i - distance) % len(devices), i) for i in devices]
    return lax.ppermute(block, axis, route)


def rms_scale(token_rows, gain_vector):
    return (
        token_rows
        * lax.rsqrt(jnp.mean(token_rows * token_rows, axis=-1, keepdims=True) + EPS)
        * gain_vector
    )


def smooth(values):
    return jax.nn.gelu(values, approximate=True)


def band_layout(span_len):
    tile_side = min(128, span_len)
    reach = MAXREL // tile_side + 2
    return (tile_side, span_len // tile_side, reach)


def band_tables(bucket_table, rel_here, span_len):
    tile_side, _, reach = band_layout(span_len)
    kinds = 2 * reach + 1
    gaps = lax.iota(jnp.int32, kinds) - reach
    rows_in = lax.iota(jnp.int32, tile_side)
    offsets = gaps[:, None, None] * tile_side + rows_in[None, None, :] - rows_in[None, :, None]
    lookup = jnp.clip(offsets, -MAXREL, MAXREL) + MAXREL
    bucket = jnp.take(bucket_table, lookup.reshape(-1), axis=0)
    onehot = (bucket[:, None] == lax.iota(jnp.int32, BUCKETS)[None, :]).astype(jnp.float32)
    band_bias = jnp.dot(rel_here, onehot.T, precision=lax.Precision.HIGHEST)
    return (band_bias.reshape(rel_here.shape[0], kinds, tile_side, tile_side), onehot)


def band_index(block_gap, span_len):
    _, tiles, reach = band_layout(span_len)
    row_tile = lax.iota(jnp.int32, tiles)[:, None, None, None]
    col_tile = lax.iota(jnp.int32, tiles)[None, None, :, None]
    return jnp.clip(block_gap * tiles + col_tile - row_tile, -reach, reach) + reach


def bias_tile(band_bias, block_gap, span_len):
    heads_count, kinds, tile_side, _ = band_bias.shape
    tiles = span_len // tile_side
    which = band_index(block_gap, span_len)
    result = jnp.zeros((heads_count, tiles, tile_side, tiles, tile_side), jnp.float32)
    for kind in range(kinds):
        result = jnp.where(which[None] == kind, band_bias[:, kind][:, None, :, None, :], result)
    return result.reshape(heads_count, span_len, span_len)


def band_sums(tile_sum, block_gap, span_len):
    tile_side, tiles, reach = band_layout(span_len)
    heads_count = tile_sum.shape[0]
    split_sum = tile_sum.reshape(heads_count, tiles, tile_side, tiles, tile_side)
    which = band_index(block_gap, span_len)
    parts = []
    for kind in range(2 * reach + 1):
        parts.append(jnp.sum(jnp.where(which[None] == kind, split_sum, 0.0), axis=(1, 3)))
    return jnp.stack(parts, axis=1).reshape(heads_count, -1)


def pass_grads(key_grad, value_grad):
    return (
        from_behind(key_grad.astype(jnp.bfloat16), "blk", 1).astype(key_grad.dtype),
        from_behind(value_grad.astype(jnp.bfloat16), "blk", 1).astype(value_grad.dtype),
    )


def ring_body(
    inputs,
    segments,
    bucket_table,
    norm_gain,
    w_query,
    w_key,
    w_value,
    w_out,
    rel_bias,
    ff_gain,
    w_in,
    w_down,
    cotangent,
):
    seq_count, _, part_len, width = inputs.shape
    cycle_size = lax.axis_size("blk")
    head_groups = lax.axis_size("head")
    heads_here = HEADS // head_groups
    span_len = part_len * head_groups
    cycle_place = lax.axis_index("blk")
    head_place = lax.axis_index("head")
    gathered = (
        lax.all_gather(norm_gain, ("head", "blk"), axis=0, tiled=True),
        lax.all_gather(w_query, ("head", "blk"), axis=0, tiled=True),
        lax.all_gather(w_key, ("head", "blk"), axis=0, tiled=True),
        lax.all_gather(w_value, ("head", "blk"), axis=0, tiled=True),
        lax.all_gather(w_out, ("head", "blk"), axis=0, tiled=True),
        lax.all_gather(rel_bias, ("head", "blk"), axis=0, tiled=True),
        lax.all_gather(ff_gain, ("head", "blk"), axis=0, tiled=True),
        lax.all_gather(w_in, ("head", "blk"), axis=0, tiled=True),
        lax.all_gather(w_down, ("head", "blk"), axis=0, tiled=True),
    )
    gain_one, query_w, key_w, value_w, out_w, rel_flat, gain_two, in_w, down_w = gathered
    token_rows = inputs.reshape(-1, width).astype(jnp.float32)
    normed, norm_one_back = jax.vjp(rms_scale, token_rows, gain_one.astype(jnp.float32))
    first_in = normed.astype(jnp.bfloat16)

    def project(weight):
        made_rows = jnp.dot(first_in, weight, preferred_element_type=jnp.float32)
        return made_rows.astype(jnp.bfloat16).reshape(seq_count, part_len, -1)

    queries, keys_home, values_home = (
        lax.all_to_all(project(query_w), "head", split_axis=2, concat_axis=1, tiled=True),
        lax.all_to_all(project(key_w), "head", split_axis=2, concat_axis=1, tiled=True),
        lax.all_to_all(project(value_w), "head", split_axis=2, concat_axis=1, tiled=True),
    )
    head_shape = (seq_count, span_len, heads_here, HD)
    queries = queries.reshape(head_shape)
    keys_home = keys_home.reshape(head_shape)
    values_home = values_home.reshape(head_shape)
    rel_table = rel_flat.astype(jnp.float32).reshape(HEADS, BUCKETS)
    rel_here = lax.dynamic_slice_in_dim(rel_table, head_place * heads_here, heads_here, 0)
    band_bias, band_onehot = band_tables(bucket_table, rel_here, span_len)

    def tile_scores(query_rows, key_rows, query_block, key_block):
        query_ids = lax.dynamic_index_in_dim(segments, query_block, 1, keepdims=False)
        key_ids = lax.dynamic_index_in_dim(segments, key_block, 1, keepdims=False)
        plain_scores = (
            jnp.einsum("sihd,sjhd->shij", query_rows, key_rows, preferred_element_type=jnp.float32)
            + bias_tile(band_bias, key_block - query_block, span_len)[None]
        )
        same_doc = query_ids[:, None, :, None] == key_ids[:, None, None, :]
        return jnp.where(same_doc, plain_scores, FLOOR)

    first_scores = tile_scores(queries, keys_home, cycle_place, cycle_place)
    row_max = jnp.max(first_scores, axis=-1)
    first_weights = jnp.exp(first_scores - row_max[..., None])
    row_total = jnp.sum(first_weights, axis=-1)
    summed = jnp.einsum(
        "shij,sjhd->sihd",
        first_weights.astype(jnp.bfloat16),
        values_home,
        preferred_element_type=jnp.float32,
    )

    def forward_turn(cycle_turn, state_now):
        old_max, old_total, old_summed, key_rows, value_rows = state_now
        key_rows, value_rows = from_behind((key_rows, value_rows), "blk", 1)
        source = (cycle_place - cycle_turn) % cycle_size
        scores = tile_scores(queries, key_rows, cycle_place, source)
        new_max = jnp.maximum(old_max, jnp.max(scores, axis=-1))
        shrink = jnp.exp(old_max - new_max)
        weights_now = jnp.exp(scores - new_max[..., None])
        new_total = old_total * shrink + jnp.sum(weights_now, axis=-1)
        new_summed = old_summed * jnp.transpose(shrink, (0, 2, 1))[..., None] + jnp.einsum(
            "shij,sjhd->sihd",
            weights_now.astype(jnp.bfloat16),
            value_rows,
            preferred_element_type=jnp.float32,
        )
        return (new_max, new_total, new_summed, key_rows, value_rows)

    row_max, row_total, summed, _, _ = lax.fori_loop(
        1, cycle_size, forward_turn, (row_max, row_total, summed, keys_home, values_home)
    )
    log_total = row_max + jnp.log(row_total)
    attended = summed / jnp.transpose(row_total, (0, 2, 1))[..., None]
    attended_low = attended.astype(jnp.bfloat16).reshape(seq_count, span_len, heads_here * HD)
    attn_rows = lax.all_to_all(
        attended_low, "head", split_axis=1, concat_axis=2, tiled=True
    ).reshape(-1, HEADS * HD)
    hidden_one = token_rows + jnp.dot(attn_rows, out_w, preferred_element_type=jnp.float32)
    normed_two, norm_two_back = jax.vjp(rms_scale, hidden_one, gain_two.astype(jnp.float32))
    second_in = normed_two.astype(jnp.bfloat16)
    upward = jnp.dot(second_in, in_w, preferred_element_type=jnp.float32)
    activated, smooth_back = jax.vjp(smooth, upward)
    activated_low = activated.astype(jnp.bfloat16)
    layer_rows = hidden_one + jnp.dot(activated_low, down_w, preferred_element_type=jnp.float32)
    layer_out = layer_rows.astype(jnp.bfloat16).reshape(inputs.shape)
    back_query, back_key, back_value, back_out, back_in, back_down = (
        query_w,
        key_w,
        value_w,
        out_w,
        in_w,
        down_w,
    )
    incoming_low = cotangent.reshape(-1, width)
    incoming = incoming_low.astype(jnp.float32)
    grad_down = jnp.dot(activated_low.T, incoming_low, preferred_element_type=jnp.float32)
    (up_grad,) = smooth_back(jnp.dot(incoming_low, back_down.T, preferred_element_type=jnp.float32))
    up_low = up_grad.astype(jnp.bfloat16)
    grad_in = jnp.dot(second_in.T, up_low, preferred_element_type=jnp.float32)
    hidden_part, grad_gain_two = norm_two_back(
        jnp.dot(up_low, back_in.T, preferred_element_type=jnp.float32)
    )
    hidden_grad = incoming + hidden_part
    branch_low = hidden_grad.astype(jnp.bfloat16)
    grad_out = jnp.dot(attn_rows.T, branch_low, preferred_element_type=jnp.float32)
    attn_grad_low = jnp.dot(branch_low, back_out.T, preferred_element_type=jnp.float32).astype(
        jnp.bfloat16
    )
    grad_heads = lax.all_to_all(
        attn_grad_low.reshape(seq_count, part_len, HEADS * HD),
        "head",
        split_axis=2,
        concat_axis=1,
        tiled=True,
    ).reshape(head_shape)
    row_delta = jnp.transpose(
        jnp.sum(grad_heads.astype(jnp.float32) * attended, axis=-1), (0, 2, 1)
    )

    def tile_grads(
        query_rows, grad_rows, log_rows, delta_rows, key_rows, value_rows, query_block, key_block
    ):
        scores = tile_scores(query_rows, key_rows, query_block, key_block)
        probs = jnp.exp(scores - log_rows[..., None])
        value_part = jnp.einsum(
            "shij,sihd->sjhd",
            probs.astype(jnp.bfloat16),
            grad_rows,
            preferred_element_type=jnp.float32,
        )
        prob_grad = jnp.einsum(
            "sihd,sjhd->shij", grad_rows, value_rows, preferred_element_type=jnp.float32
        )
        score_low = (probs * (prob_grad - delta_rows[..., None])).astype(jnp.bfloat16)
        query_part = jnp.einsum(
            "shij,sjhd->sihd", score_low, key_rows, preferred_element_type=jnp.float32
        )
        key_part = jnp.einsum(
            "shij,sihd->sjhd", score_low, query_rows, preferred_element_type=jnp.float32
        )
        tile_sum = jnp.sum(score_low.astype(jnp.float32), axis=0)
        rel_part = jnp.dot(
            band_sums(tile_sum, key_block - query_block, span_len),
            band_onehot,
            precision=lax.Precision.HIGHEST,
        )
        return (query_part, key_part, value_part, rel_part)

    query_grad, key_grad, value_grad, rel_grad = tile_grads(
        queries, grad_heads, log_total, row_delta, keys_home, values_home, cycle_place, cycle_place
    )

    def key_turn(cycle_turn, state_now):
        key_rows, value_rows, key_sum, value_sum, query_sum, rel_sum = state_now
        key_sum, value_sum = pass_grads(key_sum, value_sum)
        key_rows, value_rows = from_behind((key_rows, value_rows), "blk", 1)
        source = (cycle_place - cycle_turn) % cycle_size
        query_part, key_part, value_part, rel_part = tile_grads(
            queries, grad_heads, log_total, row_delta, key_rows, value_rows, cycle_place, source
        )
        return (
            key_rows,
            value_rows,
            key_sum + key_part,
            value_sum + value_part,
            query_sum + query_part,
            rel_sum + rel_part,
        )

    state_first = (keys_home, values_home, key_grad, value_grad, query_grad, rel_grad)
    _, _, key_grad, value_grad, query_grad, rel_grad = lax.fori_loop(
        1, cycle_size, key_turn, state_first
    )
    key_grad, value_grad = pass_grads(key_grad, value_grad)
    block_shape = (seq_count, span_len, heads_here * HD)
    query_rows, key_rows_back, value_rows_back = (
        lax.all_to_all(
            query_grad.astype(jnp.bfloat16).reshape(block_shape),
            "head",
            split_axis=1,
            concat_axis=2,
            tiled=True,
        ),
        lax.all_to_all(
            key_grad.astype(jnp.bfloat16).reshape(block_shape),
            "head",
            split_axis=1,
            concat_axis=2,
            tiled=True,
        ),
        lax.all_to_all(
            value_grad.astype(jnp.bfloat16).reshape(block_shape),
            "head",
            split_axis=1,
            concat_axis=2,
            tiled=True,
        ),
    )
    query_rows = query_rows.reshape(-1, HEADS * HD)
    key_rows_back = key_rows_back.reshape(-1, HEADS * HD)
    value_rows_back = value_rows_back.reshape(-1, HEADS * HD)
    grad_query = jnp.dot(first_in.T, query_rows, preferred_element_type=jnp.float32)
    grad_key = jnp.dot(first_in.T, key_rows_back, preferred_element_type=jnp.float32)
    grad_value = jnp.dot(first_in.T, value_rows_back, preferred_element_type=jnp.float32)
    first_grad = (
        jnp.dot(query_rows, back_query.T, preferred_element_type=jnp.float32)
        + jnp.dot(key_rows_back, back_key.T, preferred_element_type=jnp.float32)
        + jnp.dot(value_rows_back, back_value.T, preferred_element_type=jnp.float32)
    )
    input_part, grad_gain_one = norm_one_back(first_grad)
    input_grad = (hidden_grad + input_part).astype(jnp.bfloat16).reshape(inputs.shape)
    rel_full = lax.dynamic_update_slice_in_dim(
        jnp.zeros((HEADS, BUCKETS), jnp.float32), rel_grad, head_place * heads_here, 0
    ).reshape(-1)
    shards = tuple(
        (
            lax.psum_scatter(grad_gain_one, ("head", "blk"), scatter_dimension=0, tiled=True),
            lax.psum_scatter(grad_query, ("head", "blk"), scatter_dimension=0, tiled=True),
            lax.psum_scatter(grad_key, ("head", "blk"), scatter_dimension=0, tiled=True),
            lax.psum_scatter(grad_value, ("head", "blk"), scatter_dimension=0, tiled=True),
            lax.psum_scatter(grad_out, ("head", "blk"), scatter_dimension=0, tiled=True),
            lax.psum_scatter(rel_full, ("head", "blk"), scatter_dimension=0, tiled=True),
            lax.psum_scatter(grad_gain_two, ("head", "blk"), scatter_dimension=0, tiled=True),
            lax.psum_scatter(grad_in, ("head", "blk"), scatter_dimension=0, tiled=True),
            lax.psum_scatter(grad_down, ("head", "blk"), scatter_dimension=0, tiled=True),
        )
    )
    return (
        layer_out,
        input_grad,
        shards[0],
        shards[1],
        shards[2],
        shards[3],
        shards[4],
        shards[5],
        shards[6],
        shards[7],
        shards[8],
    )


TQ = 512
KT = 512
MARGIN = 128
AUG = 80
NT = (((1,), (1,)), ((), ()))


def nn(left, right):
    return jnp.dot(left, right, preferred_element_type=jnp.float32)


def flipped(block):
    return block.astype(jnp.float32).T.astype(jnp.bfloat16)


def ones_row(width):
    first = lax.broadcasted_iota(jnp.int32, (AUG - HD, width), 0) == 0
    return jnp.where(first, 1.0, 0.0).astype(jnp.bfloat16)


def pieces_of(seq_count, part_len, groups):
    for seq in range(seq_count):
        for near in range(2):
            for source in range(groups):
                yield seq, near, source, slice((near * seq_count + seq) * part_len, (near * seq_count + seq + 1) * part_len)


def lanes_of(ref, tile_at, per_tile, part_len, lane_base):
    parts = [ref[tile_at * per_tile + k, :HD, pl.ds(lane_base, part_len)] for k in range(per_tile)]
    return parts[0] if per_tile == 1 else jnp.concatenate(parts, axis=1)


def tile_class(edge_ref, row, key_at, query_at):
    first_start, last_start, first_end, last_end = (edge_ref[row * 4 + k] for k in range(4))
    touched = (key_at + KT > first_start) & (key_at < last_end)
    gap = key_at - query_at
    whole = (key_at >= last_start) & (key_at + KT <= first_end)
    plain = whole & ((gap + KT <= -MAXREL + 1) | (gap >= TQ + MAXREL - 1))
    strip_at = jnp.clip(gap, -(KT + MARGIN), TQ + MARGIN) + KT + MARGIN
    return touched, plain, gap, pl.ds(pl.multiple_of(strip_at, 128), KT)


def masked(scores, bias, key_at, start_row, end_row):
    places = lax.broadcasted_iota(jnp.int32, scores.shape, 0) + key_at
    return jnp.where((places >= start_row) & (places < end_row), scores + bias, FLOOR)


def attend_kernel(chips, base_ref, edge_ref, far_ref, *refs):
    kv_refs, q_ref = refs[:chips], refs[0]
    start_ref, end_ref, bias_ref, o_ref, ob_ref, lse_ref, k_rows, v_aug, top_ref, acc_ref = refs[chips:]
    groups, _, span = q_ref.shape
    blocks, seq_count, span_len, _ = k_rows.shape
    part_len = span_len // groups
    per_tile = TQ // part_len
    tiles, key_tiles = span_len // TQ, span_len // KT
    per_key = KT // part_len
    for far in range(chips):
        for seq, near, source, lanes in pieces_of(seq_count, part_len, groups):
            block = 2 * far + near
            k_rows[block, seq, source * part_len : (source + 1) * part_len, :] = flipped(kv_refs[far][source, HD : 2 * HD, lanes])
            at = source % per_key * part_len
            v_aug[block, seq, source // per_key, :HD, at : at + part_len] = kv_refs[far][source, 2 * HD :, lanes]
    for block in range(blocks):
        for seq in range(seq_count):
            for tile in range(key_tiles):
                v_aug[block, seq, tile, HD:, :] = ones_row(KT)

    for seq in range(seq_count):
        for near in range(2):
            lane_base = (near * seq_count + seq) * part_len

            def query_tile(tile, _, seq=seq, near=near, lane_base=lane_base):
                query_at = base_ref[near] + tile * TQ
                row = (near * seq_count + seq) * tiles + tile
                queries = lanes_of(q_ref, tile, per_tile, part_len, lane_base)
                top_ref[...] = jnp.full_like(top_ref, FLOOR)
                acc_ref[...] = jnp.zeros_like(acc_ref)
                start_row = start_ref[near, seq, pl.ds(tile, 1), :]
                end_row = end_ref[near, seq, pl.ds(tile, 1), :]

                def take(scores, shift, block, key_tile):
                    old_top = top_ref[0:1, :]
                    new_top = jnp.maximum(old_top, jnp.max(scores, axis=0, keepdims=True) + shift)
                    weights = jnp.exp(scores - (new_top - shift))
                    acc_ref[...] = acc_ref[...] * jnp.exp(old_top - new_top) + nn(
                        v_aug[block, seq, key_tile], weights.astype(jnp.bfloat16)
                    )
                    top_ref[0:1, :] = new_top

                def key_step(step, _):
                    block, key_tile = step // key_tiles, step % key_tiles
                    key_at = base_ref[block] + key_tile * KT
                    touched, plain, gap, strip = tile_class(edge_ref, row, key_at, query_at)

                    def raw():
                        keys = k_rows[block, seq, pl.ds(pl.multiple_of(key_tile * KT, KT), KT), :]
                        return nn(keys, queries)

                    @pl.when(touched & plain)
                    def _():
                        take(raw(), jnp.where(gap < 0, far_ref[0], far_ref[1]), block, key_tile)

                    @pl.when(touched & jnp.logical_not(plain))
                    def _():
                        take(masked(raw(), bias_ref[strip, :].astype(jnp.float32), key_at, start_row, end_row), 0.0, block, key_tile)

                    return 0

                lax.fori_loop(0, blocks * key_tiles, key_step, 0)
                total = acc_ref[HD : HD + 1, :]
                outs = acc_ref[:HD, :] / total
                lse_ref[near, seq, pl.ds(tile, 1), :] = top_ref[0:1, :] + jnp.log(total)
                for k in range(per_tile):
                    part = outs[:, k * part_len : (k + 1) * part_len]
                    o_ref[tile * per_tile + k, :, lane_base : lane_base + part_len] = part
                    ob_ref[2 * (tile * per_tile + k) + (near ^ base_ref[blocks])] = part.astype(jnp.bfloat16)
                return 0

            lax.fori_loop(0, tiles, query_tile, 0)


def attend_back_kernel(chips, carried, g_base, base_ref, edge_ref, far_ref, g_ref, o_ref, lse_ref, *refs):
    kv_refs, q_ref, refs = refs[:chips], refs[0], refs[chips:]
    start_ref, end_ref, bias_ref, *refs = refs
    if carried:
        old_band_ref, old_sides_ref, *refs = refs
    made_refs, refs = refs[:chips], refs[chips:]
    dq_ref = made_refs[0]
    band_ref, sides_ref, k_rows, v_rows, k_aug, dk_acc, dv_acc, dq_acc = refs
    groups, _, span = q_ref.shape
    blocks, seq_count, span_len, _ = k_rows.shape
    part_len = span_len // groups
    per_tile = TQ // part_len
    tiles, key_tiles = span_len // TQ, span_len // KT
    per_key = KT // part_len
    for far in range(chips):
        for seq, near, source, lanes in pieces_of(seq_count, part_len, groups):
            block = 2 * far + near
            rows = slice(source * part_len, (source + 1) * part_len)
            piece = kv_refs[far][source, HD : 2 * HD, lanes]
            k_rows[block, seq, rows, :] = flipped(piece)
            v_rows[block, seq, rows, :] = flipped(kv_refs[far][source, 2 * HD :, lanes])
            at = source % per_key * part_len
            k_aug[block, seq, source // per_key, :HD, at : at + part_len] = piece
    for block in range(blocks):
        for seq in range(seq_count):
            for tile in range(key_tiles):
                k_aug[block, seq, tile, HD:, :] = ones_row(KT)
    dk_acc[...] = jnp.zeros_like(dk_acc)
    dv_acc[...] = jnp.zeros_like(dv_acc)
    band_ref[...] = old_band_ref[...] if carried else jnp.zeros_like(band_ref)
    sides_ref[...] = old_sides_ref[...] if carried else jnp.zeros_like(sides_ref)

    for seq in range(seq_count):
        for near in range(2):
            lane_base = (near * seq_count + seq) * part_len

            def query_tile(tile, _, seq=seq, near=near, lane_base=lane_base):
                query_at = base_ref[near] + tile * TQ
                row = (near * seq_count + seq) * tiles + tile
                queries = lanes_of(q_ref, tile, per_tile, part_len, lane_base)
                first = 2 * tile * per_tile + (near ^ base_ref[blocks])
                grads = [g_ref[first + 2 * k, :, g_base : g_base + part_len] for k in range(per_tile)]
                grads = jnp.concatenate(grads, axis=1)
                outs = lanes_of(o_ref, tile, per_tile, part_len, lane_base)
                delta = jnp.sum(grads.astype(jnp.float32) * outs, axis=0, keepdims=True)
                query_rows, grad_rows = flipped(queries), flipped(grads)
                lse = lse_ref[near, seq, pl.ds(tile, 1), :]
                start_row = start_ref[near, seq, pl.ds(tile, 1), :]
                end_row = end_ref[near, seq, pl.ds(tile, 1), :]
                dq_acc[...] = jnp.zeros_like(dq_acc)

                def take(scores, shift, block, key_tile):
                    rows = pl.ds(pl.multiple_of(key_tile * KT, KT), KT)
                    probs = jnp.exp(scores - (lse - shift))
                    score_grad = probs * (nn(v_rows[block, seq, rows, :], grads) - delta)
                    score_low = score_grad.astype(jnp.bfloat16)
                    dv_acc[block, seq, rows, :] += nn(probs.astype(jnp.bfloat16), grad_rows)
                    dk_acc[block, seq, rows, :] += nn(score_low, query_rows)
                    made = nn(k_aug[block, seq, key_tile], score_low)
                    dq_acc[...] += made
                    return score_grad, made[HD : HD + 1, :]

                def key_step(step, _):
                    block, key_tile = step // key_tiles, step % key_tiles
                    key_at = base_ref[block] + key_tile * KT
                    touched, plain, gap, strip = tile_class(edge_ref, row, key_at, query_at)

                    def raw():
                        keys = k_rows[block, seq, pl.ds(pl.multiple_of(key_tile * KT, KT), KT), :]
                        return nn(keys, queries)

                    @pl.when(touched & plain)
                    def _():
                        _, sums = take(raw(), jnp.where(gap < 0, far_ref[0], far_ref[1]), block, key_tile)
                        side = (gap > 0).astype(jnp.int32)
                        sides_ref[pl.ds(side, 1), :] += sums

                    @pl.when(touched & jnp.logical_not(plain))
                    def _():
                        whole_grad, _ = take(
                            masked(raw(), bias_ref[strip, :].astype(jnp.float32), key_at, start_row, end_row), 0.0, block, key_tile
                        )
                        band_ref[strip, :] += whole_grad

                    return 0

                lax.fori_loop(0, blocks * key_tiles, key_step, 0)
                for k in range(per_tile):
                    part = dq_acc[:HD, k * part_len : (k + 1) * part_len].astype(jnp.bfloat16)
                    dq_ref[tile * per_tile + k, :HD, lane_base : lane_base + part_len] = part
                return 0

            lax.fori_loop(0, tiles, query_tile, 0)
    for far in range(chips):
        for seq, near, source, lanes in pieces_of(seq_count, part_len, groups):
            block = 2 * far + near
            rows = slice(source * part_len, (source + 1) * part_len)
            top = 0 if far else HD
            made_refs[far][source, top : top + HD, lanes] = dk_acc[block, seq, rows, :].T.astype(jnp.bfloat16)
            made_refs[far][source, top + HD : top + 2 * HD, lanes] = dv_acc[block, seq, rows, :].T.astype(jnp.bfloat16)


def strip_places():
    width = TQ + 128
    lane = np.arange(width)
    lane = np.where(lane < TQ, lane, lane - width)
    offset = 128 * (np.arange(TQ // 128 + 2)[:, None] - 1) - lane[None, :]
    return np.clip(offset, -MAXREL, MAXREL) + MAXREL


def strip_kernel(far_ref, wave_ref, strip_ref):
    near_blocks, _, width = wave_ref.shape
    first = KT + MARGIN - 128
    strip_ref[:first, :] = jnp.full((first, TQ), far_ref[0], jnp.float32).astype(jnp.bfloat16)
    for k in range(near_blocks):
        spread = jnp.broadcast_to(wave_ref[k], (128, width))
        turned = pltpu.roll(spread, 0, 1, stride=1, stride_axis=0)
        strip_ref[first + 128 * k : first + 128 * (k + 1), :] = turned[:, :TQ].astype(jnp.bfloat16)
    last = first + 128 * near_blocks
    strip_ref[last:, :] = jnp.full((strip_ref.shape[0] - last, TQ), far_ref[1], jnp.float32).astype(jnp.bfloat16)


def bias_strip(far_bias, waves):
    return pl.pallas_call(
        strip_kernel,
        name="bias_strip",
        out_shape=jax.ShapeDtypeStruct((2 * KT + 2 * MARGIN + TQ, TQ), jnp.bfloat16),
        in_specs=[SMEM, VMEM],
        out_specs=VMEM,
        compiler_params=pltpu.CompilerParams(vmem_limit_bytes=32 * 2**20),
    )(far_bias, waves)


def band_kernel(band_ref, sides_ref, near_ref, far_ref):
    near_blocks, _, width = near_ref.shape
    first = KT + MARGIN - 128
    last = first + 128 * near_blocks
    left = jnp.sum(band_ref[:first, :], axis=0, keepdims=True) + sides_ref[0:1, :]
    right = jnp.sum(band_ref[last:, :], axis=0, keepdims=True) + sides_ref[1:2, :]
    far_ref[...] = jnp.concatenate([left, right, jnp.zeros((6, TQ), jnp.float32)], axis=0)
    for k in range(near_blocks):
        rows = band_ref[first + 128 * k : first + 128 * (k + 1), :]
        spread = jnp.concatenate([rows, jnp.zeros((128, width - TQ), jnp.float32)], axis=1)
        row = lax.broadcasted_iota(jnp.int32, spread.shape, 0)
        for step in (1, 2, 4):
            spread = jnp.where((row & step) != 0, pltpu.roll(spread, width - step, 1), spread)
        total = spread[:8, :]
        for at in range(8, 128, 8):
            total = total + pltpu.roll(spread[at : at + 8, :], width - at, 1)
        near_ref[k] = jnp.sum(total, axis=0, keepdims=True)


def band_sums_of(band, sides):
    return pl.pallas_call(
        band_kernel,
        name="band_sums",
        out_shape=(
            jax.ShapeDtypeStruct((TQ // 128 + 2, 1, TQ + 128), jnp.float32),
            jax.ShapeDtypeStruct((8, TQ), jnp.float32),
        ),
        in_specs=[VMEM, VMEM],
        out_specs=(VMEM, VMEM),
        compiler_params=pltpu.CompilerParams(vmem_limit_bytes=32 * 2**20),
    )(band, sides)


SMEM = pl.BlockSpec(memory_space=pltpu.SMEM)
VMEM = pl.BlockSpec(memory_space=pltpu.VMEM)


def attend(base, edges, far_bias, kvs, starts, ends, bias):
    chips = len(kvs)
    groups, _, span = kvs[0].shape
    shape = (groups, HD, span)
    _, seq_count, tiles, _ = starts.shape
    blocks, span_len = 2 * chips, tiles * TQ
    return pl.pallas_call(
        functools.partial(attend_kernel, chips),
        name="attend",
        out_shape=(
            jax.ShapeDtypeStruct(shape, jnp.float32),
            jax.ShapeDtypeStruct((2 * groups, HD, span // 2), jnp.bfloat16),
            jax.ShapeDtypeStruct(starts.shape, jnp.float32),
        ),
        in_specs=[SMEM] * 3 + [VMEM] * (chips + 3),
        out_specs=(VMEM,) * 3,
        scratch_shapes=[
            pltpu.VMEM((blocks, seq_count, span_len, HD), jnp.bfloat16),
            pltpu.VMEM((blocks, seq_count, span_len // KT, AUG, KT), jnp.bfloat16),
            pltpu.VMEM((8, TQ), jnp.float32),
            pltpu.VMEM((AUG, TQ), jnp.float32),
        ],
        cost_estimate=pl.CostEstimate(flops=1, transcendentals=0, bytes_accessed=1),
        compiler_params=pltpu.CompilerParams(vmem_limit_bytes=48 * 2**20),
    )(base, edges, far_bias, *kvs, starts, ends, bias)


def attend_back(base, edges, far_bias, g, seq, o, lse, kvs, starts, ends, bias, sums=()):
    chips = len(kvs)
    groups, _, span = kvs[0].shape
    _, seq_count, tiles, _ = starts.shape
    blocks, span_len = 2 * chips, tiles * TQ
    made = pl.pallas_call(
        functools.partial(attend_back_kernel, chips, bool(sums), seq * span // 2),
        name="attend_back",
        out_shape=(jax.ShapeDtypeStruct(kvs[0].shape, jnp.bfloat16),)
        + (jax.ShapeDtypeStruct((groups, 2 * HD, span), jnp.bfloat16),) * (chips - 1)
        + (jax.ShapeDtypeStruct(bias.shape, jnp.float32), jax.ShapeDtypeStruct((8, TQ), jnp.float32)),
        in_specs=[SMEM] * 3
        + [VMEM] * (3 + chips + 3 + len(sums)),
        out_specs=(VMEM,) * (2 + chips),
        scratch_shapes=[
            pltpu.VMEM((blocks, seq_count, span_len, HD), jnp.bfloat16),
            pltpu.VMEM((blocks, seq_count, span_len, HD), jnp.bfloat16),
            pltpu.VMEM((blocks, seq_count, span_len // KT, AUG, KT), jnp.bfloat16),
            pltpu.VMEM((blocks, seq_count, span_len, HD), jnp.float32),
            pltpu.VMEM((blocks, seq_count, span_len, HD), jnp.float32),
            pltpu.VMEM((AUG, TQ), jnp.float32),
        ],
        cost_estimate=pl.CostEstimate(flops=1, transcendentals=0, bytes_accessed=1),
        compiler_params=pltpu.CompilerParams(vmem_limit_bytes=56 * 2**20),
    )(base, edges, far_bias, g, o, lse, *kvs, starts, ends, bias, *sums)
    return made[0], made[1:chips], made[-2:]


def trade(block, axis, bit):
    size = lax.axis_size(axis)
    return lax.ppermute(block, axis, [(i, i ^ bit) for i in range(size)])


def mate(block):
    return trade(block, "blk", 1)


def across_x(block):
    return trade(block, "blk", 2)


def across_y(block):
    return trade(block, "head", 1)


def across_z(block, distance):
    return trade(block, "head", 2 * distance)


def whole_block(array):
    return pl.BlockSpec(array.shape, lambda i: (0,) * len(array.shape))


def copy_kernel(plan, slots_ref, *arrays):
    for source, source_rows, target, target_rows, count in plan:
        views = []
        for which, (slot, scale, first, columns) in ((source, source_rows), (target, target_rows)):
            begin = first if slot is None else pl.multiple_of(slots_ref[slot] * scale, 8) + first
            views.append(arrays[which].at[pl.ds(begin, count), pl.ds(columns[0], columns[1])])
        views[1][...] = views[0][...]


def moved(name, slots, sources, shapes, plan):
    outs = tuple(pltpu.HBM(shape, sources[0].dtype) for shape in shapes)
    return pl.pallas_call(
        functools.partial(copy_kernel, plan),
        name=name,
        grid=(1,),
        out_shape=outs,
        in_specs=[SMEM] + [whole_block(block) for block in sources],
        out_specs=tuple(whole_block(block) for block in outs),
        compiler_params=pltpu.CompilerParams(vmem_limit_bytes=48 * 2**20),
    )(slots, *sources)


DEPTH = 4
CHIPS = 16


def turn_of(k):
    return k % DEPTH, k // DEPTH // 2, k // DEPTH % 2


def slot_table():
    n_blk = lax.axis_size("blk")
    group, place = lax.axis_index("head"), lax.axis_index("blk")
    groups = group ^ jnp.asarray([2 * turn_of(k)[0] + turn_of(k)[1] for k in range(CHIPS)], jnp.int32)
    sides = (place // 2) ^ jnp.asarray([turn_of(k)[2] for k in range(CHIPS)], jnp.int32)
    chips = groups * (n_blk // 2) + sides
    return jnp.concatenate([chips, groups, 2 * chips + place % 2, 2 * chips + 1 - place % 2])


CHIP, GROUP, DEVICE, MATE = 0, CHIPS, 2 * CHIPS, 3 * CHIPS


def after(block, *earlier):
    return lax.optimization_barrier((block, earlier))[0]


def beside(made, *sent):
    return lax.optimization_barrier((made, *sent))


def wide(block):
    return block.astype(jnp.float32)


def placed(name, slots, blocks, layout, shapes, order):
    plan = []
    for k, (which, at) in enumerate(order):
        for first, count, whole, take, target in layout:
            plan.append((which, (None, 0, at + first, take), len(blocks) + whole, target(k), count))
    return moved(name, slots, blocks, shapes, tuple(plan))


def parted(name, slots, wholes, layout, shapes, order):
    plan = []
    for k, (which, at) in enumerate(order):
        for first, count, whole, take, target in layout:
            plan.append((whole, target(k), len(wholes) + which, (None, 0, at + first, take), count))
    return moved(name, slots, wholes, shapes, tuple(plan))


def grouped(rows):
    order = []
    for k in range(CHIPS):
        group, z = k // DEPTH, k % DEPTH
        order.append((group, z * rows) if group < 3 else (3 + z // 2, z % 2 * rows))
    return order


def gather_z(payload, *earlier):
    payload = after(payload, *earlier) if earlier else payload
    return [payload] + [across_z(payload, k) for k in range(1, DEPTH)]


def gather_xy(own, *earlier):
    own = jnp.concatenate(own, axis=0)
    own = after(own, *earlier) if earlier else own
    return own, across_x(own), across_y(own)


def gather_corner(blocks, *earlier):
    own, by_x, by_y = blocks
    half = own.shape[0] // 2
    low, high = by_x[:half], by_y[half:]
    if earlier:
        low, high = after(low, *earlier), after(high, *earlier)
    return own, by_x, by_y, across_y(low), across_x(high)


def sum_parts(name, slots, wholes, layout, rows, width):
    full, half = DEPTH * rows, DEPTH // 2 * rows
    shapes = ((full, width),) * 3 + ((half, width),) * 2
    return parted(name, slots, wholes, layout, shapes, grouped(rows))


def sum_corner(blocks):
    own, by_x, by_y, low, high = blocks
    return own, by_x, by_y, across_y(low), across_x(high)


def sum_xy(blocks):
    own, by_x, by_y, low, high = blocks
    half = low.shape[0]
    return own, across_x(added(by_x, low, slice(0, half))), across_y(added(by_y, high, slice(half, 2 * half)))


def column_kernel(*refs):
    groups, outs = refs[:-DEPTH], refs[-DEPTH:]
    first = 0
    for at in range(0, len(groups), 3):
        rows = groups[at].shape[0] // DEPTH
        for k, out_ref in enumerate(outs):
            here = slice(k * rows, (k + 1) * rows)
            total = sum(wide(ref[here]) for ref in groups[at : at + 3])
            out_ref[first : first + rows, :] = total.astype(out_ref.dtype)
        first += rows


def column_sent(*groups):
    rows, width = sum(group[0].shape[0] for group in groups) // DEPTH, groups[0][0].shape[1]
    blocks = [block for group in groups for block in group]
    here, *given = pl.pallas_call(
        column_kernel,
        name="column",
        out_shape=[jax.ShapeDtypeStruct((rows, width), jnp.float32)]
        + [jax.ShapeDtypeStruct((rows, width), jnp.bfloat16)] * (DEPTH - 1),
        in_specs=[VMEM] * len(blocks),
        out_specs=[VMEM] * DEPTH,
        compiler_params=pltpu.CompilerParams(vmem_limit_bytes=32 * 2**20),
    )(*blocks)
    return [here] + [across_z(block, k + 1) for k, block in enumerate(given)]


def column_total(blocks):
    here, *met = blocks
    return here + sum(wide(block) for block in met)


def norm_kernel(here_ref, there_ref, gain_ref, rows_ref, scale_ref, *normed_refs):
    seqs, part, _ = here_ref.shape
    for seq in range(seqs):
        for which, ref in enumerate((here_ref, there_ref)):
            rows = wide(ref[seq])
            scale = lax.rsqrt(jnp.mean(rows * rows, axis=-1, keepdims=True) + EPS)
            normed = (rows * scale * gain_ref[...]).astype(here_ref.dtype)
            normed_refs[seq][which * part : (which + 1) * part, :] = normed
            if which == 0:
                rows_ref[seq * part : (seq + 1) * part, :] = rows
                scale_ref[seq * part : (seq + 1) * part, :] = scale


def normed_by_seq(here, there, gain):
    seqs, part, width = here.shape
    shapes = [(seqs * part, width), (seqs * part, 1)]
    return pl.pallas_call(
        norm_kernel,
        name="normed_by_seq",
        out_shape=[jax.ShapeDtypeStruct(shape, jnp.float32) for shape in shapes]
        + [jax.ShapeDtypeStruct((2 * part, width), here.dtype)] * seqs,
        in_specs=[VMEM] * 3,
        out_specs=[VMEM] * (2 + seqs),
    )(here, there, gain.reshape(1, width))


def feed_kernel(rows_ref, grad_ref, in_ref, down_ref, act_ref, up_ref, out_near, out_far, back_near, back_far):
    half = rows_ref.shape[0] // 2
    values, rise = gelu_both(nn(rows_ref[...], in_ref[...]))
    values = values.astype(act_ref.dtype)
    act_ref[...] = values
    up = (dot_on(grad_ref[...], down_ref[...], 1, 1) * rise).astype(up_ref.dtype)
    up_ref[...] = up
    made, back = nn(values, down_ref[...]), dot_on(up, in_ref[...], 1, 1)
    parts = ((out_near, made[:half]), (out_far, made[half:]), (back_near, back[:half]), (back_far, back[half:]))

    @pl.when(pl.program_id(0) == 0)
    def _():
        for ref, part in parts:
            ref[...] = part

    @pl.when(pl.program_id(0) > 0)
    def _():
        for ref, part in parts:
            ref[...] += part


def feed(rows, grads, in_w, down_w):
    tokens, width = rows.shape
    hidden, step = in_w.shape[1], 512
    whole = pl.BlockSpec((tokens, width), lambda i: (0, 0))
    half = pl.BlockSpec((tokens // 2, width), lambda i: (0, 0))
    units = pl.BlockSpec((tokens, step), lambda i: (0, i))
    return pl.pallas_call(
        feed_kernel,
        name="feed",
        grid=(hidden // step,),
        out_shape=[pltpu.HBM((tokens, hidden), rows.dtype)] * 2
        + [pltpu.HBM((tokens // 2, width), jnp.float32)] * 4,
        in_specs=[
            whole,
            whole,
            pl.BlockSpec((width, step), lambda i: (0, i)),
            pl.BlockSpec((step, width), lambda i: (i, 0)),
        ],
        out_specs=[units] * 2 + [half] * 4,
        cost_estimate=pl.CostEstimate(flops=1, transcendentals=0, bytes_accessed=1),
        compiler_params=pltpu.CompilerParams(vmem_limit_bytes=32 * 2**20),
    )(rows, grads, in_w, down_w)


def weight_grad_kernel(left_ref, right_ref, out_ref):
    out_ref[...] = dot_on(left_ref[...], right_ref[...], 0, 0).astype(out_ref.dtype)


def weight_grad(left, right):
    tokens, rows = left.shape
    cols, step = right.shape[1], 512
    left, right = (pltpu.with_memory_space_constraint(block, pltpu.HBM) for block in (left, right))
    return pl.pallas_call(
        weight_grad_kernel,
        name="weight_grad",
        grid=(rows // step,),
        out_shape=jax.ShapeDtypeStruct((rows, cols), left.dtype),
        in_specs=[pl.BlockSpec((tokens, step), lambda i: (0, i)), pl.BlockSpec((tokens, cols), lambda i: (0, 0))],
        out_specs=pl.BlockSpec((step, cols), lambda i: (i, 0)),
        cost_estimate=pl.CostEstimate(flops=1, transcendentals=0, bytes_accessed=1),
        compiler_params=pltpu.CompilerParams(vmem_limit_bytes=32 * 2**20),
    )(left, right)


def first_back_kernel(plan, slots_ref, in_0, made_0, in_1, made_1, *refs):
    *parts, whole_ref = refs
    rows = whole_ref.shape[0]
    step = 256
    for at in range(0, rows, step):
        here = slice(at, at + step)
        product = dot_on(in_0[here], made_0[...], 1, 1) + dot_on(in_1[here], made_1[...], 1, 1)
        whole_ref[here, :] = product.astype(whole_ref.dtype)
    for slot, scale, which, at in plan:
        source = pl.ds(pl.multiple_of(slots_ref[slot] * scale, scale), scale)
        parts[which][at : at + scale, :] = whole_ref[source, :]


def first_back(slots, plan, shapes, ins, made):
    outs = [pltpu.HBM(shape, made[0].dtype) for shape in shapes]
    sources = (ins[0], made[0], ins[1], made[1])
    sources = [pltpu.with_memory_space_constraint(block, pltpu.HBM) for block in sources]
    return pl.pallas_call(
        functools.partial(first_back_kernel, plan),
        name="first_back",
        grid=(1,),
        out_shape=outs,
        in_specs=[SMEM] + [whole_block(block) for block in sources],
        out_specs=[whole_block(block) for block in outs],
        scratch_shapes=[pltpu.VMEM((ins[0].shape[0], made[0].shape[0]), made[0].dtype)],
        compiler_params=pltpu.CompilerParams(vmem_limit_bytes=48 * 2**20),
    )(slots, *sources)


def last_kernel(first_ref, second_ref, wq_ref, wk_ref, wv_ref, q_ref, k_ref, v_ref, gain_ref):
    groups = first_ref.shape[1] // (3 * HD)
    for g in range(groups):
        for which, out_ref in enumerate((q_ref, k_ref, v_ref)):
            at = (3 * g + which) * HD
            pair = [ref[:, at : at + HD] for ref in (first_ref, second_ref)]
            out_ref[:, 2 * g * HD : 2 * (g + 1) * HD] = jnp.concatenate(pair, axis=1)
    products = sum(wide(w[...]) * grad[...] for w, grad in ((wq_ref, q_ref), (wk_ref, k_ref), (wv_ref, v_ref)))
    gain_ref[...] = jnp.sum(products, axis=1, keepdims=True)


def by_weight(first, second, *weights):
    rows, width = weights[0].shape
    return pl.pallas_call(
        last_kernel,
        name="by_weight",
        out_shape=[jax.ShapeDtypeStruct((rows, width), jnp.float32)] * 3 + [jax.ShapeDtypeStruct((rows, 1), jnp.float32)],
        in_specs=[VMEM] * 5,
        out_specs=[VMEM] * 4,
    )(first, second, *weights)


def halves_kernel(place_ref, in_ref, out_ref, *refs):
    *down_refs, in_w_ref, out_w_ref, down_w_ref = refs
    devices, rows, width = out_ref.shape
    for d in range(devices):
        here = pl.ds(d * rows, rows)
        for j in range(in_ref.shape[1] // rows):
            in_w_ref[here, j * width : (j + 1) * width] = in_ref[d, j * rows : (j + 1) * rows, :]
        out_w_ref[here, :] = out_ref[d]
    rows = down_refs[0].shape[1]
    for chip, down_ref in enumerate(down_refs):
        down_w_ref[pl.ds(chip * rows, rows), :] = down_ref[0]


def own_halves(core, whole, down_rows, shard):
    devices, rows, width = whole.shape
    steps, chips = 4, devices // 2
    in_rows = (rows - down_rows - shard) // 2
    in_at, out_at = down_rows // in_rows, (rows - shard) // shard
    shapes = (
        (devices * shard, in_rows // shard * width),
        (devices * shard, width),
        (chips * down_rows, width),
    )
    return pl.pallas_call(
        halves_kernel,
        name="own_halves",
        grid_spec=pltpu.PrefetchScalarGridSpec(
            num_scalar_prefetch=1,
            grid=(steps,),
            in_specs=[
                pl.BlockSpec((devices // steps, in_rows, width), lambda i, place_ref: (i, in_at + place_ref[0], 0)),
                pl.BlockSpec((devices // steps, shard, width), lambda i, place_ref: (i, out_at, 0)),
            ]
            + [
                pl.BlockSpec(
                    (1, down_rows, width), lambda i, place_ref, j=j: (2 * (i * chips // steps + j) + place_ref[0], 0, 0)
                )
                for j in range(chips // steps)
            ],
            out_specs=[pl.BlockSpec((shape[0] // steps, shape[1]), lambda i, place_ref: (i, 0)) for shape in shapes],
        ),
        out_shape=[pltpu.HBM(shape, whole.dtype) for shape in shapes],
        compiler_params=pltpu.CompilerParams(vmem_limit_bytes=32 * 2**20),
    )(core.reshape(1), *[whole] * (2 + chips // steps))


def add_kernel(place, whole_ref, part_ref, sum_ref):
    sum_ref[...] = whole_ref[...]
    sum_ref[place] = (wide(whole_ref[place]) + wide(part_ref[...])).astype(sum_ref.dtype)


def added(whole, part, place):
    return pl.pallas_call(
        functools.partial(add_kernel, place),
        name="added",
        out_shape=jax.ShapeDtypeStruct(whole.shape, whole.dtype),
        in_specs=[VMEM] * 2,
        out_specs=VMEM,
        compiler_params=pltpu.CompilerParams(vmem_limit_bytes=32 * 2**20),
    )(whole, part)


def document_bounds(segments):
    seq_count, blocks, span_len = segments.shape
    length = blocks * span_len
    numbers = lax.iota(jnp.int32, length // min(512, length) + 2)
    flat = segments.reshape(seq_count, length)
    below = jnp.sum((flat[:, :, None] < numbers).astype(jnp.int32), axis=1)
    here = flat[:, :, None] == numbers[:-1]
    starts = jnp.sum(jnp.where(here, below[:, None, :-1], 0), axis=2)
    ends = jnp.sum(jnp.where(here, below[:, None, 1:], 0), axis=2)
    return starts.reshape(segments.shape), ends.reshape(segments.shape)


def query_bounds(bounds, place, tile):
    near = [lax.dynamic_index_in_dim(bounds, place ^ k, 1, keepdims=False) for k in (0, 2)]
    near = jnp.stack(near, axis=0)
    return near.reshape(near.shape[0], near.shape[1], -1, tile)


def gelu_both(values):
    slope = float(np.sqrt(2.0 / np.pi))
    square = values * values
    curve = jnp.tanh(slope * values * (1.0 + 0.044715 * square))
    half = 0.5 * (1.0 + curve)
    rise = half + 0.5 * values * (1.0 - curve * curve) * (slope * (1.0 + 3 * 0.044715 * square))
    return values * half, rise


def joined(block):
    return jnp.concatenate([block, mate(block)], axis=0)


def halves_added(block):
    half = block.shape[0] // 2
    return block[:half] + mate(block[half:])


def norm_back(grad, rows, scale, gain):
    weighted = grad * gain
    inner = jnp.mean(rows * weighted, axis=-1, keepdims=True)
    return scale * weighted - rows * (scale * scale * scale) * inner


def dot_on(left, right, left_dim, right_dim):
    return lax.dot_general(left, right, (((left_dim,), (right_dim,)), ((), ())), preferred_element_type=jnp.float32)


def pair_body(
    inputs,
    segments,
    bucket_table,
    norm_gain,
    w_query,
    w_key,
    w_value,
    w_out,
    rel_bias,
    ff_gain,
    w_in,
    w_down,
    cotangent,
):
    low = jnp.bfloat16
    seq_count, _, part_len, width = inputs.shape
    groups = lax.axis_size("head")
    span_len = part_len * groups
    blocks = lax.axis_size("blk")
    group, place = lax.axis_index("head"), lax.axis_index("blk")
    core, side = place % 2, place // 2
    slots = slot_table()
    shard = w_query.shape[0]
    chip_rows = 2 * shard
    head_cols = 3 * HD
    first_cols = groups * head_cols
    half_width = groups * HD
    half_hidden = w_in.shape[1] // 2
    down_rows = w_down.shape[0]
    tokens = seq_count * part_len

    def all_rows(pieces):
        return jnp.concatenate(pieces, axis=0)

    turned = segments[1, -1, -1] < segments[0, -1, -1]

    def in_order(block):
        return jnp.where(turned, block[::-1], block)

    inputs, cotangent, segments = in_order(inputs), in_order(cotangent), in_order(segments)

    def by_core(first, second):
        return jnp.where(core == 0, first, second)

    def by_side(first, second):
        return jnp.where(side == 0, first, second)

    cores = [[g * blocks + 2 * s + c for g in range(groups) for s in range(blocks // 2)] for c in range(2)]

    def exchanged_all(block):
        return lax.all_to_all(block, ("head", "blk"), split_axis=0, concat_axis=0, tiled=True, axis_index_groups=cores)

    def exchanged(block):
        return lax.all_to_all(block, "head", split_axis=0, concat_axis=0, tiled=True)

    every, first_every = (0, width), (0, first_cols)
    def head_columns(weight, which):
        return weight.reshape(shard, groups, 2, HD)[:, :, which]

    def cut(which):
        return jnp.stack([head_columns(w, which) for w in (w_query, w_key, w_value)], axis=2).reshape(shard, -1)

    first_cut, second_cut = cut(0), cut(1)
    chunks = [by_side(first_cut, second_cut), across_x(by_side(second_cut, first_cut))]
    gains = jnp.concatenate([norm_gain, ff_gain, rel_bias, jnp.zeros((128 - 5 * shard // 2,), low)])
    gains = jnp.broadcast_to(jnp.pad(gains[None, :], ((0, 7), (0, 0))), (2 * CHIPS, 8, 128))
    gain_w = lax.all_to_all(after(gains, chunks[1]), ("head", "blk"), split_axis=0, concat_axis=0, tiled=True)
    gain_w = wide(gain_w[:, 0])
    gain_one = gain_w[:, :shard].reshape(-1)
    gain_two = gain_w[:, shard : 2 * shard].reshape(-1)

    input_rows = inputs.reshape(seq_count, part_len, width)
    token_rows, scale_one, *first_in = normed_by_seq(input_rows, across_x(input_rows), gain_one)

    first_blocks = []
    for at, chunk in enumerate(chunks):
        own = jnp.concatenate(gather_z(chunk), axis=0)
        if at == 0:
            own, chunks[1] = beside(own, chunks[1])
        by_y = across_y(own)
        if at == 1:
            by_y, first_in = beside(by_y, first_in)
        both = jnp.concatenate([own, by_y], axis=0)
        first_blocks += [both, mate(both)]
    plan = []
    for k in range(CHIPS):
        z, y, x = turn_of(k)
        for far, slot in enumerate((DEVICE, MATE)):
            source = (None, 0, (DEPTH * y + z) * shard, first_every)
            plan.append((2 * x + far, source, 4, (slot + k, shard, 0, first_every), shard))
    (first_w,) = moved("whole_first", slots, first_blocks, ((width, first_cols),), tuple(plan))

    def hidden_columns(which):
        return w_in.reshape(shard, -1, 2, down_rows)[:, :, which].reshape(shard, -1, width)

    payload_in = jnp.stack([hidden_columns(0), hidden_columns(1)], axis=0).transpose(0, 2, 1, 3).reshape(-1, width)
    in_rows = 2 * chip_rows + shard
    payload = jnp.concatenate([w_down, payload_in, w_out], axis=0)
    whole = lax.all_gather(payload, ("head", "blk"), axis=0, tiled=False)
    whole = pltpu.with_memory_space_constraint(whole, pltpu.HBM)

    lay_in = (
        (0, chip_rows, 0, every, lambda k: (CHIP + k, chip_rows, 0, (0, width))),
        (chip_rows, chip_rows, 0, every, lambda k: (CHIP + k, chip_rows, 0, (width, width))),
        (2 * chip_rows, shard, 1, every, lambda k: (CHIP + k, shard, 0, every)),
    )
    lay_down = ((0, down_rows, 0, every, lambda k: (CHIP + k, down_rows, 0, every)),)

    rel_table = gain_w[:, 2 * shard : 5 * shard // 2].reshape(HEADS, BUCKETS)
    rel_here = lax.dynamic_index_in_dim(rel_table, 2 * group + side, 0, keepdims=False)

    bucket_hot = bucket_table[:, None] == lax.iota(jnp.int32, BUCKETS)[None, :]
    by_offset = jnp.sum(jnp.where(bucket_hot, rel_here[None, :], 0.0), axis=1)
    places = strip_places()
    place_hot = jnp.asarray(places.reshape(-1))[:, None] == lax.iota(jnp.int32, 2 * MAXREL + 1)[None, :]
    place_hot = place_hot.astype(jnp.float32)
    waves = jnp.dot(place_hot, by_offset, precision=lax.Precision.HIGHEST)
    waves = waves.reshape(places.shape[0], 1, places.shape[1])
    far_bias = jnp.stack([by_offset[0], by_offset[-1]])
    bias = bias_strip(far_bias, waves)
    starts, ends = document_bounds(segments)
    starts, ends = query_bounds(starts, place, TQ), query_bounds(ends, place, TQ)
    edges = jnp.stack([starts[..., 0], starts[..., -1], ends[..., 0], ends[..., -1]], axis=-1)
    base = (place ^ jnp.asarray([0, 2, 1, 3], jnp.int32)) * span_len
    base = jnp.concatenate([base, side.reshape(1)])

    made = [dot_on(first_w, rows, 0, 1).astype(low) for rows in first_in]
    sent = exchanged(made[0].reshape(groups, head_cols, 2 * part_len))
    sent, bias, far_bias, starts, ends, edges = beside(sent, bias, far_bias, starts, ends, edges)
    bounds = [(starts[:, seq : seq + 1], ends[:, seq : seq + 1], bias) for seq in range(seq_count)]
    edges = [edges[:, seq].reshape(-1) for seq in range(seq_count)]
    attended, heads, attn_cols = [], [], [None] * seq_count
    for seq in range(seq_count):
        heads.append([sent, mate(sent)])
        if seq + 1 < seq_count:
            heads[seq][1], made[seq + 1] = beside(heads[seq][1], made[seq + 1])
        done = attend(base, edges[seq], far_bias, heads[seq], *bounds[seq])
        if seq + 1 < seq_count:
            done, sent = beside(done, exchanged(made[seq + 1].reshape(groups, head_cols, 2 * part_len)))
        else:
            done, attn_cols[seq - 1] = beside(done, attn_cols[seq - 1])
        attended.append(done)
        attn_cols[seq] = exchanged_all(done[1])
    attn_cols[1], in_w, out_w, down_w = beside(attn_cols[1], *own_halves(core, whole, down_rows, shard))
    attn_cols = jnp.concatenate([block.reshape(2 * half_width, part_len) for block in attn_cols], axis=1)
    hidden_one = token_rows + dot_on(attn_cols, out_w, 0, 0)
    scale_two = lax.rsqrt(jnp.mean(hidden_one * hidden_one, axis=-1, keepdims=True) + EPS)
    second_in = joined((hidden_one * scale_two * gain_two).astype(low))
    incoming_low = cotangent.reshape(tokens, width)
    incoming = joined(incoming_low)
    activated, up_grad, layer_near, layer_far, back_near, back_far = feed(second_in, incoming, in_w, down_w)
    whole_down = weight_grad(activated, incoming)
    down_parts = sum_parts("parts_down", slots, (whole_down,), lay_down, down_rows, width)
    down_parts = sum_corner(down_parts)
    second_grad = back_near + mate(back_far)
    hidden_part = norm_back(second_grad, hidden_one, scale_two, gain_two)
    hidden_grad = wide(incoming_low) + hidden_part
    branch = hidden_grad.astype(low)
    grads = dot_on(out_w, branch, 1, 1).astype(low).reshape(HEADS, HD, tokens)
    late_in, late_branch = after((second_in, branch), grads, down_parts)
    whole_in = weight_grad(late_in, up_grad)
    whole_out = dot_on(attn_cols, late_branch, 1, 0).astype(low).reshape(-1, 2, shard, width)
    out_mine, out_given = by_core(whole_out[:, 0], whole_out[:, 1]), by_core(whole_out[:, 1], whole_out[:, 0])
    whole_out = (wide(out_mine) + wide(mate(out_given))).astype(low).reshape(half_width, width)
    in_parts = sum_parts("parts_in", slots, (whole_in, whole_out), lay_in, in_rows, width)
    grads, in_parts = beside(exchanged_all(grads), in_parts)
    in_parts = sum_corner(in_parts)
    down_parts = sum_xy(down_parts)

    def offset_grads(band, sides, earlier):
        near_sums, far_sums = band_sums_of(after(band, *earlier), sides)
        offset_sums = jnp.dot(near_sums.reshape(-1), place_hot, precision=lax.Precision.HIGHEST)
        far_sums = jnp.sum(far_sums, axis=1)
        end_hot = lax.iota(jnp.int32, 2 * MAXREL + 1)
        offset_sums = offset_sums + jnp.where(end_hot == 0, far_sums[0], 0.0)
        offset_sums = offset_sums + jnp.where(end_hot == 2 * MAXREL, far_sums[1], 0.0)
        return jnp.sum(jnp.where(bucket_hot, offset_sums[:, None], 0.0), axis=0)

    sums, made, sent = (), [], None
    for seq in range(seq_count):
        outs, _, lse = attended[seq]
        done = attend_back(base, edges[seq], far_bias, grads, seq, outs, lse, heads[seq], *bounds[seq], sums)
        if seq == 0:
            done, in_parts, down_parts = beside(done, in_parts, down_parts)
        else:
            done, in_parts, down_sent, made[0] = beside(done, in_parts, down_sent, made[0])
        near_grad, (far_grad,), sums = done
        near_grad = added(near_grad, mate(far_grad), (slice(None), slice(HD, 3 * HD)))
        if seq == 0:
            grads, near_grad = beside(grads, near_grad)
            in_parts = sum_xy(in_parts)
            down_sent = column_sent(down_parts)
        made.append(exchanged(near_grad))
    band, sides = sums
    layer_out = (hidden_one + layer_near + mate(layer_far)).astype(low).reshape(inputs.shape)
    made = [block.reshape(first_cols, 2 * part_len) for block in made]
    first_grads = [dot_on(after(made[0], near_grad), first_w, 0, 1)]
    far_parts = [across_x(first_grads[0][part_len:].astype(low))]
    made[1], rel_grad, far_parts = beside(made[1], offset_grads(band, sides, (near_grad,)), far_parts)
    plan, column = [], 2 * DEPTH * shard
    for k in range(CHIPS):
        z, y, x = turn_of(k)
        plan.append((MATE + k, shard, 0, y * column + (2 * z + x) * shard))
        plan.append((DEVICE + k, shard, 1 + y, (2 * z + x) * shard))
    shapes = ((2 * column, first_cols), (column, first_cols), (column, first_cols))
    given, near, by_y = first_back(slots, tuple(plan), shapes, [block.T for block in first_in], made)
    in_sent = column_sent(after(in_parts, made[1]))
    got = mate(given)
    by_y = across_y((wide(by_y) + wide(got[column:])).astype(low))
    by_y, in_sent[1] = beside(by_y, in_sent[1])
    first_sent = column_sent((near, got[:column], by_y))
    first_sum = column_total(first_sent)
    first_sums = [first_sum[:shard], across_x(first_sum[shard:])]
    in_sum = column_total(after(in_sent, first_sent[0]))
    grad_down = column_total(down_sent)
    first_grads.append(dot_on(after(made[1], first_sent[0]), first_w, 0, 1))
    far_parts.append(across_x(first_grads[1][part_len:].astype(low)))
    first_grad = all_rows([grad[:part_len] for grad in first_grads]) + wide(all_rows(far_parts))
    input_part = norm_back(first_grad, token_rows, scale_one, gain_one)
    input_grad = (hidden_grad + input_part).astype(low).reshape(inputs.shape)

    grad_query, grad_key, grad_value, norm_sums = by_weight(
        by_side(*first_sums), by_side(*first_sums[::-1]), w_query, w_key, w_value
    )

    hidden_rows = jnp.concatenate([in_sum[:chip_rows], in_sum[chip_rows : 2 * chip_rows]], axis=1)
    mine = by_core(hidden_rows[:shard], hidden_rows[shard:])
    other = mate(by_core(hidden_rows[shard:], hidden_rows[:shard]))
    in_pair = [block.reshape(shard, -1, down_rows) for block in (by_core(mine, other), by_core(other, mine))]
    grad_in = jnp.stack(in_pair, axis=2).reshape(shard, -1)
    grad_out = in_sum[2 * chip_rows :]

    grad_norm_gain = norm_sums[:, 0] / wide(norm_gain)
    grad_ff_gain = jnp.sum(wide(w_in) * grad_in, axis=1) / wide(ff_gain)

    rel_grad = jnp.pad(rel_grad[None, :], ((0, 7), (0, 128 - BUCKETS)))
    rel_sum = (rel_grad + mate(rel_grad))[0]
    rel_mine = by_core(rel_sum[: BUCKETS // 2], rel_sum[BUCKETS // 2 : BUCKETS])

    return (
        in_order(layer_out),
        in_order(input_grad),
        grad_norm_gain,
        grad_query,
        grad_key,
        grad_value,
        grad_out,
        rel_mine,
        grad_ff_gain,
        grad_in,
        grad_down,
    )


def solution(mesh):
    placed = (
        P(None, "blk", "head", None),
        P(),
        P(),
        P(("head", "blk")),
        P(("head", "blk"), None),
        P(("head", "blk"), None),
        P(("head", "blk"), None),
        P(("head", "blk"), None),
        P(("head", "blk")),
        P(("head", "blk")),
        P(("head", "blk"), None),
        P(("head", "blk"), None),
        P(None, "blk", "head", None),
    )
    n_head, n_blk = mesh.shape["head"], mesh.shape["blk"]
    paired = HEADS == 2 * n_head and (n_head, n_blk) == (8, 4)
    return jax.shard_map(
        pair_body if paired else ring_body,
        mesh=mesh,
        in_specs=placed,
        out_specs=(
            P(None, "blk", "head", None),
            P(None, "blk", "head", None),
            P(("head", "blk")),
            P(("head", "blk"), None),
            P(("head", "blk"), None),
            P(("head", "blk"), None),
            P(("head", "blk"), None),
            P(("head", "blk")),
            P(("head", "blk")),
            P(("head", "blk"), None),
            P(("head", "blk"), None),
        ),
        check_vma=False,
    )
```
